512 devices in a mesh: lon: 128 (over z, y, core), lat: 4 (over x).
Axes of the slice: x: 4, y: 8, z: 8, core: 2. Of those that a mesh axis runs over, the one named last changes fastest.
Arguments:
- initial: float32 [2, 8, 4096, 1024], P(None, None, 'lon', 'lat'), may hold values from -6 to 6
- depth_levels: int32 [4096, 1024], P('lon', 'lat'), may hold values from 0 to 8, as said below
- mixing: float32 [4096, 1024], P('lon', 'lat'), may hold values from 0.02 to 0.2
- controls: float32 [4, 2, 256, 64], replicated, may hold values from -6 to 6
- drift_move: int32 [2, 2097152], P(None, ('lon', 'lat')), may hold values from 0 to 8, as said below
- drift_cell: int32 [2, 2097152], P(None, ('lon', 'lat')), may hold values from 0 to 8191
- drift_weight: float32 [4, 2, 2097152], P(None, None, ('lon', 'lat')), may hold values from 0 to 1, as said below
- drift_obs: float32 [2, 2, 2097152], P(None, None, ('lon', 'lat')), may hold values from -6 to 6
- drift_precision: float32 [2, 2097152], P(None, ('lon', 'lat')), may hold values from 0.1 to 8, as said below
Outputs:
- grad_initial: float32 [2, 8, 4096, 1024], P(None, None, 'lon', 'lat')
- grad_controls: float32 [4, 2, 256, 64], replicated
The draws below stay inside these ranges and needn't reach their ends.
Inputs may be any that keep to these rules, and one draw needn't show every extreme that they name: `depth_levels`: the first and last latitude rows of the grid are land (0). `drift_move`: code d means that at that step the drifter lies in the block of the device at lon offset d // 3 - 1 (periodic) and lat offset d % 3 - 1 from its home block, column n having home block n // 4096 in lon-major order; no code leaves the latitude range. For each step and home block at most 128 drifters carry any one code other than 4; in every draw some block receives exactly 128 from each of its neighbours. `drift_cell`: index cx * 256 + cy of the cell within the owning block. `drift_weight`: bilinear weights of the corners (cell, next in longitude, next in latitude, both); non-negative, summing to one. `drift_precision`: Positive.
All inputs are finite; a program needn't handle non-finite values.
Results may differ from the reference program's by a relative error of at most 0.0003.
Values sent between devices are 32-bit elements; how exact they have to be, the bound alone decides.
No kernel may reach another device: no remote copies, remote signals or barrier semaphores. Data moves between devices by JAX's collectives and lax.ppermute only.
A program may use at most 128 MiB of HBM per device.

```python
import math
import jax
import jax.numpy as jnp
from jax import lax

CELLS_LON = 32
CELLS_LAT = 256
LEVELS = 8
STEPS = 2
PERIODS = 4
REFINE = 16
DRIFT_DEV = 4096
CAPACITY = 128
GRID_LON = 4096
GRID_LAT = 1024
CTRL_LON = 256
CTRL_LAT = 64
DRIFTERS = 2097152
N_LON = 128
N_LAT = 4


def draw_depth_levels(key, part):
    key = jax.random.fold_in(key, 11)
    depth = jax.random.randint(key, (GRID_LON, GRID_LAT), -(LEVELS // 4) - 1, LEVELS + 1)
    depth = jnp.maximum(depth, 0)
    row_ids = jnp.arange(GRID_LAT, dtype=jnp.int32)[None, :]
    polar = (row_ids == 0) | (row_ids == GRID_LAT - 1)
    return jnp.where(polar, 0, depth).astype(jnp.int32)


def draw_drift_move(key, part):
    key = jax.random.fold_in(key, 12)
    crowd_key, count_key, order_key, pick_key = jax.random.split(key, 4)
    devices_all = N_LON * N_LAT
    device_ids = jnp.arange(devices_all, dtype=jnp.int32)
    chosen = jax.random.randint(pick_key, (), 0, devices_all)
    crowded = (jax.random.randint(crowd_key, (devices_all,), 0, 4) == 0) | (device_ids == chosen)
    code_list = jnp.array([0, 1, 2, 3, 5, 6, 7, 8], jnp.int32)
    lon_offset = code_list // 3 - 1
    lat_offset = code_list % 3 - 1
    home_lon = device_ids // N_LAT
    home_lat = device_ids % N_LAT
    dest_lon = (home_lon[:, None] + lon_offset[None]) % N_LON
    dest_lat = home_lat[:, None] + lat_offset[None]
    inside = (dest_lat >= 0) & (dest_lat < N_LAT)
    dest_crowded = crowded[dest_lon * N_LAT + jnp.clip(dest_lat, 0, N_LAT - 1)]
    partial_counts = jax.random.randint(count_key, (STEPS, devices_all, 8), CAPACITY // 4, CAPACITY)
    counts = jnp.where(inside[None], jnp.where(dest_crowded[None], CAPACITY, partial_counts), 0)
    bounds = jnp.cumsum(counts, axis=-1)
    positions = jnp.arange(DRIFT_DEV, dtype=jnp.int32)
    bucket = jnp.sum((positions[None, None, :, None] >= bounds[:, :, None, :]).astype(jnp.int32), axis=-1)
    code_table = jnp.array([0, 1, 2, 3, 5, 6, 7, 8, 4], jnp.int32)
    sorted_codes = code_table[bucket]
    scores = jax.random.randint(order_key, (STEPS, devices_all, DRIFT_DEV), 0, 2 ** 30)
    ordering = jnp.argsort(scores, axis=-1, stable=True)
    shuffled = jnp.take_along_axis(sorted_codes, ordering, axis=-1)
    return shuffled.reshape(STEPS, devices_all * DRIFT_DEV).astype(jnp.int32)


def draw_drift_weight(key, part):
    key = jax.random.fold_in(key, 13)
    lon_key, lat_key = jax.random.split(key)
    along = jax.random.uniform(lon_key, (STEPS, DRIFTERS), jnp.float32)
    across = jax.random.uniform(lat_key, (STEPS, DRIFTERS), jnp.float32)
    return jnp.stack([(1.0 - along) * (1.0 - across), along * (1.0 - across), (1.0 - along) * across, along * across])


def draw_drift_precision(key, part):
    key = jax.random.fold_in(key, 14)
    columns = jnp.arange(DRIFTERS, dtype=jnp.int32)
    home_lon = (columns // DRIFT_DEV // N_LAT).astype(jnp.float32)
    spread = jax.random.uniform(key, (STEPS, DRIFTERS), jnp.float32, math.log(0.1), 0.0)
    return jnp.exp(spread) * (1.0 + 2.0 * home_lon[None] / max(N_LON - 1, 1))


def with_ends(drawn, stream_key, smallest, largest):
    spot = [jax.random.randint(jax.random.fold_in(stream_key, axis), (), 0, length) for axis, length in enumerate(drawn.shape)]
    widest = drawn.shape.index(max(drawn.shape))
    next_to = spot[:widest] + [(spot[widest] + 1) % drawn.shape[widest]] + spot[widest + 1:]
    return drawn.at[tuple(spot)].set(smallest).at[tuple(next_to)].set(largest)


def level_of(key, shape, pieces, low, high):
    def one(dim, blocks):
        steps = jax.random.uniform(jax.random.fold_in(jax.random.fold_in(key, 6), dim), (blocks,), jnp.float32, low / len(pieces), high / len(pieces))
        return jnp.repeat(jnp.exp(steps), shape[dim] // blocks).reshape((-1,) + (1,) * (len(shape) - dim - 1))

    level = one(*pieces[0])
    for cut in pieces[1:]:
        level = level * one(*cut)
    return level


def gaussian(own_key, shape, scale, reach, cuts=(), kind=jnp.bfloat16):
    drawn = scale * jax.random.normal(own_key, shape, jnp.float32)
    if cuts:
        drawn = drawn * level_of(own_key, shape, cuts, -0.22, 0.18)
    return jnp.clip(drawn, -reach, reach).astype(kind)


def setup_inputs(seed: int = 0) -> dict:
    key_list = jax.random.split(jax.random.key(seed), 10)
    initial = gaussian(key_list[0], (2, LEVELS, GRID_LON, GRID_LAT), 1.0, 6.0, ((2, 128), (3, 4)), jnp.float32)
    depth_levels = draw_depth_levels(jax.random.fold_in(key_list[9], 71), 0)
    mixing = jnp.clip(jnp.exp(math.log(0.2) - 2.3025851 * jax.random.uniform(key_list[2], (GRID_LON, GRID_LAT), jnp.float32) ** level_of(key_list[2], (GRID_LON, GRID_LAT), ((0, 128), (1, 4)), -0.2, 0.2)), 0.02, 0.2)
    controls = gaussian(key_list[3], (PERIODS, 2, CTRL_LON, CTRL_LAT), 1.0, 6.0, (), jnp.float32)
    drift_move = draw_drift_move(jax.random.fold_in(key_list[9], 71), 0)
    drift_cell = with_ends(jax.random.randint(key_list[5], (STEPS, DRIFTERS), 0, CELLS_LON * CELLS_LAT), jax.random.fold_in(key_list[5], 1), 0, (CELLS_LON * CELLS_LAT) - 1).astype(jnp.int32)
    drift_weight = draw_drift_weight(jax.random.fold_in(key_list[9], 71), 0)
    drift_obs = gaussian(key_list[7], (2, STEPS, DRIFTERS), 1.0, 6.0, ((2, 512),), jnp.float32)
    drift_precision = draw_drift_precision(jax.random.fold_in(key_list[9], 71), 0)
    return dict(initial=initial, depth_levels=depth_levels, mixing=mixing, controls=controls, drift_move=drift_move, drift_cell=drift_cell, drift_weight=drift_weight, drift_obs=drift_obs, drift_precision=drift_precision)


VISCOUS = 0.1
FRICTION = 0.02
ROTATION = 0.3
HIGHEST_PRECISION = lax.Precision.HIGHEST

def coarse_weights(points, span_count, refine, offset, periodic):
    shifted = points - refine // 2
    low_point = shifted // refine
    fraction = ((shifted - low_point * refine).astype(jnp.float32) + 0.5) / refine
    high_point = low_point + 1 - offset
    low_point = low_point - offset
    if periodic:
        low_point = low_point % span_count
        high_point = high_point % span_count
    return (1.0 - fraction)[:, None] * jax.nn.one_hot(low_point, span_count, dtype=jnp.float32) + fraction[:, None] * jax.nn.one_hot(high_point, span_count, dtype=jnp.float32)

def period_weights(steps_total, periods):
    time_table = []
    for step_index in range(steps_total):
        position = (step_index + 0.5) * (periods - 1) / steps_total
        time_table.append([max(0.0, 1.0 - abs(position - period)) for period in range(periods)])
    return time_table

def horizontal(values):
    to_east = jnp.roll(values, -1, axis=-2)
    to_west = jnp.roll(values, 1, axis=-2)
    zeros_row = jnp.zeros_like(values[..., :1])
    to_north = jnp.concatenate([values[..., 1:], zeros_row], axis=-1)
    to_south = jnp.concatenate([zeros_row, values[..., :-1]], axis=-1)
    return to_east + to_west + to_north + to_south - 4.0 * values

def vertical(values):
    above_level = jnp.concatenate([values[:, :1], values[:, :-1]], axis=1)
    below_level = jnp.concatenate([values[:, 1:], values[:, -1:]], axis=1)
    return above_level + below_level - 2.0 * values

def reference(initial, depth_levels, mixing, controls, drift_move, drift_cell, drift_weight, drift_obs, drift_precision):
    wet_mask = (jnp.arange(LEVELS, dtype=jnp.int32)[:, None, None] < depth_levels[None]).astype(jnp.float32)
    row_ids = jnp.arange(GRID_LAT, dtype=jnp.int32)
    rotation = ROTATION * jnp.sin((row_ids.astype(jnp.float32) + 0.5) * (math.pi / GRID_LAT) - 0.5 * math.pi)
    lon_interp = coarse_weights(jnp.arange(GRID_LON, dtype=jnp.int32), CTRL_LON, REFINE, 0, True)
    lat_interp = coarse_weights(row_ids, CTRL_LAT, REFINE, 0, False)
    time_table = period_weights(STEPS, PERIODS)
    columns = jnp.arange(DRIFTERS, dtype=jnp.int32)
    home_device = columns // DRIFT_DEV
    home_lon = home_device // N_LAT
    home_lat = home_device % N_LAT
    owner_lon = (home_lon[None] + drift_move // 3 - 1) % N_LON
    owner_lat = home_lat[None] + drift_move % 3 - 1
    cell_lon = owner_lon * CELLS_LON + drift_cell // CELLS_LAT
    cell_lat = owner_lat * CELLS_LAT + drift_cell % CELLS_LAT
    next_lon = (cell_lon + 1) % GRID_LON
    next_lat = cell_lat + 1
    mean_precision = jnp.sum(drift_precision) / (STEPS * DRIFTERS)

    def forcing_at(controls_now, step_index):
        blended = time_table[step_index][0] * controls_now[0]
        for period in range(1, PERIODS):
            blended = blended + time_table[step_index][period] * controls_now[period]
        across = jnp.einsum('xa,cab->cxb', lon_interp, blended, precision=HIGHEST_PRECISION)
        return jnp.einsum('cxb,yb->cxy', across, lat_interp, precision=HIGHEST_PRECISION)

    def window_cost(initial_now, controls_now):
        ocean_state = wet_mask * initial_now
        running_total = jnp.zeros((), jnp.float32)
        for step_index in range(STEPS):
            turning = jnp.stack([rotation * ocean_state[1], -rotation * ocean_state[0]])
            tendency = ocean_state + mixing * horizontal(ocean_state) + VISCOUS * vertical(ocean_state) - FRICTION * ocean_state + turning
            tendency = tendency.at[:, 0].add(forcing_at(controls_now, step_index))
            ocean_state = wet_mask * tendency
            surface = jnp.pad(ocean_state[:, 0], ((0, 0), (0, 0), (0, 1)))
            lon_here = cell_lon[step_index]
            lat_here = cell_lat[step_index]
            lon_next = next_lon[step_index]
            lat_next = next_lat[step_index]
            modeled = drift_weight[0, step_index] * surface[:, lon_here, lat_here]
            modeled = modeled + drift_weight[1, step_index] * surface[:, lon_next, lat_here]
            modeled = modeled + drift_weight[2, step_index] * surface[:, lon_here, lat_next]
            modeled = modeled + drift_weight[3, step_index] * surface[:, lon_next, lat_next]
            mismatch = modeled - drift_obs[:, step_index]
            running_total = running_total + jnp.sum(drift_precision[step_index] * lax.optimization_barrier(jnp.sum(mismatch * mismatch, axis=0)))
        return running_total / (2.0 * mean_precision)
    grad_initial, grad_controls = jax.grad(window_cost, argnums=(0, 1))(initial, controls)
    return (grad_initial, grad_controls)
```

```python
import functools
import math

import jax
import jax.numpy as jnp
from jax import lax
from jax.experimental import pallas as pl
from jax.experimental.pallas import tpu as pltpu
from jax.sharding import PartitionSpec as P

CAPACITY = 128
VISCOUS = 0.1
FRICTION = 0.02
ROTATION = 0.3
STEPS = 2
DEPTH = STEPS + 1
CODES = (0, 1, 2, 3, 5, 6, 7, 8)
FIELDS = 8
PLANES = 2 * DEPTH + 2
LOW, HIGH = 2, 3
X0, Y0 = 8, 128
GROUP = 32
F32, BF16 = jnp.float32, jnp.bfloat16
VMEM = pltpu.CompilerParams(vmem_limit_bytes=48 * 1024 * 1024)


def iota(shape, dim):
    return lax.broadcasted_iota(jnp.int32, shape, dim)


def split(value):
    high = value.astype(BF16)
    return high, (value - high.astype(F32)).astype(BF16)


def dot(a, b):
    return lax.dot_general(a, b, (((1,), (0,)), ((), ())), preferred_element_type=F32)


def dot_lanes(a, b):
    return lax.dot_general(a, b, (((1,), (1,)), ((), ())), preferred_element_type=F32)


def roll(value, shift, axis):
    return pltpu.roll(value, shift % value.shape[axis], axis)


def period_weights(steps_total, periods):
    table = []
    for step in range(steps_total):
        position = (step + 0.5) * (periods - 1) / steps_total
        table.append([max(0.0, 1.0 - abs(position - period)) for period in range(periods)])
    return table


def pack_kernel(move, cell, weight, obs, prec, init, depth, mixing, fields, east, west, south, north):
    count = move.shape[1]
    for step in range(STEPS):
        base = step * FIELDS
        for i in range(4):
            fields[base + i : base + i + 1, :] = weight[i, step : step + 1, :]
        for i in range(2):
            fields[base + 4 + i : base + 5 + i, :] = obs[i, step : step + 1, :]
        fields[base + 6 : base + 7, :] = prec[step : step + 1, :]
        fields[base + 7 : base + 8, :] = cell[step : step + 1, :].astype(F32)
    rows = init.shape[2]
    planes = [init.at[c, k] for c in range(2) for k in range(DEPTH)]
    for p in range(PLANES):
        if p < 2 * DEPTH:
            first, last = planes[p][:HIGH, :], planes[p][rows - LOW :, :]
        elif p == 2 * DEPTH:
            first, last = depth[:HIGH, :].astype(F32), depth[rows - LOW :, :].astype(F32)
        else:
            first, last = mixing[:HIGH, :], mixing[rows - LOW :, :]
        west[3 * FIELDS + HIGH * p : 3 * FIELDS + HIGH * (p + 1), :] = first
        east[3 * FIELDS + LOW * p : 3 * FIELDS + LOW * (p + 1), :] = last
    width = 256
    triangle = (iota((width, width), 0) <= iota((width, width), 1)).astype(F32).astype(BF16)
    code = iota((8, 1), 0)
    code = code + (code >= 4).astype(jnp.int32)
    carry = [jnp.zeros((8, 1), F32) for _ in range(STEPS)]
    packed = [jnp.zeros((8 * 2 * FIELDS, CAPACITY), F32) for _ in range(STEPS)]
    slot = iota((CAPACITY, width), 0)
    for at in range(0, count, width):
        for step in range(STEPS):
            match = (move[step : step + 1, at : at + width] == code).astype(F32)
            rank = dot(match.astype(BF16), triangle) + carry[step]
            carry[step] = rank[:, width - 1 :]
            place = jnp.sum(match * (rank - 1.0), axis=0, keepdims=True).astype(jnp.int32)
            spots = (slot == place).astype(F32).astype(BF16)
            record = fields[step * FIELDS : (step + 1) * FIELDS, at : at + width]
            high, low = split(record)
            both = jnp.concatenate([high.astype(F32), low.astype(F32)], axis=0)
            masked = jnp.concatenate([both * match[d : d + 1] for d in range(8)], axis=0)
            packed[step] = packed[step] + dot_lanes(masked.astype(BF16), spots)
    for step in range(STEPS):
        lanes = slice(step * CAPACITY, (step + 1) * CAPACITY)
        for d in range(8):
            at = d * 2 * FIELDS
            record = packed[step][at : at + FIELDS] + packed[step][at + FIELDS : at + 2 * FIELDS]
            code = CODES[d]
            if code // 3 == 1:
                (south if code % 3 == 0 else north)[:, lanes] = record
            else:
                row = (code % 3) * FIELDS
                (west if code // 3 == 0 else east)[row : row + FIELDS, lanes] = record
    for step in range(STEPS):
        row = step * FIELDS + 6
        fields[row : row + 1, :] = jnp.where(move[step : step + 1, :] == 4, prec[step : step + 1, :], 0.0)


def extend_lon(ext, p, own, from_west, from_east, rows, cells_lat):
    lanes = slice(Y0, Y0 + cells_lat)
    ext[p, X0 : X0 + rows, lanes] = own
    at = 3 * FIELDS + LOW * p
    ext[p, X0 - LOW : X0, lanes] = from_west[at : at + LOW, :]
    at = 3 * FIELDS + HIGH * p
    ext[p, X0 + rows : X0 + rows + HIGH, lanes] = from_east[at : at + HIGH, :]


def merge_kernel(init, depth, mixing, to_south, to_north, from_west, from_east, ext, south, north):
    rows, cells_lat = depth.shape
    ext[...] = jnp.zeros_like(ext)
    for p in range(PLANES):
        if p < 2 * DEPTH:
            own = init[p // DEPTH, p % DEPTH]
        else:
            own = depth[...].astype(F32) if p == 2 * DEPTH else mixing[...]
        extend_lon(ext, p, own, from_west, from_east, rows, cells_lat)
    tall = ext.shape[1]
    lane = iota((tall, 128), 1)
    first = jnp.zeros((tall, 128), F32)
    last = jnp.zeros((tall, 128), F32)
    for p in range(PLANES):
        head = jnp.where(lane < HIGH, ext[p, :, Y0 : Y0 + 128], 0.0)
        tail = jnp.where(lane >= 128 - LOW, ext[p, :, Y0 + cells_lat - 128 : Y0 + cells_lat], 0.0)
        first = first + roll(head, HIGH * p, 1)
        last = last + roll(tail, -LOW * p, 1)
    for out, kept, row, strip in ((south, to_south, 0, first), (north, to_north, 2, last)):
        out[0:FIELDS, :] = kept[...]
        out[FIELDS : 2 * FIELDS, :] = from_west[row * FIELDS : (row + 1) * FIELDS, :]
        out[2 * FIELDS : 3 * FIELDS, :] = from_east[row * FIELDS : (row + 1) * FIELDS, :]
        out[3 * FIELDS :, 0:128] = strip[: tall // 2]
        out[3 * FIELDS :, 128:] = strip[tall // 2 :]


def lap(v):
    return roll(v, 1, 0) + roll(v, -1, 0) + roll(v, 1, 1) + roll(v, -1, 1) - 4.0 * v


def vz(column, k, levels):
    above = column[max(k - 1, 0)]
    below = min(k + 1, levels - 1)
    total = above - 2.0 * column[k] if k < len(column) else above
    return total + column[below] if below < len(column) else total


def tendency(v, k, mixing, rotation, levels):
    out = []
    for c in range(2):
        value = v[c][k] + mixing(v[c][k]) + VISCOUS * vz(v[c], k, levels) - FRICTION * v[c][k]
        turned = rotation * v[1 - c][k]
        out.append(value + turned if c == 0 else value - turned)
    return out


def main_kernel(
    levels, refine, lon_count, lat_count, controls, fields, precision, from_west, from_east, from_south, from_north,
    padded, partial, share, to_west, to_east, ext, spot,
):
    rows, cells_lat = partial.shape[1] - 16, partial.shape[2] - 256
    tall, wide = ext.shape[1:]
    lon_index, lat_index = lax.axis_index("lon"), lax.axis_index("lat")
    grid_lat = cells_lat * lat_count
    periods, _, ctrl_lon, ctrl_lat = controls.shape
    table = period_weights(STEPS, periods)
    lane = iota((tall, 128), 1)
    half = tall // 2
    below = jnp.concatenate([from_south[3 * FIELDS :, 0:128], from_south[3 * FIELDS :, 128:]], axis=0)
    above = jnp.concatenate([from_north[3 * FIELDS :, 0:128], from_north[3 * FIELDS :, 128:]], axis=0)
    full = []
    for p in range(PLANES):
        left = jnp.where(lane >= 128 - LOW, roll(below, LOW * p, 1), 0.0)
        right = jnp.where(lane < HIGH, roll(above, -HIGH * p, 1), 0.0)
        full.append(jnp.concatenate([left, padded[p, :, Y0 : Y0 + cells_lat], right], axis=1))
    mixing = full[2 * DEPTH + 1]
    wet = [(full[2 * DEPTH] > float(k)).astype(F32) for k in range(DEPTH)]
    row_ids = iota((1, wide), 1) - Y0 + lat_index * cells_lat
    rotation = ROTATION * jnp.sin((row_ids.astype(F32) + 0.5) * (math.pi / grid_lat) - 0.5 * math.pi)
    offset = iota((tall, ctrl_lon), 0) - X0 + lon_index * rows - refine // 2
    low = lax.shift_right_arithmetic(offset, refine.bit_length() - 1)
    part = ((offset - low * refine).astype(F32) + 0.5) / refine
    column = iota((tall, ctrl_lon), 1)
    wrapped, after = (low + ctrl_lon) % ctrl_lon, (low + 1 + ctrl_lon) % ctrl_lon
    lon_interp = jnp.where(column == wrapped, 1.0 - part, 0.0) + jnp.where(column == after, part, 0.0)
    offset = iota((ctrl_lat, wide), 1) - Y0 + lat_index * cells_lat - refine // 2
    low = lax.shift_right_arithmetic(offset, refine.bit_length() - 1)
    part = ((offset - low * refine).astype(F32) + 0.5) / refine
    column = iota((ctrl_lat, wide), 0)
    lat_interp = jnp.where(column == low, 1.0 - part, 0.0) + jnp.where(column == low + 1, part, 0.0)
    lon_interp, lat_interp = lon_interp.astype(BF16), lat_interp.astype(BF16)
    forcing = []
    for step in range(STEPS):
        forcing.append([])
        for c in range(2):
            blended = table[step][0] * controls[0, c]
            for period in range(1, periods):
                blended = blended + table[step][period] * controls[period, c]
            high, low = split(blended)
            high, low = split(dot(lon_interp, high) + dot(lon_interp, low))
            forcing[step].append(dot(high, lat_interp) + dot(low, lat_interp))
    state = [[wet[k] * full[c * DEPTH + k] for k in range(DEPTH)] for c in range(2)]
    surfaces = []
    for step in range(STEPS):
        ahead = [[], []]
        for k in range(DEPTH - 1 - step):
            moved = tendency(state, k, lambda v: mixing * lap(v), rotation, levels)
            for c in range(2):
                value = moved[c] + forcing[step][c] if k == 0 else moved[c]
                ahead[c].append(wet[k] * value)
        state = ahead
        surfaces.append([state[0][0], state[1][0]])
    strip = rows + 8
    chunk = 512
    lat_of = iota((cells_lat, chunk), 0)
    lon_of = iota((strip, chunk), 0)
    sources = []
    for step in range(STEPS):
        views = []
        for c in range(2):
            surface = surfaces[step][c][X0 : X0 + strip]
            views += [surface[:, Y0 : Y0 + cells_lat], roll(surface, -1, 1)[:, Y0 : Y0 + cells_lat]]
        views_high, views_low = split(jnp.concatenate(views, axis=0))

        def spread(record, total):
            cell = record[7:8].astype(jnp.int32)
            lon = lax.shift_right_logical(cell, cells_lat.bit_length() - 1)
            lat = cell & (cells_lat - 1)
            hot = (lat_of == lat).astype(F32).astype(BF16)
            found = dot(views_high, hot) + dot(views_low, hot)
            here, there = lon_of == lon, lon_of == lon + 1
            near = jnp.where(here, record[0:1], jnp.where(there, record[1:2], 0.0))
            far = jnp.where(here, record[2:3], jnp.where(there, record[3:4], 0.0))
            terms = []
            for c in range(2):
                at = 2 * c * strip
                seen = near * found[at : at + strip] + far * found[at + strip : at + 2 * strip]
                miss = jnp.sum(seen, axis=0, keepdims=True) - record[4 + c : 5 + c]
                miss = record[6:7] * miss
                terms += [near * miss, far * miss]
            high, low = split(jnp.concatenate(terms, axis=0))
            return total + dot_lanes(high, hot) + dot_lanes(low, hot)

        total = jnp.zeros((4 * strip, cells_lat), F32)
        for at in range(0, fields.shape[1], chunk):
            total = spread(fields[step * FIELDS : (step + 1) * FIELDS, at : at + chunk], total)
        lanes = slice(step * CAPACITY, (step + 1) * CAPACITY)
        came = [from_west[FIELDS : 2 * FIELDS, lanes], from_east[FIELDS : 2 * FIELDS, lanes]]
        came += [message[i * FIELDS : (i + 1) * FIELDS, lanes] for message in (from_south, from_north) for i in range(3)]
        for at in range(0, 8, chunk // CAPACITY):
            total = spread(jnp.concatenate(came[at : at + chunk // CAPACITY], axis=1), total)
        sources.append([])
        for c in range(2):
            at = 2 * c * strip
            spot[...] = jnp.zeros_like(spot)
            spot[0, X0 : X0 + strip, Y0 : Y0 + cells_lat] = total[at : at + strip]
            spot[1, X0 : X0 + strip, Y0 : Y0 + cells_lat] = total[at + strip : at + 2 * strip]
            sources[step].append(spot[0] + roll(spot[1], 1, 1))
    adjoint = None
    nudges = [None] * STEPS
    for step in reversed(range(STEPS)):
        if adjoint is None:
            adjoint = [[sources[step][c]] for c in range(2)]
        else:
            adjoint = [[adjoint[c][0] + sources[step][c]] + adjoint[c][1:] for c in range(2)]
        nudged = [[wet[k] * adjoint[c][k] for k in range(len(adjoint[c]))] for c in range(2)]
        nudges[step] = [nudged[0][0], nudged[1][0]]
        reach = len(nudged[0])
        adjoint = [[], []]
        for k in range(reach):
            moved = tendency(nudged, k, lambda v: lap(mixing * v), -rotation, levels)
            for c in range(2):
                adjoint[c].append(moved[c])
        for c in range(2):
            adjoint[c].append(VISCOUS * vz(nudged[c], reach, levels))
    for c in range(2):
        for k in range(DEPTH):
            p = c * DEPTH + k
            ext[p] = adjoint[c][k]
            partial[p] = adjoint[c][k]
            to_west[LOW * p : LOW * (p + 1), :] = ext[p, X0 - LOW : X0, :]
            to_east[HIGH * p : HIGH * (p + 1), :] = ext[p, X0 + rows : X0 + rows + HIGH, :]
    offset = iota((wide, 128), 0) - Y0 - refine // 2
    low = lax.shift_right_arithmetic(offset, refine.bit_length() - 1)
    part = ((offset - low * refine).astype(F32) + 0.5) / refine
    column = iota((wide, 128), 1) % GROUP - 1
    onto_lat = jnp.where(column == low, 1.0 - part, 0.0) + jnp.where(column == low + 1, part, 0.0)
    onto_lat = onto_lat.astype(BF16)
    offset = iota((tall, 128), 0) - X0 - refine // 2
    low = lax.shift_right_arithmetic(offset, refine.bit_length() - 1)
    part = ((offset - low * refine).astype(F32) + 0.5) / refine
    column = iota((tall, 128), 1) // GROUP - 1
    onto_lon = jnp.where(column == low, 1.0 - part, 0.0) + jnp.where(column == low + 1, part, 0.0)
    for step in range(STEPS):
        for c in range(2):
            high, low = split(nudges[step][c])
            across = dot(high, onto_lat) + dot(low, onto_lat)
            row = 2 * step + c
            share[row : row + 1, :] = jnp.sum(onto_lon * across, axis=0, keepdims=True)
    weight = jnp.sum(jnp.sum(precision[...], axis=0, keepdims=True), axis=1, keepdims=True)
    share[0:1, :] = jnp.where(iota((1, 128), 1) == GROUP - 1, weight, share[0:1, :])


def join_kernel(partial, from_west, from_east, own, south, north):
    rows, cells_lat = own.shape[1:]
    lane = iota((rows, 128), 1)
    first = jnp.zeros((rows, 128), F32)
    last = jnp.zeros((rows, 128), F32)
    for p in range(2 * DEPTH):
        partial[p, X0 : X0 + HIGH, :] += from_west[HIGH * p : HIGH * (p + 1), :]
        partial[p, X0 + rows - LOW : X0 + rows, :] += from_east[LOW * p : LOW * (p + 1), :]
        block = partial[p, X0 : X0 + rows, :]
        own[p] = block[:, Y0 : Y0 + cells_lat]
        tail = jnp.where(lane >= 128 - LOW, block[:, Y0 - 128 : Y0], 0.0)
        head = jnp.where(lane < HIGH, block[:, Y0 + cells_lat : Y0 + cells_lat + 128], 0.0)
        first = first + roll(tail, -LOW * p, 1)
        last = last + roll(head, HIGH * p, 1)
    south[...] = first
    north[...] = last


def finish_kernel(normalizer, lat_count, own, depth, from_south, from_north, shares, grad, out):
    levels, rows, cells_lat = grad.shape[1:]
    periods = out.shape[0]
    table = period_weights(STEPS, periods)
    lon_count = out.shape[2] // 2
    per = out.shape[3] // lat_count
    lane = iota(shares.shape, 1)
    row = iota(shares.shape, 0)
    held = jnp.where((lane == GROUP - 1) & (row % (2 * STEPS) == 0), shares[...], 0.0)
    scale = normalizer / jnp.sum(jnp.sum(held, axis=0, keepdims=True), axis=1, keepdims=True)
    side = iota((rows, 128), 1)
    wet_levels = depth[...]
    for c in range(2):
        for k in range(levels):
            if k >= DEPTH:
                grad[c, k] = jnp.zeros((rows, cells_lat), F32)
                continue
            p = c * DEPTH + k
            low = jnp.where(side < HIGH, roll(from_south[...], -HIGH * p, 1), 0.0)
            high = jnp.where(side >= 128 - LOW, roll(from_north[...], LOW * p, 1), 0.0)
            value = own[p] + jnp.concatenate([low, high], axis=1)
            grad[c, k] = jnp.where(wet_levels > k, value * scale, 0.0)
    source = iota((128, 384), 0)
    target = iota((128, 384), 1)
    a, b = source // GROUP, source % GROUP
    kind, i, column = target // 128, target % 128 // 64, target % 64
    right_row = ((kind == 0) & (a == i + 1)) | ((kind == 1) & (a == 3) & (i == 0)) | ((kind == 2) & (a == 0) & (i == 1))
    right_row = right_row & (b < per + 2)
    gathered = [jnp.zeros((lon_count, 384), F32) for _ in range(2 * STEPS)]
    for m in range(lat_count):
        pick = (right_row & (column == per * m - 1 + b)).astype(F32).astype(BF16)
        for t in range(2 * STEPS):
            high, low = split(shares[pl.ds(m * 2 * STEPS + t, lon_count, stride=lat_count * 2 * STEPS), :])
            gathered[t] = gathered[t] + dot(high, pick) + dot(low, pick)
    scaled = []
    for t in range(2 * STEPS):
        part = gathered[t]
        scaled.append(scale * (part[:, :128] + roll(part[:, 128:256], 1, 0) + roll(part[:, 256:], -1, 0)))
    for period in range(periods):
        for c in range(2):
            value = table[0][period] * scaled[c]
            for step in range(1, STEPS):
                value = value + table[step][period] * scaled[2 * step + c]
            for i in range(2):
                out[period, c, pl.ds(i, lon_count, stride=2), :] = value[:, 64 * i : 64 * i + 64]


def around(value, distance):
    count = lax.axis_size("lon")
    return lax.ppermute(value, "lon", [(i, (i + distance) % count) for i in range(count)])


def along(value, distance):
    count = lax.axis_size("lat")
    return lax.ppermute(value, "lat", [(i, i + distance) for i in range(max(0, -distance), min(count, count - distance))])


def whole(shape):
    return pl.BlockSpec(shape, lambda i: (0,) * len(shape))


def call(kernel, ins, outs, blocks=None, scratch=(), **kwargs):
    blocks = blocks or {}
    return pl.pallas_call(
        kernel,
        grid=(1,),
        out_shape=[jax.ShapeDtypeStruct(shape, F32) for shape in outs],
        in_specs=[whole(blocks.get(i, value.shape)) for i, value in enumerate(ins)],
        out_specs=[whole(shape) for shape in outs],
        scratch_shapes=[pltpu.VMEM(shape, F32) for shape in scratch],
        compiler_params=VMEM,
        **kwargs,
    )(*ins)


def shards(
    initial, depth_levels, mixing, controls, drift_move, drift_cell, drift_weight, drift_obs, drift_precision
):
    _, levels, rows, cells_lat = initial.shape
    periods, _, ctrl_lon, ctrl_lat = controls.shape
    count = drift_move.shape[1]
    lon_count, lat_count = lax.axis_size("lon"), lax.axis_size("lat")
    refine = rows * lon_count // ctrl_lon
    tall, wide = rows + 16, cells_lat + 256
    surface = (2, DEPTH, rows, cells_lat)
    lon_low, lon_high = (3 * FIELDS + LOW * PLANES, 256), (3 * FIELDS + HIGH * PLANES, 256)
    fields, east, west, south, north = call(
        pack_kernel,
        (drift_move, drift_cell, drift_weight, drift_obs, drift_precision, initial, depth_levels, mixing),
        ((STEPS * FIELDS, count), lon_low, lon_high, (FIELDS, 256), (FIELDS, 256)),
        {5: surface},
    )
    from_west, from_east = around(east, 1), around(west, -1)
    message = (3 * FIELDS + tall // 2, 256)
    padded, south, north = call(
        merge_kernel,
        (initial, depth_levels, mixing, south, north, from_west, from_east),
        ((PLANES, tall, wide), message, message),
        {0: surface},
    )
    from_south, from_north = along(north, 1), along(south, -1)
    partial, share, to_west, to_east = call(
        functools.partial(main_kernel, levels, refine, lon_count, lat_count),
        (controls, fields, drift_precision, from_west, from_east, from_south, from_north, padded),
        ((2 * DEPTH, tall, wide), (2 * STEPS, 128), (2 * DEPTH * LOW, wide), (2 * DEPTH * HIGH, wide)),
        scratch=((2 * DEPTH, tall, wide), (2, tall, wide)),
    )
    shares = lax.all_gather(share, ("lon", "lat"), axis=0, tiled=True)
    from_west, from_east = around(to_east, 1), around(to_west, -1)
    own, to_south, to_north = call(
        join_kernel,
        (partial, from_west, from_east),
        ((2 * DEPTH, rows, cells_lat), (rows, 128), (rows, 128)),
    )
    from_south, from_north = along(to_north, 1), along(to_south, -1)
    grad_initial, grad_controls = call(
        functools.partial(finish_kernel, float(STEPS * count * lon_count * lat_count), lat_count),
        (own, depth_levels, from_south, from_north, shares),
        (initial.shape, controls.shape),
    )
    return grad_initial, grad_controls


def solution(mesh):
    return jax.shard_map(
        shards,
        mesh=mesh,
        in_specs=(
            P(None, None, "lon", "lat"),
            P("lon", "lat"),
            P("lon", "lat"),
            P(),
            P(None, ("lon", "lat")),
            P(None, ("lon", "lat")),
            P(None, None, ("lon", "lat")),
            P(None, None, ("lon", "lat")),
            P(None, ("lon", "lat")),
        ),
        out_specs=(P(None, None, "lon", "lat"), P()),
        check_vma=False,
    )
```

```python
import functools
import math

import jax
import jax.numpy as jnp
from jax import lax
from jax.experimental import pallas as pl
from jax.experimental.pallas import tpu as pltpu
from jax.sharding import PartitionSpec as P

CAPACITY = 128
VISCOUS = 0.1
FRICTION = 0.02
ROTATION = 0.3
STEPS = 2
DEPTH = STEPS + 1
CODES = (0, 1, 2, 3, 5, 6, 7, 8)
FIELDS = 8
PLANES = 2 * DEPTH + 2
LOW, HIGH = 2, 3
X0, Y0 = 8, 128
CORES = 2
RING = 8
GROUP = 32
F32, BF16 = jnp.float32, jnp.bfloat16
MIB = 1024 * 1024


def iota(shape, dim):
    return lax.broadcasted_iota(jnp.int32, shape, dim)


def split(value):
    high = value.astype(BF16)
    return high, (value - high.astype(F32)).astype(BF16)


def dot(a, b):
    return lax.dot_general(a, b, (((1,), (0,)), ((), ())), preferred_element_type=F32)


def dot_lanes(a, b):
    return lax.dot_general(a, b, (((1,), (1,)), ((), ())), preferred_element_type=F32)


def roll(value, shift, axis):
    return pltpu.roll(value, shift % value.shape[axis], axis)


def parity():
    return lax.axis_index("lon") % CORES


def pick(first, second):
    even = parity() == 0
    inner, outer = first[...], second[...]
    return jnp.where(even, outer, inner), jnp.where(even, inner, outer)


def address(east, west, first, second):
    even = parity() == 0
    first[...] = jnp.where(even, east[...], west[...])
    second[...] = jnp.where(even, west[...], east[...])


def interpolation(offset, refine):
    low = lax.shift_right_arithmetic(offset, refine.bit_length() - 1)
    return low, ((offset - low * refine).astype(F32) + 0.5) / refine


def period_weights(steps_total, periods):
    table = []
    for step in range(steps_total):
        position = (step + 0.5) * (periods - 1) / steps_total
        table.append([max(0.0, 1.0 - abs(position - period)) for period in range(periods)])
    return table


def pack_kernel(move, cell, weight, obs, prec, init, depth, mixing, fields, inner, outer, south, north, east, west):
    count = move.shape[1]
    for step in range(STEPS):
        base = step * FIELDS
        for i in range(4):
            fields[base + i : base + i + 1, :] = weight[i, step : step + 1, :]
        for i in range(2):
            fields[base + 4 + i : base + 5 + i, :] = obs[i, step : step + 1, :]
        fields[base + 6 : base + 7, :] = prec[step : step + 1, :]
        fields[base + 7 : base + 8, :] = cell[step : step + 1, :].astype(F32)
    rows = init.shape[2]
    planes = [init.at[c, k] for c in range(2) for k in range(DEPTH)]
    for p in range(PLANES):
        if p < 2 * DEPTH:
            first, last = planes[p][:HIGH, :], planes[p][rows - LOW :, :]
        elif p == 2 * DEPTH:
            first, last = depth[:HIGH, :].astype(F32), depth[rows - LOW :, :].astype(F32)
        else:
            first, last = mixing[:HIGH, :], mixing[rows - LOW :, :]
        west[3 * FIELDS + HIGH * p : 3 * FIELDS + HIGH * (p + 1), :] = first
        east[3 * FIELDS + LOW * p : 3 * FIELDS + LOW * (p + 1), :] = last
    width = 256
    triangle = (iota((width, width), 0) <= iota((width, width), 1)).astype(F32).astype(BF16)
    code = iota((8, 1), 0)
    code = code + (code >= 4).astype(jnp.int32)
    carry = [jnp.zeros((8, 1), F32) for _ in range(STEPS)]
    packed = [jnp.zeros((8 * 2 * FIELDS, CAPACITY), F32) for _ in range(STEPS)]
    slot = iota((CAPACITY, width), 0)
    for at in range(0, count, width):
        for step in range(STEPS):
            match = (move[step : step + 1, at : at + width] == code).astype(F32)
            rank = dot(match.astype(BF16), triangle) + carry[step]
            carry[step] = rank[:, width - 1 :]
            place = jnp.sum(match * (rank - 1.0), axis=0, keepdims=True).astype(jnp.int32)
            spots = (slot == place).astype(F32).astype(BF16)
            record = fields[step * FIELDS : (step + 1) * FIELDS, at : at + width]
            high, low = split(record)
            both = jnp.concatenate([high.astype(F32), low.astype(F32)], axis=0)
            masked = jnp.concatenate([both * match[d : d + 1] for d in range(8)], axis=0)
            packed[step] = packed[step] + dot_lanes(masked.astype(BF16), spots)
    for step in range(STEPS):
        lanes = slice(step * CAPACITY, (step + 1) * CAPACITY)
        for d in range(8):
            at = d * 2 * FIELDS
            record = packed[step][at : at + FIELDS] + packed[step][at + FIELDS : at + 2 * FIELDS]
            code = CODES[d]
            if code // 3 == 1:
                (south if code % 3 == 0 else north)[:, lanes] = record
            else:
                row = (code % 3) * FIELDS
                (west if code // 3 == 0 else east)[row : row + FIELDS, lanes] = record
    for step in range(STEPS):
        row = step * FIELDS + 6
        fields[row : row + 1, :] = jnp.where(move[step : step + 1, :] == 4, prec[step : step + 1, :], 0.0)
    address(east, west, inner, outer)


def extend_lon(ext, p, own, from_west, from_east, rows, cells_lat):
    lanes = slice(Y0, Y0 + cells_lat)
    ext[p, X0 : X0 + rows, lanes] = own
    at = 3 * FIELDS + LOW * p
    ext[p, X0 - LOW : X0, lanes] = from_west[at : at + LOW, :]
    at = 3 * FIELDS + HIGH * p
    ext[p, X0 + rows : X0 + rows + HIGH, lanes] = from_east[at : at + HIGH, :]


def merge_kernel(init, depth, mixing, to_south, to_north, inner, outer, ext, south, north):
    from_west, from_east = pick(inner, outer)
    rows, cells_lat = depth.shape
    ext[...] = jnp.zeros_like(ext)
    for p in range(PLANES):
        if p < 2 * DEPTH:
            own = init[p // DEPTH, p % DEPTH]
        else:
            own = depth[...].astype(F32) if p == 2 * DEPTH else mixing[...]
        extend_lon(ext, p, own, from_west, from_east, rows, cells_lat)
    tall = ext.shape[1]
    lane = iota((tall, 128), 1)
    first = jnp.zeros((tall, 128), F32)
    last = jnp.zeros((tall, 128), F32)
    for p in range(PLANES):
        head = jnp.where(lane < HIGH, ext[p, :, Y0 : Y0 + 128], 0.0)
        tail = jnp.where(lane >= 128 - LOW, ext[p, :, Y0 + cells_lat - 128 : Y0 + cells_lat], 0.0)
        first = first + roll(head, HIGH * p, 1)
        last = last + roll(tail, -LOW * p, 1)
    for out, kept, row, strip in ((south, to_south, 0, first), (north, to_north, 2, last)):
        out[0:FIELDS, :] = kept[...]
        out[FIELDS : 2 * FIELDS, :] = from_west[row * FIELDS : (row + 1) * FIELDS, :]
        out[2 * FIELDS : 3 * FIELDS, :] = from_east[row * FIELDS : (row + 1) * FIELDS, :]
        out[3 * FIELDS :, 0:128] = strip[: tall // 2]
        out[3 * FIELDS :, 128:] = strip[tall // 2 :]


def lap(v):
    return roll(v, 1, 0) + roll(v, -1, 0) + roll(v, 1, 1) + roll(v, -1, 1) - 4.0 * v


def vz(column, k, levels):
    above = column[max(k - 1, 0)]
    below = min(k + 1, levels - 1)
    total = above - 2.0 * column[k] if k < len(column) else above
    return total + column[below] if below < len(column) else total


def tendency(v, k, mixing, rotation, levels):
    out = []
    for c in range(2):
        value = v[c][k] + mixing(v[c][k]) + VISCOUS * vz(v[c], k, levels) - FRICTION * v[c][k]
        turned = rotation * v[1 - c][k]
        out.append(value + turned if c == 0 else value - turned)
    return out


def main_kernel(
    levels, refine, lon_count, lat_count, controls, fields, precision, inner, outer, from_south, from_north,
    padded, partial, share, to_inner, to_outer, ext, spot, to_west, to_east,
):
    from_west, from_east = pick(inner, outer)
    rows, cells_lat = partial.shape[1] - 16, partial.shape[2] - 256
    tall, wide = ext.shape[1:]
    lon_index, lat_index = lax.axis_index("lon"), lax.axis_index("lat")
    grid_lat = cells_lat * lat_count
    periods, _, ctrl_lat, ctrl_lon = controls.shape
    table = period_weights(STEPS, periods)
    lane = iota((tall, 128), 1)
    half = tall // 2
    below = jnp.concatenate([from_south[3 * FIELDS :, 0:128], from_south[3 * FIELDS :, 128:]], axis=0)
    above = jnp.concatenate([from_north[3 * FIELDS :, 0:128], from_north[3 * FIELDS :, 128:]], axis=0)
    full = []
    for p in range(PLANES):
        left = jnp.where(lane >= 128 - LOW, roll(below, LOW * p, 1), 0.0)
        right = jnp.where(lane < HIGH, roll(above, -HIGH * p, 1), 0.0)
        full.append(jnp.concatenate([left, padded[p, :, Y0 : Y0 + cells_lat], right], axis=1))
    mixing = full[2 * DEPTH + 1]
    wet = [(full[2 * DEPTH] > float(k)).astype(F32) for k in range(DEPTH)]
    row_ids = iota((1, wide), 1) - Y0 + lat_index * cells_lat
    rotation = ROTATION * jnp.sin((row_ids.astype(F32) + 0.5) * (math.pi / grid_lat) - 0.5 * math.pi)
    offset = iota((tall, ctrl_lon), 0) - X0 + lon_index * rows - refine // 2
    low, part = interpolation(offset, refine)
    column = iota((tall, ctrl_lon), 1)
    wrapped, after = (low + ctrl_lon) % ctrl_lon, (low + 1 + ctrl_lon) % ctrl_lon
    lon_interp = jnp.where(column == wrapped, 1.0 - part, 0.0) + jnp.where(column == after, part, 0.0)
    offset = iota((ctrl_lat, wide), 1) - Y0 + lat_index * cells_lat - refine // 2
    low, part = interpolation(offset, refine)
    column = iota((ctrl_lat, wide), 0)
    lat_interp = jnp.where(column == low, 1.0 - part, 0.0) + jnp.where(column == low + 1, part, 0.0)
    lon_interp, lat_interp = lon_interp.astype(BF16), lat_interp.astype(BF16)
    forcing = []
    for step in range(STEPS):
        forcing.append([])
        for c in range(2):
            blended = table[step][0] * controls[0, c]
            for period in range(1, periods):
                blended = blended + table[step][period] * controls[period, c]
            high, low = split(blended)
            high, low = split(dot_lanes(lon_interp, high) + dot_lanes(lon_interp, low))
            forcing[step].append(dot(high, lat_interp) + dot(low, lat_interp))
    state = [[wet[k] * full[c * DEPTH + k] for k in range(DEPTH)] for c in range(2)]
    surfaces = []
    for step in range(STEPS):
        ahead = [[], []]
        for k in range(DEPTH - 1 - step):
            moved = tendency(state, k, lambda v: mixing * lap(v), rotation, levels)
            for c in range(2):
                value = moved[c] + forcing[step][c] if k == 0 else moved[c]
                ahead[c].append(wet[k] * value)
        state = ahead
        surfaces.append([state[0][0], state[1][0]])
    strip = rows + 8
    chunk = 512
    lat_of = iota((cells_lat, chunk), 0)
    lon_of = iota((strip, chunk), 0)
    sources = []
    for step in range(STEPS):
        views = []
        for c in range(2):
            surface = surfaces[step][c][X0 : X0 + strip]
            views += [surface[:, Y0 : Y0 + cells_lat], roll(surface, -1, 1)[:, Y0 : Y0 + cells_lat]]
        views_high, views_low = split(jnp.concatenate(views, axis=0))

        def spread(record, total):
            cell = record[7:8].astype(jnp.int32)
            lon = lax.shift_right_logical(cell, cells_lat.bit_length() - 1)
            lat = cell & (cells_lat - 1)
            hot = (lat_of == lat).astype(F32).astype(BF16)
            found = dot(views_high, hot) + dot(views_low, hot)
            here, there = lon_of == lon, lon_of == lon + 1
            near = jnp.where(here, record[0:1], jnp.where(there, record[1:2], 0.0))
            far = jnp.where(here, record[2:3], jnp.where(there, record[3:4], 0.0))
            terms = []
            for c in range(2):
                at = 2 * c * strip
                seen = near * found[at : at + strip] + far * found[at + strip : at + 2 * strip]
                miss = jnp.sum(seen, axis=0, keepdims=True) - record[4 + c : 5 + c]
                miss = record[6:7] * miss
                terms += [near * miss, far * miss]
            high, low = split(jnp.concatenate(terms, axis=0))
            return total + dot_lanes(high, hot) + dot_lanes(low, hot)

        total = jnp.zeros((4 * strip, cells_lat), F32)
        for at in range(0, fields.shape[1], chunk):
            total = spread(fields[step * FIELDS : (step + 1) * FIELDS, at : at + chunk], total)
        lanes = slice(step * CAPACITY, (step + 1) * CAPACITY)
        came = [from_west[FIELDS : 2 * FIELDS, lanes], from_east[FIELDS : 2 * FIELDS, lanes]]
        came += [message[i * FIELDS : (i + 1) * FIELDS, lanes] for message in (from_south, from_north) for i in range(3)]
        for at in range(0, 8, chunk // CAPACITY):
            total = spread(jnp.concatenate(came[at : at + chunk // CAPACITY], axis=1), total)
        sources.append([])
        for c in range(2):
            at = 2 * c * strip
            spot[...] = jnp.zeros_like(spot)
            spot[0, X0 : X0 + strip, Y0 : Y0 + cells_lat] = total[at : at + strip]
            spot[1, X0 : X0 + strip, Y0 : Y0 + cells_lat] = total[at + strip : at + 2 * strip]
            sources[step].append(spot[0] + roll(spot[1], 1, 1))
    adjoint = None
    nudges = [None] * STEPS
    for step in reversed(range(STEPS)):
        if adjoint is None:
            adjoint = [[sources[step][c]] for c in range(2)]
        else:
            adjoint = [[adjoint[c][0] + sources[step][c]] + adjoint[c][1:] for c in range(2)]
        nudged = [[wet[k] * adjoint[c][k] for k in range(len(adjoint[c]))] for c in range(2)]
        nudges[step] = [nudged[0][0], nudged[1][0]]
        reach = len(nudged[0])
        adjoint = [[], []]
        for k in range(reach):
            moved = tendency(nudged, k, lambda v: lap(mixing * v), -rotation, levels)
            for c in range(2):
                adjoint[c].append(moved[c])
        for c in range(2):
            adjoint[c].append(VISCOUS * vz(nudged[c], reach, levels))
    for c in range(2):
        for k in range(DEPTH):
            p = c * DEPTH + k
            ext[p] = adjoint[c][k]
            partial[p] = adjoint[c][k]
            to_west[LOW * p : LOW * (p + 1), :] = ext[p, X0 - LOW : X0, :]
            to_east[HIGH * p : HIGH * (p + 1), :] = ext[p, X0 + rows : X0 + rows + HIGH, :]
    address(to_east, to_west, to_inner, to_outer)
    low, part = interpolation(iota((wide, 4 * GROUP), 0) - Y0 - refine // 2, refine)
    column = iota((wide, 4 * GROUP), 1) % GROUP - 1
    onto_lat = jnp.where(column == low, 1.0 - part, 0.0) + jnp.where(column == low + 1, part, 0.0)
    onto_lat = onto_lat.astype(BF16)
    low, part = interpolation(iota((tall, 4 * GROUP), 0) - X0 - refine // 2, refine)
    column = iota((tall, 4 * GROUP), 1) // GROUP - 1
    onto_lon = jnp.where(column == low, 1.0 - part, 0.0) + jnp.where(column == low + 1, part, 0.0)
    weight = jnp.sum(jnp.sum(precision[...], axis=0, keepdims=True), axis=1, keepdims=True)
    parts = []
    for step in range(STEPS):
        for c in range(2):
            high, rest = split(nudges[step][c])
            across = dot(high, onto_lat) + dot(rest, onto_lat)
            parts.append(jnp.sum(onto_lon * across, axis=0, keepdims=True))
    parts[0] = jnp.where(iota((1, 4 * GROUP), 1) == 4 * GROUP - 1, weight, parts[0])
    share[...] = jnp.broadcast_to(jnp.concatenate(parts, axis=0)[None], share.shape)


def plane_kernel(lat_count, per, shares, out, rows, total):
    members = shares.shape[0]
    ring = members // (CORES * lat_count)
    ctrl_lat = per * lat_count
    for m in range(members):
        rows[4 * m : 4 * m + 4, :] = shares[m]
    total[...] = jnp.zeros_like(total)
    lane = iota((ring, 4 * GROUP), 1)
    height = total.shape[0] // STEPS
    weight = jnp.zeros((ring, 4 * GROUP), F32)
    for core in range(CORES):
        for step in range(STEPS):
            sums = [jnp.zeros((ring, 4 * GROUP), F32) for _ in range(4)]
            for band in range(lat_count):
                for c in range(2):
                    at = 4 * (core * lat_count + band) + 2 * step + c
                    held = rows[pl.ds(at, ring, stride=4 * CORES * lat_count), :]
                    if step == 0 and c == 0:
                        weight = weight + held
                    start = c * ctrl_lat + per * band - 1
                    first, last = max(start, c * ctrl_lat), min(start + per + 1, (c + 1) * ctrl_lat - 1)
                    mine = (lane >= first) & (lane <= last)
                    for a in range(4):
                        sums[a] = sums[a] + jnp.where(mine, roll(held, start - GROUP * a, 1), 0.0)
            for a in range(4):
                at = step * height + 2 * core + a
                total[pl.ds(at, ring, stride=4), :] = total[pl.ds(at, ring, stride=4), :] + sums[a]
    weight = jnp.sum(jnp.where(lane == 4 * GROUP - 1, weight, 0.0), axis=0, keepdims=True)
    weight = jnp.sum(weight, axis=1, keepdims=True)
    total[4 * ring + 2 : 4 * ring + 3, :] = jnp.broadcast_to(weight, (1, 4 * GROUP))
    out[...] = jnp.broadcast_to(total[...][None], out.shape)


def join_kernel(partial, inner, outer, own, south, north):
    from_west, from_east = pick(inner, outer)
    rows, cells_lat = own.shape[1:]
    lane = iota((rows, 128), 1)
    first = jnp.zeros((rows, 128), F32)
    last = jnp.zeros((rows, 128), F32)
    for p in range(2 * DEPTH):
        partial[p, X0 : X0 + HIGH, :] += from_west[HIGH * p : HIGH * (p + 1), :]
        partial[p, X0 + rows - LOW : X0 + rows, :] += from_east[LOW * p : LOW * (p + 1), :]
        block = partial[p, X0 : X0 + rows, :]
        own[p] = block[:, Y0 : Y0 + cells_lat]
        tail = jnp.where(lane >= 128 - LOW, block[:, Y0 - 128 : Y0], 0.0)
        head = jnp.where(lane < HIGH, block[:, Y0 + cells_lat : Y0 + cells_lat + 128], 0.0)
        first = first + roll(tail, -LOW * p, 1)
        last = last + roll(head, HIGH * p, 1)
    south[...] = first
    north[...] = last


def finish_kernel(normalizer, own, depth, from_south, from_north, shares, grad, out, full):
    levels, rows, cells_lat = grad.shape[1:]
    periods, _, ctrl_lat, ctrl_lon = out.shape
    table = period_weights(STEPS, periods)
    members, size = shares.shape[:2]
    span = ctrl_lon // members
    total = shares[0, span + 2 : span + 3, :]
    for m in range(1, members):
        total = total + shares[m, span + 2 : span + 3, :]
    scale = normalizer / total[:, 0:1]
    side = iota((rows, 128), 1)
    wet_levels = depth[...]
    for c in range(2):
        for k in range(levels):
            if k >= DEPTH:
                grad[c, k] = jnp.zeros((rows, cells_lat), F32)
                continue
            p = c * DEPTH + k
            low = jnp.where(side < HIGH, roll(from_south[...], -HIGH * p, 1), 0.0)
            high = jnp.where(side >= 128 - LOW, roll(from_north[...], LOW * p, 1), 0.0)
            value = own[p] + jnp.concatenate([low, high], axis=1)
            grad[c, k] = jnp.where(wet_levels > k, value * scale, 0.0)
    for step in range(STEPS):
        at = step * size // STEPS
        for m in range(members):
            full[step, m * span : (m + 1) * span, :] = shares[m, at + 1 : at + 1 + span, :]
        for m in range(members):
            before, after = (m * span + ctrl_lon - 1) % ctrl_lon, (m + 1) * span % ctrl_lon
            full[step, before : before + 1, :] += shares[m, at : at + 1, :]
            full[step, after : after + 1, :] += shares[m, at + span + 1 : at + span + 2, :]
    scaled = [scale * full[step] for step in range(STEPS)]
    for period in range(periods):
        value = table[0][period] * scaled[0]
        for step in range(1, STEPS):
            value = value + table[step][period] * scaled[step]
        value = value.T
        for c in range(2):
            out[period, c] = value[c * ctrl_lat : (c + 1) * ctrl_lat]


def swap(inner, outer):
    count = lax.axis_size("lon")
    inner = lax.ppermute(inner, "lon", [(i, i ^ 1) for i in range(count)])
    outer = lax.ppermute(outer, "lon", [((i + 1) % count, ((i ^ 1) + 1) % count) for i in range(count)])
    return inner, outer


def gather(copies, chips, stride, whole_chips):
    if copies.shape[0] == 1:
        return copies
    count = lax.axis_size("lat")
    per_chip = CORES * count
    inside = [range(per_chip)] if whole_chips else [(i,) for i in range(per_chip)]
    groups = []
    for base in range(lax.axis_size("lon") // CORES):
        if base // stride % chips == 0:
            for few in inside:
                groups.append([(base + chip * stride) * per_chip + i for chip in range(chips) for i in few])
    return lax.all_to_all(copies, ("lon", "lat"), 0, 0, axis_index_groups=groups, tiled=True)


def along(value, distance):
    count = lax.axis_size("lat")
    return lax.ppermute(value, "lat", [(i, i + distance) for i in range(max(0, -distance), min(count, count - distance))])


def whole(shape):
    return pl.BlockSpec(shape, lambda i: (0,) * len(shape))


def call(kernel, ins, outs, blocks=None, scratch=(), vmem=16):
    blocks = blocks or {}
    return pl.pallas_call(
        kernel,
        grid=(1,),
        out_shape=[jax.ShapeDtypeStruct(shape, F32) for shape in outs],
        in_specs=[whole(blocks.get(i, value.shape)) for i, value in enumerate(ins)],
        out_specs=[whole(shape) for shape in outs],
        scratch_shapes=[pltpu.VMEM(shape, F32) for shape in scratch],
        compiler_params=pltpu.CompilerParams(vmem_limit_bytes=vmem * MIB),
    )(*ins)


def shards(
    initial, depth_levels, mixing, controls, drift_move, drift_cell, drift_weight, drift_obs, drift_precision
):
    _, levels, rows, cells_lat = initial.shape
    periods, _, ctrl_lon, ctrl_lat = controls.shape
    count = drift_move.shape[1]
    lon_count, lat_count = lax.axis_size("lon"), lax.axis_size("lat")
    refine = rows * lon_count // ctrl_lon
    tall, wide = rows + 16, cells_lat + 256
    surface = (2, DEPTH, rows, cells_lat)
    lon_message = (3 * FIELDS + HIGH * PLANES, 256)
    fields, inner, outer, south, north = call(
        pack_kernel,
        (drift_move, drift_cell, drift_weight, drift_obs, drift_precision, initial, depth_levels, mixing),
        ((STEPS * FIELDS, count), lon_message, lon_message, (FIELDS, 256), (FIELDS, 256)),
        {5: surface},
        scratch=(lon_message, lon_message),
        vmem=60,
    )
    inner, outer = swap(inner, outer)
    message = (3 * FIELDS + tall // 2, 256)
    padded, south, north = call(
        merge_kernel,
        (initial, depth_levels, mixing, south, north, inner, outer),
        ((PLANES, tall, wide), message, message),
        {0: surface},
    )
    from_south, from_north = along(north, 1), along(south, -1)
    edge = (2 * DEPTH * HIGH, wide)
    ring = min(RING, lon_count // CORES)
    members = lon_count // (CORES * ring)
    partial, share, inner, outer = call(
        functools.partial(main_kernel, levels, refine, lon_count, lat_count),
        (jnp.swapaxes(controls, 2, 3), fields, drift_precision, inner, outer, from_south, from_north, padded),
        ((2 * DEPTH, tall, wide), (ring * CORES * lat_count, 2 * STEPS, 4 * GROUP), edge, edge),
        scratch=((2 * DEPTH, tall, wide), (2, tall, wide), edge, edge),
    )
    shares = gather(share, ring, 1, True)
    height = -(-(4 * ring + 3) // 8) * 8
    (share,) = call(
        functools.partial(plane_kernel, lat_count, ctrl_lat // lat_count),
        (shares,),
        ((members, STEPS * height, 2 * ctrl_lat),),
        scratch=((4 * ring * CORES * lat_count, 4 * GROUP), (STEPS * height, 2 * ctrl_lat)),
    )
    shares = gather(share, members, ring, False)
    inner, outer = swap(inner, outer)
    own, to_south, to_north = call(
        join_kernel,
        (partial, inner, outer),
        ((2 * DEPTH, rows, cells_lat), (rows, 128), (rows, 128)),
    )
    from_south, from_north = along(to_north, 1), along(to_south, -1)
    grad_initial, grad_controls = call(
        functools.partial(finish_kernel, float(STEPS * count * lon_count * lat_count)),
        (own, depth_levels, from_south, from_north, shares),
        (initial.shape, (periods, 2, ctrl_lat, ctrl_lon)),
        scratch=((STEPS, ctrl_lon, 2 * ctrl_lat),),
    )
    return grad_initial, jnp.swapaxes(grad_controls, 2, 3)


def solution(mesh):
    return jax.shard_map(
        shards,
        mesh=mesh,
        in_specs=(
            P(None, None, "lon", "lat"),
            P("lon", "lat"),
            P("lon", "lat"),
            P(),
            P(None, ("lon", "lat")),
            P(None, ("lon", "lat")),
            P(None, None, ("lon", "lat")),
            P(None, None, ("lon", "lat")),
            P(None, ("lon", "lat")),
        ),
        out_specs=(P(None, None, "lon", "lat"), P()),
        check_vma=False,
    )
```

```python
import functools
import math

import jax
import jax.numpy as jnp
from jax import lax
from jax.experimental import pallas as pl
from jax.experimental.pallas import tpu as pltpu
from jax.sharding import PartitionSpec as P

CAPACITY = 128
VISCOUS = 0.1
FRICTION = 0.02
ROTATION = 0.3
STEPS = 2
DEPTH = STEPS + 1
CODES = (0, 1, 2, 3, 5, 6, 7, 8)
FIELDS = 8
PLANES = 2 * DEPTH + 2
LOW, HIGH = 2, 3
X0, Y0 = 8, 128
CORES = 2
RING = 8
GROUP = 32
F32, BF16 = jnp.float32, jnp.bfloat16
MIB = 1024 * 1024


def iota(shape, dim):
    return lax.broadcasted_iota(jnp.int32, shape, dim)


def split(value):
    high = value.astype(BF16)
    return high, (value - high.astype(F32)).astype(BF16)


def dot(a, b):
    return lax.dot_general(a, b, (((1,), (0,)), ((), ())), preferred_element_type=F32)


def dot_lanes(a, b):
    return lax.dot_general(a, b, (((1,), (1,)), ((), ())), preferred_element_type=F32)


def roll(value, shift, axis):
    return pltpu.roll(value, shift % value.shape[axis], axis)


def parity():
    return lax.axis_index("lon") % CORES


def pick(first, second):
    even = parity() == 0
    inner, outer = first[...], second[...]
    return jnp.where(even, outer, inner), jnp.where(even, inner, outer)


def address(east, west, first, second):
    even = parity() == 0
    first[...] = jnp.where(even, east[...], west[...])
    second[...] = jnp.where(even, west[...], east[...])


def interpolation(offset, refine):
    low = lax.shift_right_arithmetic(offset, refine.bit_length() - 1)
    return low, ((offset - low * refine).astype(F32) + 0.5) / refine


def period_weights(steps_total, periods):
    table = []
    for step in range(steps_total):
        position = (step + 0.5) * (periods - 1) / steps_total
        table.append([max(0.0, 1.0 - abs(position - period)) for period in range(periods)])
    return table


def stage(fields, cell, weight, obs):
    for step in range(STEPS):
        base = step * FIELDS
        for i in range(4):
            fields[base + i : base + i + 1, :] = weight[i, step : step + 1, :]
        for i in range(2):
            fields[base + 4 + i : base + 5 + i, :] = obs[i, step : step + 1, :]
        fields[base + 7 : base + 8, :] = cell[step : step + 1, :].astype(F32)


def own_kernel(refine, lat_count, controls, move, cell, weight, obs, prec, fields, forcing):
    stage(fields, cell, weight, obs)
    for step in range(STEPS):
        row = step * FIELDS + 6
        fields[row : row + 1, :] = jnp.where(move[step : step + 1, :] == 4, prec[step : step + 1, :], 0.0)
    tall, wide = forcing.shape[1:]
    rows, cells_lat = tall - 16, wide - 256
    periods, _, ctrl_lat, ctrl_lon = controls.shape
    table = period_weights(STEPS, periods)
    low, part = interpolation(iota((tall, ctrl_lon), 0) - X0 + lax.axis_index("lon") * rows - refine // 2, refine)
    column = iota((tall, ctrl_lon), 1)
    wrapped, after = (low + ctrl_lon) % ctrl_lon, (low + 1 + ctrl_lon) % ctrl_lon
    lon_interp = jnp.where(column == wrapped, 1.0 - part, 0.0) + jnp.where(column == after, part, 0.0)
    low, part = interpolation(iota((ctrl_lat, wide), 1) - Y0 + lax.axis_index("lat") * cells_lat - refine // 2, refine)
    column = iota((ctrl_lat, wide), 0)
    lat_interp = jnp.where(column == low, 1.0 - part, 0.0) + jnp.where(column == low + 1, part, 0.0)
    lon_interp, lat_interp = lon_interp.astype(BF16), lat_interp.astype(BF16)
    for step in range(STEPS):
        for c in range(2):
            blended = table[step][0] * controls[0, c]
            for period in range(1, periods):
                blended = blended + table[step][period] * controls[period, c]
            high, low = split(blended)
            high, low = split(dot_lanes(lon_interp, high) + dot_lanes(lon_interp, low))
            forcing[2 * step + c] = dot(high, lat_interp) + dot(low, lat_interp)


def pack_kernel(move, cell, weight, obs, prec, init, depth, mixing, inner, outer, beside, fields, east, west):
    count = move.shape[1]
    stage(fields, cell, weight, obs)
    for step in range(STEPS):
        fields[step * FIELDS + 6 : step * FIELDS + 7, :] = prec[step : step + 1, :]
    rows = init.shape[2]
    planes = [init.at[c, k] for c in range(2) for k in range(DEPTH)]
    for p in range(PLANES):
        if p < 2 * DEPTH:
            first, last = planes[p][:HIGH, :], planes[p][rows - LOW :, :]
        elif p == 2 * DEPTH:
            first, last = depth[:HIGH, :].astype(F32), depth[rows - LOW :, :].astype(F32)
        else:
            first, last = mixing[:HIGH, :], mixing[rows - LOW :, :]
        west[3 * FIELDS + HIGH * p : 3 * FIELDS + HIGH * (p + 1), :] = first
        east[3 * FIELDS + LOW * p : 3 * FIELDS + LOW * (p + 1), :] = last
    width = 256
    triangle = (iota((width, width), 0) <= iota((width, width), 1)).astype(F32).astype(BF16)
    code = iota((8, 1), 0)
    code = code + (code >= 4).astype(jnp.int32)
    carry = [jnp.zeros((8, 1), F32) for _ in range(STEPS)]
    packed = [jnp.zeros((8 * 2 * FIELDS, CAPACITY), F32) for _ in range(STEPS)]
    slot = iota((CAPACITY, width), 0)
    for at in range(0, count, width):
        for step in range(STEPS):
            match = (move[step : step + 1, at : at + width] == code).astype(F32)
            rank = dot(match.astype(BF16), triangle) + carry[step]
            carry[step] = rank[:, width - 1 :]
            place = jnp.sum(match * (rank - 1.0), axis=0, keepdims=True).astype(jnp.int32)
            spots = (slot == place).astype(F32).astype(BF16)
            record = fields[step * FIELDS : (step + 1) * FIELDS, at : at + width]
            high, low = split(record)
            both = jnp.concatenate([high.astype(F32), low.astype(F32)], axis=0)
            masked = jnp.concatenate([both * match[d : d + 1] for d in range(8)], axis=0)
            packed[step] = packed[step] + dot_lanes(masked.astype(BF16), spots)
    for step in range(STEPS):
        lanes = slice(step * CAPACITY, (step + 1) * CAPACITY)
        for d in range(8):
            at = d * 2 * FIELDS
            record = packed[step][at : at + FIELDS] + packed[step][at + FIELDS : at + 2 * FIELDS]
            code = CODES[d]
            if code // 3 == 1:
                row = code % 3 // 2 * FIELDS
                beside[row : row + FIELDS, lanes] = record
            else:
                row = (code % 3) * FIELDS
                (west if code // 3 == 0 else east)[row : row + FIELDS, lanes] = record
    address(east, west, inner, outer)


def extend_lon(ext, p, own, from_west, from_east, rows, cells_lat):
    lanes = slice(Y0, Y0 + cells_lat)
    ext[p, X0 : X0 + rows, lanes] = own
    at = 3 * FIELDS + LOW * p
    ext[p, X0 - LOW : X0, lanes] = from_west[at : at + LOW, :]
    at = 3 * FIELDS + HIGH * p
    ext[p, X0 + rows : X0 + rows + HIGH, lanes] = from_east[at : at + HIGH, :]


def merge_kernel(init, depth, mixing, beside, inner, outer, ext, south, north):
    from_west, from_east = pick(inner, outer)
    rows, cells_lat = depth.shape
    ext[...] = jnp.zeros_like(ext)
    for p in range(PLANES):
        if p < 2 * DEPTH:
            own = init[p // DEPTH, p % DEPTH]
        else:
            own = depth[...].astype(F32) if p == 2 * DEPTH else mixing[...]
        extend_lon(ext, p, own, from_west, from_east, rows, cells_lat)
    tall = ext.shape[1]
    lane = iota((tall, 128), 1)
    first = jnp.zeros((tall, 128), F32)
    last = jnp.zeros((tall, 128), F32)
    for p in range(PLANES):
        head = jnp.where(lane < HIGH, ext[p, :, Y0 : Y0 + 128], 0.0)
        tail = jnp.where(lane >= 128 - LOW, ext[p, :, Y0 + cells_lat - 128 : Y0 + cells_lat], 0.0)
        first = first + roll(head, HIGH * p, 1)
        last = last + roll(tail, -LOW * p, 1)
    for out, kept, row, strip in ((south, 0, 0, first), (north, 1, 2, last)):
        out[0:FIELDS, :] = beside[kept * FIELDS : (kept + 1) * FIELDS, :]
        out[FIELDS : 2 * FIELDS, :] = from_west[row * FIELDS : (row + 1) * FIELDS, :]
        out[2 * FIELDS : 3 * FIELDS, :] = from_east[row * FIELDS : (row + 1) * FIELDS, :]
        out[3 * FIELDS :, 0:128] = strip[: tall // 2]
        out[3 * FIELDS :, 128:] = strip[tall // 2 :]


def lap(v):
    return roll(v, 1, 0) + roll(v, -1, 0) + roll(v, 1, 1) + roll(v, -1, 1) - 4.0 * v


def vz(column, k, levels):
    above = column[max(k - 1, 0)]
    below = min(k + 1, levels - 1)
    total = above - 2.0 * column[k] if k < len(column) else above
    return total + column[below] if below < len(column) else total


def tendency(v, k, mixing, rotation, levels):
    out = []
    for c in range(2):
        value = v[c][k] + mixing(v[c][k]) + VISCOUS * vz(v[c], k, levels) - FRICTION * v[c][k]
        turned = rotation * v[1 - c][k]
        out.append(value + turned if c == 0 else value - turned)
    return out


def main_kernel(
    levels, refine, lat_count, forcing, fields, precision, inner, outer, from_south, from_north,
    padded, partial, share, to_inner, to_outer, ext, spot, to_west, to_east,
):
    from_west, from_east = pick(inner, outer)
    rows, cells_lat = partial.shape[1] - 16, partial.shape[2] - 256
    tall, wide = ext.shape[1:]
    lat_index = lax.axis_index("lat")
    grid_lat = cells_lat * lat_count
    lane = iota((tall, 128), 1)
    half = tall // 2
    below = jnp.concatenate([from_south[3 * FIELDS :, 0:128], from_south[3 * FIELDS :, 128:]], axis=0)
    above = jnp.concatenate([from_north[3 * FIELDS :, 0:128], from_north[3 * FIELDS :, 128:]], axis=0)
    full = []
    for p in range(PLANES):
        left = jnp.where(lane >= 128 - LOW, roll(below, LOW * p, 1), 0.0)
        right = jnp.where(lane < HIGH, roll(above, -HIGH * p, 1), 0.0)
        full.append(jnp.concatenate([left, padded[p, :, Y0 : Y0 + cells_lat], right], axis=1))
    mixing = full[2 * DEPTH + 1]
    wet = [(full[2 * DEPTH] > float(k)).astype(F32) for k in range(DEPTH)]
    row_ids = iota((1, wide), 1) - Y0 + lat_index * cells_lat
    rotation = ROTATION * jnp.sin((row_ids.astype(F32) + 0.5) * (math.pi / grid_lat) - 0.5 * math.pi)
    state = [[wet[k] * full[c * DEPTH + k] for k in range(DEPTH)] for c in range(2)]
    surfaces = []
    for step in range(STEPS):
        ahead = [[], []]
        for k in range(DEPTH - 1 - step):
            moved = tendency(state, k, lambda v: mixing * lap(v), rotation, levels)
            for c in range(2):
                value = moved[c] + forcing[2 * step + c] if k == 0 else moved[c]
                ahead[c].append(wet[k] * value)
        state = ahead
        surfaces.append([state[0][0], state[1][0]])
    strip, tiles = rows + 8, rows + 16
    chunk = 512
    lat_of = iota((cells_lat, chunk), 0).astype(F32).astype(BF16)
    lon_of = iota((strip, chunk), 0).astype(F32)
    lon_tile = iota((tiles, chunk), 0).astype(F32).astype(BF16)
    one, nought = jnp.ones((), BF16), jnp.zeros((), BF16)
    sources = []
    for step in range(STEPS):
        views = []
        for c in range(2):
            surface = surfaces[step][c][X0 : X0 + strip]
            views += [surface[:, Y0 : Y0 + cells_lat], roll(surface, -1, 1)[:, Y0 : Y0 + cells_lat]]
        views = jnp.concatenate(split(jnp.concatenate(views, axis=0)), axis=0)

        def spread(record, total):
            cell = record[7:8].astype(jnp.int32)
            lon = lax.shift_right_logical(cell, cells_lat.bit_length() - 1).astype(F32)
            lat = (cell & (cells_lat - 1)).astype(F32).astype(BF16)
            hot = jnp.where(lat_of == lat, one, nought)
            found = dot(views, hot)
            found = found[: 4 * strip] + found[4 * strip :]
            here, there = lon_of == lon, lon_of == lon + 1.0
            near = jnp.where(here, record[0:1], jnp.where(there, record[1:2], 0.0))
            far = jnp.where(here, record[2:3], jnp.where(there, record[3:4], 0.0))
            lon = lon.astype(BF16)
            here, there = lon_tile == lon, lon_tile == lon + one
            terms = [[], []]
            for c in range(2):
                at = 2 * c * strip
                seen = near * found[at : at + strip] + far * found[at + strip : at + 2 * strip]
                miss = jnp.sum(seen, axis=0, keepdims=True) - record[4 + c : 5 + c]
                parts = split(record[0:4] * (record[6:7] * miss))
                for part, term in zip(parts, terms):
                    for d in (0, 2):
                        term.append(jnp.where(here, part[d : d + 1], jnp.where(there, part[d + 1 : d + 2], nought)))
            return total + dot_lanes(jnp.concatenate(terms[0] + terms[1], axis=0), hot)

        total = jnp.zeros((8 * tiles, cells_lat), F32)
        for at in range(0, fields.shape[1], chunk):
            total = spread(fields[step * FIELDS : (step + 1) * FIELDS, at : at + chunk], total)
        lanes = slice(step * CAPACITY, (step + 1) * CAPACITY)
        came = [from_west[FIELDS : 2 * FIELDS, lanes], from_east[FIELDS : 2 * FIELDS, lanes]]
        came += [message[i * FIELDS : (i + 1) * FIELDS, lanes] for message in (from_south, from_north) for i in range(3)]
        for at in range(0, 8, chunk // CAPACITY):
            total = spread(jnp.concatenate(came[at : at + chunk // CAPACITY], axis=1), total)
        sources.append([])
        total = total[: 4 * tiles] + total[4 * tiles :]
        for c in range(2):
            at = 2 * c * tiles
            spot[...] = jnp.zeros_like(spot)
            spot[0, X0 : X0 + strip, Y0 : Y0 + cells_lat] = total[at : at + strip]
            spot[1, X0 : X0 + strip, Y0 : Y0 + cells_lat] = total[at + tiles : at + tiles + strip]
            sources[step].append(spot[0] + roll(spot[1], 1, 1))
    adjoint = None
    nudges = [None] * STEPS
    for step in reversed(range(STEPS)):
        if adjoint is None:
            adjoint = [[sources[step][c]] for c in range(2)]
        else:
            adjoint = [[adjoint[c][0] + sources[step][c]] + adjoint[c][1:] for c in range(2)]
        nudged = [[wet[k] * adjoint[c][k] for k in range(len(adjoint[c]))] for c in range(2)]
        nudges[step] = [nudged[0][0], nudged[1][0]]
        reach = len(nudged[0])
        adjoint = [[], []]
        for k in range(reach):
            moved = tendency(nudged, k, lambda v: lap(mixing * v), -rotation, levels)
            for c in range(2):
                adjoint[c].append(moved[c])
        for c in range(2):
            adjoint[c].append(VISCOUS * vz(nudged[c], reach, levels))
    for c in range(2):
        for k in range(DEPTH):
            p = c * DEPTH + k
            ext[p] = adjoint[c][k]
            partial[p] = adjoint[c][k]
            to_west[LOW * p : LOW * (p + 1), :] = ext[p, X0 - LOW : X0, :]
            to_east[HIGH * p : HIGH * (p + 1), :] = ext[p, X0 + rows : X0 + rows + HIGH, :]
    address(to_east, to_west, to_inner, to_outer)
    low, part = interpolation(iota((wide, 4 * GROUP), 0) - Y0 - refine // 2, refine)
    column = iota((wide, 4 * GROUP), 1) % GROUP - 1
    onto_lat = jnp.where(column == low, 1.0 - part, 0.0) + jnp.where(column == low + 1, part, 0.0)
    onto_lat = onto_lat.astype(BF16)
    low, part = interpolation(iota((tall, 4 * GROUP), 0) - X0 - refine // 2, refine)
    column = iota((tall, 4 * GROUP), 1) // GROUP - 1
    onto_lon = jnp.where(column == low, 1.0 - part, 0.0) + jnp.where(column == low + 1, part, 0.0)
    weight = jnp.sum(jnp.sum(precision[...], axis=0, keepdims=True), axis=1, keepdims=True)
    parts = []
    for step in range(STEPS):
        for c in range(2):
            high, rest = split(nudges[step][c])
            across = dot(high, onto_lat) + dot(rest, onto_lat)
            parts.append(jnp.sum(onto_lon * across, axis=0, keepdims=True))
    parts[0] = jnp.where(iota((1, 4 * GROUP), 1) == 4 * GROUP - 1, weight, parts[0])
    share[...] = jnp.broadcast_to(jnp.concatenate(parts, axis=0)[None], share.shape)


def plane_kernel(lat_count, per, shares, partial, inner, outer, out, own, south, north, rows, total):
    join(partial, inner, outer, own, south, north)
    members = shares.shape[0]
    ring = members // (CORES * lat_count)
    ctrl_lat = per * lat_count
    for m in range(members):
        rows[4 * m : 4 * m + 4, :] = shares[m]
    total[...] = jnp.zeros_like(total)
    lane = iota((ring, 4 * GROUP), 1)
    height = total.shape[0] // STEPS
    weight = jnp.zeros((ring, 4 * GROUP), F32)
    for core in range(CORES):
        for step in range(STEPS):
            sums = [jnp.zeros((ring, 4 * GROUP), F32) for _ in range(4)]
            for band in range(lat_count):
                for c in range(2):
                    at = 4 * (core * lat_count + band) + 2 * step + c
                    held = rows[pl.ds(at, ring, stride=4 * CORES * lat_count), :]
                    if step == 0 and c == 0:
                        weight = weight + held
                    start = c * ctrl_lat + per * band - 1
                    first, last = max(start, c * ctrl_lat), min(start + per + 1, (c + 1) * ctrl_lat - 1)
                    mine = (lane >= first) & (lane <= last)
                    for a in range(4):
                        sums[a] = sums[a] + jnp.where(mine, roll(held, start - GROUP * a, 1), 0.0)
            for a in range(4):
                at = step * height + 2 * core + a
                total[pl.ds(at, ring, stride=4), :] = total[pl.ds(at, ring, stride=4), :] + sums[a]
    weight = jnp.sum(jnp.where(lane == 4 * GROUP - 1, weight, 0.0), axis=0, keepdims=True)
    weight = jnp.sum(weight, axis=1, keepdims=True)
    total[4 * ring + 2 : 4 * ring + 3, :] = jnp.broadcast_to(weight, (1, 4 * GROUP))
    out[...] = jnp.broadcast_to(total[...][None], out.shape)


def join(partial, inner, outer, own, south, north):
    from_west, from_east = pick(inner, outer)
    rows, cells_lat = own.shape[1:]
    lane = iota((rows, 128), 1)
    first = jnp.zeros((rows, 128), F32)
    last = jnp.zeros((rows, 128), F32)
    for p in range(2 * DEPTH):
        partial[p, X0 : X0 + HIGH, :] += from_west[HIGH * p : HIGH * (p + 1), :]
        partial[p, X0 + rows - LOW : X0 + rows, :] += from_east[LOW * p : LOW * (p + 1), :]
        block = partial[p, X0 : X0 + rows, :]
        own[p] = block[:, Y0 : Y0 + cells_lat]
        tail = jnp.where(lane >= 128 - LOW, block[:, Y0 - 128 : Y0], 0.0)
        head = jnp.where(lane < HIGH, block[:, Y0 + cells_lat : Y0 + cells_lat + 128], 0.0)
        first = first + roll(tail, -LOW * p, 1)
        last = last + roll(head, HIGH * p, 1)
    south[...] = first
    north[...] = last


def finish_kernel(normalizer, own, depth, from_south, from_north, shares, grad, out, full):
    levels, rows, cells_lat = grad.shape[1:]
    periods, _, ctrl_lat, ctrl_lon = out.shape
    table = period_weights(STEPS, periods)
    members, size = shares.shape[:2]
    span = ctrl_lon // members
    total = shares[0, span + 2 : span + 3, :]
    for m in range(1, members):
        total = total + shares[m, span + 2 : span + 3, :]
    scale = normalizer / total[:, 0:1]
    side = iota((rows, 128), 1)
    wet_levels = depth[...]
    for c in range(2):
        for k in range(levels):
            if k >= DEPTH:
                grad[c, k] = jnp.zeros((rows, cells_lat), F32)
                continue
            p = c * DEPTH + k
            low = jnp.where(side < HIGH, roll(from_south[...], -HIGH * p, 1), 0.0)
            high = jnp.where(side >= 128 - LOW, roll(from_north[...], LOW * p, 1), 0.0)
            value = own[p] + jnp.concatenate([low, high], axis=1)
            grad[c, k] = jnp.where(wet_levels > k, value * scale, 0.0)
    for step in range(STEPS):
        at = step * size // STEPS
        for m in range(members):
            full[step, m * span : (m + 1) * span, :] = shares[m, at + 1 : at + 1 + span, :]
        for m in range(members):
            before, after = (m * span + ctrl_lon - 1) % ctrl_lon, (m + 1) * span % ctrl_lon
            full[step, before : before + 1, :] += shares[m, at : at + 1, :]
            full[step, after : after + 1, :] += shares[m, at + span + 1 : at + span + 2, :]
    scaled = [scale * full[step] for step in range(STEPS)]
    for period in range(periods):
        value = table[0][period] * scaled[0]
        for step in range(1, STEPS):
            value = value + table[step][period] * scaled[step]
        value = value.T
        for c in range(2):
            out[period, c] = value[c * ctrl_lat : (c + 1) * ctrl_lat]


def swap(inner, outer):
    count = lax.axis_size("lon")
    inner = lax.ppermute(inner, "lon", [(i, i ^ 1) for i in range(count)])
    outer = lax.ppermute(outer, "lon", [((i + 1) % count, ((i ^ 1) + 1) % count) for i in range(count)])
    return inner, outer


def gather(copies, chips, stride, whole_chips):
    if copies.shape[0] == 1:
        return copies
    count = lax.axis_size("lat")
    per_chip = CORES * count
    inside = [range(per_chip)] if whole_chips else [(i,) for i in range(per_chip)]
    groups = []
    for base in range(lax.axis_size("lon") // CORES):
        if base // stride % chips == 0:
            for few in inside:
                groups.append([(base + chip * stride) * per_chip + i for chip in range(chips) for i in few])
    return lax.all_to_all(copies, ("lon", "lat"), 0, 0, axis_index_groups=groups, tiled=True)


def along(value, distance):
    count = lax.axis_size("lat")
    return lax.ppermute(value, "lat", [(i, i + distance) for i in range(max(0, -distance), min(count, count - distance))])


def whole(shape):
    return pl.BlockSpec(shape, lambda i: (0,) * len(shape))


def call(kernel, ins, outs, blocks=None, scratch=(), vmem=16):
    blocks = blocks or {}
    return pl.pallas_call(
        kernel,
        grid=(1,),
        out_shape=[jax.ShapeDtypeStruct(shape, F32) for shape in outs],
        in_specs=[whole(blocks.get(i, value.shape)) for i, value in enumerate(ins)],
        out_specs=[whole(shape) for shape in outs],
        scratch_shapes=[pltpu.VMEM(shape, F32) for shape in scratch],
        compiler_params=pltpu.CompilerParams(vmem_limit_bytes=vmem * MIB),
    )(*ins)


def shards(
    initial, depth_levels, mixing, controls, drift_move, drift_cell, drift_weight, drift_obs, drift_precision
):
    _, levels, rows, cells_lat = initial.shape
    periods, _, ctrl_lon, ctrl_lat = controls.shape
    count = drift_move.shape[1]
    lon_count, lat_count = lax.axis_size("lon"), lax.axis_size("lat")
    refine = rows * lon_count // ctrl_lon
    tall, wide = rows + 16, cells_lat + 256
    surface = (2, DEPTH, rows, cells_lat)
    lon_message = (3 * FIELDS + HIGH * PLANES, 256)
    inner, outer, beside = call(
        pack_kernel,
        (drift_move, drift_cell, drift_weight, drift_obs, drift_precision, initial, depth_levels, mixing),
        (lon_message, lon_message, (2 * FIELDS, 256)),
        {5: surface},
        scratch=((STEPS * FIELDS, count), lon_message, lon_message),
        vmem=60,
    )
    inner, outer = swap(inner, outer)
    fields, forcing = call(
        functools.partial(own_kernel, refine, lat_count),
        (jnp.swapaxes(controls, 2, 3), drift_move, drift_cell, drift_weight, drift_obs, drift_precision),
        ((STEPS * FIELDS, count), (2 * STEPS, tall, wide)),
    )
    message = (3 * FIELDS + tall // 2, 256)
    padded, south, north = call(
        merge_kernel,
        (initial, depth_levels, mixing, beside, inner, outer),
        ((PLANES, tall, wide), message, message),
        {0: surface},
    )
    from_south, from_north = along(north, 1), along(south, -1)
    edge = (2 * DEPTH * HIGH, wide)
    ring = min(RING, lon_count // CORES)
    members = lon_count // (CORES * ring)
    partial, share, inner, outer = call(
        functools.partial(main_kernel, levels, refine, lat_count),
        (forcing, fields, drift_precision, inner, outer, from_south, from_north, padded),
        ((2 * DEPTH, tall, wide), (ring * CORES * lat_count, 2 * STEPS, 4 * GROUP), edge, edge),
        scratch=((2 * DEPTH, tall, wide), (2, tall, wide), edge, edge),
    )
    shares = gather(share, ring, 1, True)
    inner, outer = swap(inner, outer)
    height = -(-(4 * ring + 3) // 8) * 8
    share, own, to_south, to_north = call(
        functools.partial(plane_kernel, lat_count, ctrl_lat // lat_count),
        (shares, partial, inner, outer),
        ((members, STEPS * height, 2 * ctrl_lat), (2 * DEPTH, rows, cells_lat), (rows, 128), (rows, 128)),
        scratch=((4 * ring * CORES * lat_count, 4 * GROUP), (STEPS * height, 2 * ctrl_lat)),
    )
    from_south, from_north = along(to_north, 1), along(to_south, -1)
    shares = gather(share, members, ring, False)
    grad_initial, grad_controls = call(
        functools.partial(finish_kernel, float(STEPS * count * lon_count * lat_count)),
        (own, depth_levels, from_south, from_north, shares),
        (initial.shape, (periods, 2, ctrl_lat, ctrl_lon)),
        scratch=((STEPS, ctrl_lon, 2 * ctrl_lat),),
    )
    return grad_initial, jnp.swapaxes(grad_controls, 2, 3)


def solution(mesh):
    return jax.shard_map(
        shards,
        mesh=mesh,
        in_specs=(
            P(None, None, "lon", "lat"),
            P("lon", "lat"),
            P("lon", "lat"),
            P(),
            P(None, ("lon", "lat")),
            P(None, ("lon", "lat")),
            P(None, None, ("lon", "lat")),
            P(None, None, ("lon", "lat")),
            P(None, ("lon", "lat")),
        ),
        out_specs=(P(None, None, "lon", "lat"), P()),
        check_vma=False,
    )
```

```python
import functools
import math

import jax
import jax.numpy as jnp
from jax import lax
from jax.experimental import pallas as pl
from jax.experimental.pallas import tpu as pltpu
from jax.sharding import PartitionSpec as P

CAPACITY = 128
VISCOUS = 0.1
FRICTION = 0.02
ROTATION = 0.3
STEPS = 2
DEPTH = STEPS + 1
CODES = (0, 1, 2, 3, 5, 6, 7, 8)
FIELDS = 8
PLANES = 2 * DEPTH + 2
LOW, HIGH = 2, 3
X0, Y0 = 8, 128
CORES = 2
RING = 8
GROUP = 32
F32, BF16 = jnp.float32, jnp.bfloat16


def iota(shape, dim):
    return lax.broadcasted_iota(jnp.int32, shape, dim)


def split(value):
    high = value.astype(BF16)
    return high, (value - high.astype(F32)).astype(BF16)


def dot(a, b):
    return lax.dot_general(a, b, (((1,), (0,)), ((), ())), preferred_element_type=F32)


def dot_lanes(a, b):
    return lax.dot_general(a, b, (((1,), (1,)), ((), ())), preferred_element_type=F32)


def roll(value, shift, axis):
    return pltpu.roll(value, shift % value.shape[axis], axis)


def parity():
    return lax.axis_index("lon") % CORES


def pick(first, second):
    even = parity() == 0
    inner, outer = first[...], second[...]
    return jnp.where(even, outer, inner), jnp.where(even, inner, outer)


def address(east, west, first, second):
    even = parity() == 0
    first[...] = jnp.where(even, east[...], west[...])
    second[...] = jnp.where(even, west[...], east[...])


def interpolation(offset, refine):
    low = lax.shift_right_arithmetic(offset, refine.bit_length() - 1)
    return low, ((offset - low * refine).astype(F32) + 0.5) / refine


def period_weights(steps_total, periods):
    table = []
    for step in range(steps_total):
        position = (step + 0.5) * (periods - 1) / steps_total
        table.append([max(0.0, 1.0 - abs(position - period)) for period in range(periods)])
    return table


def stage(fields, cell, weight, obs):
    for step in range(STEPS):
        base = step * FIELDS
        for i in range(4):
            fields[base + i : base + i + 1, :] = weight[i, step : step + 1, :]
        for i in range(2):
            fields[base + 4 + i : base + 5 + i, :] = obs[i, step : step + 1, :]
        fields[base + 7 : base + 8, :] = cell[step : step + 1, :].astype(F32)


def own_kernel(refine, lat_count, controls, move, cell, weight, obs, prec, beside, fields, forcing, near):
    near[...] = beside[...]
    stage(fields, cell, weight, obs)
    for step in range(STEPS):
        row = step * FIELDS + 6
        fields[row : row + 1, :] = jnp.where(move[step : step + 1, :] == 4, prec[step : step + 1, :], 0.0)
    tall, wide = forcing.shape[1:]
    rows, cells_lat = tall - 16, wide - 256
    periods, _, ctrl_lat, ctrl_lon = controls.shape
    table = period_weights(STEPS, periods)
    low, part = interpolation(iota((tall, ctrl_lon), 0) - X0 + lax.axis_index("lon") * rows - refine // 2, refine)
    column = iota((tall, ctrl_lon), 1)
    wrapped, after = (low + ctrl_lon) % ctrl_lon, (low + 1 + ctrl_lon) % ctrl_lon
    lon_interp = jnp.where(column == wrapped, 1.0 - part, 0.0) + jnp.where(column == after, part, 0.0)
    low, part = interpolation(iota((ctrl_lat, wide), 1) - Y0 + lax.axis_index("lat") * cells_lat - refine // 2, refine)
    column = iota((ctrl_lat, wide), 0)
    lat_interp = jnp.where(column == low, 1.0 - part, 0.0) + jnp.where(column == low + 1, part, 0.0)
    lon_interp, lat_interp = lon_interp.astype(BF16), lat_interp.astype(BF16)
    for step in range(STEPS):
        for c in range(2):
            blended = table[step][0] * controls[0, c]
            for period in range(1, periods):
                blended = blended + table[step][period] * controls[period, c]
            high, low = split(blended)
            high, low = split(dot_lanes(lon_interp, high) + dot_lanes(lon_interp, low))
            forcing[2 * step + c] = dot(high, lat_interp) + dot(low, lat_interp)


def pack_kernel(
    move_far, cell_far, weight_far, obs_far, prec_far, init_far, depth_far, mixing_far, inner, outer, beside,
    move, cell, weight, obs, prec, init, depth, mixing, fields, east, west, arrived,
):
    count = move.shape[1]
    rows = depth_far.shape[0]
    whole_arrays = [(move_far, move), (cell_far, cell), (weight_far, weight), (obs_far, obs), (prec_far, prec)]
    edges = []
    for end, first in enumerate((0, rows - 8)):
        edges.append((init_far.at[:, :DEPTH, pl.ds(first, 8), :], init.at[end]))
        edges.append((depth_far.at[pl.ds(first, 8), :], depth.at[end]))
        edges.append((mixing_far.at[pl.ds(first, 8), :], mixing.at[end]))
    copies = [pltpu.make_async_copy(far, near, arrived.at[i]) for i, (far, near) in enumerate(whole_arrays + edges)]
    for copy in copies:
        copy.start()
    copies[0].wait()
    width = 256
    blocks = count // width
    triangle = (iota((width, width), 0) <= iota((width, width), 1)).astype(F32).astype(BF16)
    code = iota((8, 1), 0)
    code = code + (code >= 4).astype(jnp.int32)
    matches = []
    for step in range(STEPS):
        for block in range(blocks):
            matches.append((move[step : step + 1, block * width : (block + 1) * width] == code).astype(F32))
    ranks = dot(jnp.concatenate(matches, axis=0).astype(BF16), triangle)
    places = []
    for step in range(STEPS):
        carry = jnp.full((8, 1), -1.0, F32)
        for block in range(blocks):
            at = step * blocks + block
            rank = ranks[8 * at : 8 * at + 8]
            places.append(jnp.sum(matches[at] * (rank + carry), axis=0, keepdims=True))
            carry = carry + rank[:, width - 1 :]
    for copy in copies[1:]:
        copy.wait()
    stage(fields, cell, weight, obs)
    for step in range(STEPS):
        fields[step * FIELDS + 6 : step * FIELDS + 7, :] = prec[step : step + 1, :]
    for p in range(PLANES):
        for end, strip, first, size in ((0, west, 0, HIGH), (1, east, 8 - LOW, LOW)):
            if p < 2 * DEPTH:
                line = init[end, p // DEPTH, p % DEPTH, first : first + size, :]
            elif p == 2 * DEPTH:
                line = depth[end, first : first + size, :].astype(F32)
            else:
                line = mixing[end, first : first + size, :]
            strip[3 * FIELDS + size * p : 3 * FIELDS + size * (p + 1), :] = line
    joined = 2
    slot = iota((CAPACITY, joined * width), 0).astype(F32).astype(BF16)
    one, nought = jnp.ones((), BF16), jnp.zeros((), BF16)
    for step in range(STEPS):
        packed = jnp.zeros((8 * 2 * FIELDS, CAPACITY), F32)
        for block in range(0, blocks, joined):
            at = step * blocks + block
            place = jnp.concatenate(places[at : at + joined], axis=1).astype(BF16)
            spots = jnp.where(slot == place, one, nought)
            lanes = slice(block * width, (block + joined) * width)
            both = jnp.concatenate(split(fields[step * FIELDS : (step + 1) * FIELDS, lanes]), axis=0)
            kind = jnp.broadcast_to(move[step : step + 1, lanes].astype(F32), both.shape).astype(BF16)
            masked = jnp.concatenate([jnp.where(kind == jnp.full((), c, BF16), both, nought) for c in CODES], axis=0)
            packed = packed + dot_lanes(masked, spots)
        lanes = slice(step * CAPACITY, (step + 1) * CAPACITY)
        for d in range(8):
            at = d * 2 * FIELDS
            record = packed[at : at + FIELDS] + packed[at + FIELDS : at + 2 * FIELDS]
            if CODES[d] // 3 == 1:
                row = CODES[d] % 3 // 2 * FIELDS
                beside[row : row + FIELDS, lanes] = record
            else:
                row = (CODES[d] % 3) * FIELDS
                (west if CODES[d] // 3 == 0 else east)[row : row + FIELDS, lanes] = record
    address(east, west, inner, outer)


def extend_lon(ext, p, own, from_west, from_east, rows, cells_lat):
    lanes = slice(Y0, Y0 + cells_lat)
    ext[p, X0 : X0 + rows, lanes] = own
    at = 3 * FIELDS + LOW * p
    ext[p, X0 - LOW : X0, lanes] = from_west[at : at + LOW, :]
    at = 3 * FIELDS + HIGH * p
    ext[p, X0 + rows : X0 + rows + HIGH, lanes] = from_east[at : at + HIGH, :]


def merge_kernel(init, depth, mixing, beside, inner, outer, ext, south, north):
    from_west, from_east = pick(inner, outer)
    rows, cells_lat = depth.shape
    ext[...] = jnp.zeros_like(ext)
    for p in range(PLANES):
        if p < 2 * DEPTH:
            own = init[p // DEPTH, p % DEPTH]
        else:
            own = depth[...].astype(F32) if p == 2 * DEPTH else mixing[...]
        extend_lon(ext, p, own, from_west, from_east, rows, cells_lat)
    tall = ext.shape[1]
    lane = iota((tall, 128), 1)
    first = jnp.zeros((tall, 128), F32)
    last = jnp.zeros((tall, 128), F32)
    for p in range(PLANES):
        head = jnp.where(lane < HIGH, ext[p, :, Y0 : Y0 + 128], 0.0)
        tail = jnp.where(lane >= 128 - LOW, ext[p, :, Y0 + cells_lat - 128 : Y0 + cells_lat], 0.0)
        first = first + roll(head, HIGH * p, 1)
        last = last + roll(tail, -LOW * p, 1)
    for out, kept, row, strip in ((south, 0, 0, first), (north, 1, 2, last)):
        out[0:FIELDS, :] = beside[kept * FIELDS : (kept + 1) * FIELDS, :]
        out[FIELDS : 2 * FIELDS, :] = from_west[row * FIELDS : (row + 1) * FIELDS, :]
        out[2 * FIELDS : 3 * FIELDS, :] = from_east[row * FIELDS : (row + 1) * FIELDS, :]
        out[3 * FIELDS :, 0:128] = strip[: tall // 2]
        out[3 * FIELDS :, 128:] = strip[tall // 2 :]


def lap(v):
    return roll(v, 1, 0) + roll(v, -1, 0) + roll(v, 1, 1) + roll(v, -1, 1) - 4.0 * v


def vz(column, k, levels):
    above = column[max(k - 1, 0)]
    below = min(k + 1, levels - 1)
    total = above - 2.0 * column[k] if k < len(column) else above
    return total + column[below] if below < len(column) else total


def tendency(v, k, mixing, rotation, levels):
    out = []
    for c in range(2):
        value = v[c][k] + mixing(v[c][k]) + VISCOUS * vz(v[c], k, levels) - FRICTION * v[c][k]
        turned = rotation * v[1 - c][k]
        out.append(value + turned if c == 0 else value - turned)
    return out


def main_kernel(
    levels, refine, lat_count, forcing, fields, precision, inner, outer, from_south, from_north,
    padded, partial, share, to_inner, to_outer, ext, spot, to_west, to_east,
):
    from_west, from_east = pick(inner, outer)
    rows, cells_lat = partial.shape[1] - 16, partial.shape[2] - 256
    tall, wide = ext.shape[1:]
    lat_index = lax.axis_index("lat")
    grid_lat = cells_lat * lat_count
    lane = iota((tall, 128), 1)
    half = tall // 2
    below = jnp.concatenate([from_south[3 * FIELDS :, 0:128], from_south[3 * FIELDS :, 128:]], axis=0)
    above = jnp.concatenate([from_north[3 * FIELDS :, 0:128], from_north[3 * FIELDS :, 128:]], axis=0)
    full = []
    for p in range(PLANES):
        left = jnp.where(lane >= 128 - LOW, roll(below, LOW * p, 1), 0.0)
        right = jnp.where(lane < HIGH, roll(above, -HIGH * p, 1), 0.0)
        full.append(jnp.concatenate([left, padded[p, :, Y0 : Y0 + cells_lat], right], axis=1))
    mixing = full[2 * DEPTH + 1]
    wet = [(full[2 * DEPTH] > float(k)).astype(F32) for k in range(DEPTH)]
    row_ids = iota((1, wide), 1) - Y0 + lat_index * cells_lat
    rotation = ROTATION * jnp.sin((row_ids.astype(F32) + 0.5) * (math.pi / grid_lat) - 0.5 * math.pi)
    state = [[wet[k] * full[c * DEPTH + k] for k in range(DEPTH)] for c in range(2)]
    surfaces = []
    for step in range(STEPS):
        ahead = [[], []]
        for k in range(DEPTH - 1 - step):
            moved = tendency(state, k, lambda v: mixing * lap(v), rotation, levels)
            for c in range(2):
                value = moved[c] + forcing[2 * step + c] if k == 0 else moved[c]
                ahead[c].append(wet[k] * value)
        state = ahead
        surfaces.append([state[0][0], state[1][0]])
    chunk = 512
    lat_of = iota((cells_lat, chunk), 0).astype(F32).astype(BF16)
    lon_of = iota((rows, chunk), 0).astype(F32)
    lon_tile = lon_of.astype(BF16)
    one, nought = jnp.ones((), BF16), jnp.zeros((), BF16)
    sources = []
    for step in range(STEPS):
        views, edges = [], []
        for c in range(2):
            surface = surfaces[step][c][X0 : X0 + rows + 8]
            for view in (surface, roll(surface, -1, 1)):
                views.append(view[:rows, Y0 : Y0 + cells_lat])
                edges.append(view[rows : rows + 1, Y0 : Y0 + cells_lat])
        views = jnp.concatenate(views + edges + [jnp.zeros((4, cells_lat), F32)], axis=0)
        high, low = split(views)
        views = jnp.concatenate([high.astype(F32), low.astype(F32)], axis=0).astype(BF16)
        seen_rows = 4 * rows + 8

        def spread(record, total):
            cell = record[7:8].astype(jnp.int32)
            lon = lax.shift_right_logical(cell, cells_lat.bit_length() - 1).astype(F32)
            lat = (cell & (cells_lat - 1)).astype(F32).astype(BF16)
            hot = jnp.where(lat_of == lat, one, nought)
            found = dot(views, hot)
            found = found[:seen_rows] + found[seen_rows:]
            here, there, edge = lon_of == lon, lon_of == lon + 1.0, lon == rows - 1.0
            near = jnp.where(here, record[0:1], jnp.where(there, record[1:2], 0.0))
            far = jnp.where(here, record[2:3], jnp.where(there, record[3:4], 0.0))
            near_edge, far_edge = jnp.where(edge, record[1:2], 0.0), jnp.where(edge, record[3:4], 0.0)
            lon = lon.astype(BF16)
            here, there = lon_tile == lon, lon_tile == lon + one
            terms, outside = [[], []], []
            for c in range(2):
                at, last = 2 * c * rows, 4 * rows + 2 * c
                seen = near * found[at : at + rows] + far * found[at + rows : at + 2 * rows]
                miss = jnp.sum(seen, axis=0, keepdims=True) - record[4 + c : 5 + c]
                miss = miss + near_edge * found[last : last + 1] + far_edge * found[last + 1 : last + 2]
                parts = split(record[0:4] * (record[6:7] * miss))
                for part, term in zip(parts, terms):
                    outside.append(jnp.where(edge, part.astype(F32), 0.0))
                    for d in (0, 2):
                        term.append(jnp.where(here, part[d : d + 1], jnp.where(there, part[d + 1 : d + 2], nought)))
            outside = jnp.concatenate(outside, axis=0).astype(BF16)
            return total + dot_lanes(jnp.concatenate(terms[0] + terms[1] + [outside], axis=0), hot)

        total = jnp.zeros((8 * rows + 16, cells_lat), F32)
        for at in range(0, fields.shape[1], chunk):
            total = spread(fields[step * FIELDS : (step + 1) * FIELDS, at : at + chunk], total)
        lanes = slice(step * CAPACITY, (step + 1) * CAPACITY)
        came = [from_west[FIELDS : 2 * FIELDS, lanes], from_east[FIELDS : 2 * FIELDS, lanes]]
        came += [message[i * FIELDS : (i + 1) * FIELDS, lanes] for message in (from_south, from_north) for i in range(3)]
        for at in range(0, 8, chunk // CAPACITY):
            total = spread(jnp.concatenate(came[at : at + chunk // CAPACITY], axis=1), total)
        sources.append([])
        outside = total[8 * rows :]
        total = total[: 4 * rows] + total[4 * rows : 8 * rows]
        for c in range(2):
            spot[...] = jnp.zeros_like(spot)
            for d in range(2):
                at, last = (2 * c + d) * rows, 8 * c + 2 * d + 1
                spot[d, X0 : X0 + rows, Y0 : Y0 + cells_lat] = total[at : at + rows]
                edge = outside[last : last + 1] + outside[last + 4 : last + 5]
                spot[d, X0 + rows : X0 + rows + 1, Y0 : Y0 + cells_lat] = edge
            sources[step].append(spot[0] + roll(spot[1], 1, 1))
    adjoint = None
    nudges = [None] * STEPS
    for step in reversed(range(STEPS)):
        if adjoint is None:
            adjoint = [[sources[step][c]] for c in range(2)]
        else:
            adjoint = [[adjoint[c][0] + sources[step][c]] + adjoint[c][1:] for c in range(2)]
        nudged = [[wet[k] * adjoint[c][k] for k in range(len(adjoint[c]))] for c in range(2)]
        nudges[step] = [nudged[0][0], nudged[1][0]]
        reach = len(nudged[0])
        adjoint = [[], []]
        for k in range(reach):
            moved = tendency(nudged, k, lambda v: lap(mixing * v), -rotation, levels)
            for c in range(2):
                adjoint[c].append(moved[c])
        for c in range(2):
            adjoint[c].append(VISCOUS * vz(nudged[c], reach, levels))
    for c in range(2):
        for k in range(DEPTH):
            p = c * DEPTH + k
            ext[p] = adjoint[c][k]
            partial[p] = adjoint[c][k]
            to_west[LOW * p : LOW * (p + 1), :] = ext[p, X0 - LOW : X0, :]
            to_east[HIGH * p : HIGH * (p + 1), :] = ext[p, X0 + rows : X0 + rows + HIGH, :]
    address(to_east, to_west, to_inner, to_outer)
    low, part = interpolation(iota((wide, 4 * GROUP), 0) - Y0 - refine // 2, refine)
    column = iota((wide, 4 * GROUP), 1) % GROUP - 1
    onto_lat = jnp.where(column == low, 1.0 - part, 0.0) + jnp.where(column == low + 1, part, 0.0)
    onto_lat = onto_lat.astype(BF16)
    low, part = interpolation(iota((tall, 4 * GROUP), 0) - X0 - refine // 2, refine)
    column = iota((tall, 4 * GROUP), 1) // GROUP - 1
    onto_lon = jnp.where(column == low, 1.0 - part, 0.0) + jnp.where(column == low + 1, part, 0.0)
    weight = jnp.sum(jnp.sum(precision[...], axis=0, keepdims=True), axis=1, keepdims=True)
    parts = []
    for step in range(STEPS):
        for c in range(2):
            high, rest = split(nudges[step][c])
            across = dot(high, onto_lat) + dot(rest, onto_lat)
            parts.append(jnp.sum(onto_lon * across, axis=0, keepdims=True))
    parts[0] = jnp.where(iota((1, 4 * GROUP), 1) == 4 * GROUP - 1, weight, parts[0])
    share[...] = jnp.broadcast_to(jnp.concatenate(parts, axis=0)[None], share.shape)


def plane_kernel(lat_count, per, shares, partial, inner, outer, out, own, south, north, rows, total):
    join(partial, inner, outer, own, south, north)
    members = shares.shape[0]
    ring = members // (CORES * lat_count)
    ctrl_lat = per * lat_count
    for m in range(members):
        rows[4 * m : 4 * m + 4, :] = shares[m]
    total[...] = jnp.zeros_like(total)
    lane = iota((ring, 4 * GROUP), 1)
    height = total.shape[0] // STEPS
    weight = jnp.zeros((ring, 4 * GROUP), F32)
    for core in range(CORES):
        for step in range(STEPS):
            sums = [jnp.zeros((ring, 4 * GROUP), F32) for _ in range(4)]
            for band in range(lat_count):
                for c in range(2):
                    at = 4 * (core * lat_count + band) + 2 * step + c
                    held = rows[pl.ds(at, ring, stride=4 * CORES * lat_count), :]
                    if step == 0 and c == 0:
                        weight = weight + held
                    start = c * ctrl_lat + per * band - 1
                    first, last = max(start, c * ctrl_lat), min(start + per + 1, (c + 1) * ctrl_lat - 1)
                    mine = (lane >= first) & (lane <= last)
                    for a in range(4):
                        sums[a] = sums[a] + jnp.where(mine, roll(held, start - GROUP * a, 1), 0.0)
            for a in range(4):
                at = step * height + 2 * core + a
                total[pl.ds(at, ring, stride=4), :] = total[pl.ds(at, ring, stride=4), :] + sums[a]
    weight = jnp.sum(jnp.where(lane == 4 * GROUP - 1, weight, 0.0), axis=0, keepdims=True)
    weight = jnp.sum(weight, axis=1, keepdims=True)
    total[4 * ring + 2 : 4 * ring + 3, :] = jnp.broadcast_to(weight, (1, 4 * GROUP))
    out[...] = jnp.broadcast_to(total[...][None], out.shape)


def join(partial, inner, outer, own, south, north):
    from_west, from_east = pick(inner, outer)
    rows, cells_lat = own.shape[1:]
    lane = iota((rows, 128), 1)
    first = jnp.zeros((rows, 128), F32)
    last = jnp.zeros((rows, 128), F32)
    for p in range(2 * DEPTH):
        partial[p, X0 : X0 + HIGH, :] += from_west[HIGH * p : HIGH * (p + 1), :]
        partial[p, X0 + rows - LOW : X0 + rows, :] += from_east[LOW * p : LOW * (p + 1), :]
        block = partial[p, X0 : X0 + rows, :]
        own[p] = block[:, Y0 : Y0 + cells_lat]
        tail = jnp.where(lane >= 128 - LOW, block[:, Y0 - 128 : Y0], 0.0)
        head = jnp.where(lane < HIGH, block[:, Y0 + cells_lat : Y0 + cells_lat + 128], 0.0)
        first = first + roll(tail, -LOW * p, 1)
        last = last + roll(head, HIGH * p, 1)
    south[...] = first
    north[...] = last


def finish_kernel(normalizer, own, depth, from_south, from_north, shares, grad, out, full):
    levels, rows, cells_lat = grad.shape[1:]
    periods, _, ctrl_lat, ctrl_lon = out.shape
    table = period_weights(STEPS, periods)
    members, size = shares.shape[:2]
    span = ctrl_lon // members
    total = shares[0, span + 2 : span + 3, :]
    for m in range(1, members):
        total = total + shares[m, span + 2 : span + 3, :]
    scale = normalizer / total[:, 0:1]
    side = iota((rows, 128), 1)
    wet_levels = depth[...]
    for c in range(2):
        for k in range(levels):
            if k >= DEPTH:
                grad[c, k] = jnp.zeros((rows, cells_lat), F32)
                continue
            p = c * DEPTH + k
            low = jnp.where(side < HIGH, roll(from_south[...], -HIGH * p, 1), 0.0)
            high = jnp.where(side >= 128 - LOW, roll(from_north[...], LOW * p, 1), 0.0)
            value = own[p] + jnp.concatenate([low, high], axis=1)
            grad[c, k] = jnp.where(wet_levels > k, value * scale, 0.0)
    for step in range(STEPS):
        at = step * size // STEPS
        for m in range(members):
            full[step, m * span : (m + 1) * span, :] = shares[m, at + 1 : at + 1 + span, :]
        for m in range(members):
            before, after = (m * span + ctrl_lon - 1) % ctrl_lon, (m + 1) * span % ctrl_lon
            full[step, before : before + 1, :] += shares[m, at : at + 1, :]
            full[step, after : after + 1, :] += shares[m, at + span + 1 : at + span + 2, :]
    scaled = [scale * full[step] for step in range(STEPS)]
    for period in range(periods):
        value = table[0][period] * scaled[0]
        for step in range(1, STEPS):
            value = value + table[step][period] * scaled[step]
        value = value.T
        for c in range(2):
            out[period, c] = value[c * ctrl_lat : (c + 1) * ctrl_lat]


def swap(inner, outer):
    count = lax.axis_size("lon")
    inner = lax.ppermute(inner, "lon", [(i, i ^ 1) for i in range(count)])
    outer = lax.ppermute(outer, "lon", [((i + 1) % count, ((i ^ 1) + 1) % count) for i in range(count)])
    return inner, outer


def gather(copies, chips, stride, whole_chips):
    if copies.shape[0] == 1:
        return copies
    count = lax.axis_size("lat")
    per_chip = CORES * count
    inside = [range(per_chip)] if whole_chips else [(i,) for i in range(per_chip)]
    groups = []
    for base in range(lax.axis_size("lon") // CORES):
        if base // stride % chips == 0:
            for few in inside:
                groups.append([(base + chip * stride) * per_chip + i for chip in range(chips) for i in few])
    return lax.all_to_all(copies, ("lon", "lat"), 0, 0, axis_index_groups=groups, tiled=True)


def along(value, distance):
    count = lax.axis_size("lat")
    return lax.ppermute(value, "lat", [(i, i + distance) for i in range(max(0, -distance), min(count, count - distance))])


def whole(shape):
    return pl.BlockSpec(shape, lambda i: (0,) * len(shape))


def call(kernel, ins, outs, blocks=None, scratch=(), far=False, vmem=16):
    blocks = blocks or {}
    specs = [whole(blocks.get(i, value.shape)) for i, value in enumerate(ins)]
    if far:
        specs = [pl.BlockSpec(memory_space=pltpu.HBM) for _ in ins]
    return pl.pallas_call(
        kernel,
        grid=(1,),
        out_shape=[jax.ShapeDtypeStruct(shape, F32) for shape in outs],
        in_specs=specs,
        out_specs=[whole(shape) for shape in outs],
        scratch_shapes=[pltpu.VMEM(shape, F32) if isinstance(shape, tuple) else shape for shape in scratch],
        compiler_params=pltpu.CompilerParams(vmem_limit_bytes=vmem * 1024 * 1024),
    )(*ins)


def shards(
    initial, depth_levels, mixing, controls, drift_move, drift_cell, drift_weight, drift_obs, drift_precision
):
    _, levels, rows, cells_lat = initial.shape
    periods, _, ctrl_lon, ctrl_lat = controls.shape
    count = drift_move.shape[1]
    lon_count, lat_count = lax.axis_size("lon"), lax.axis_size("lat")
    refine = rows * lon_count // ctrl_lon
    tall, wide = rows + 16, cells_lat + 256
    surface = (2, DEPTH, rows, cells_lat)
    lon_message = (3 * FIELDS + HIGH * PLANES, 256)
    inner, outer, beside = call(
        pack_kernel,
        (drift_move, drift_cell, drift_weight, drift_obs, drift_precision, initial, depth_levels, mixing),
        (lon_message, lon_message, (2 * FIELDS, 256)),
        scratch=(
            pltpu.VMEM(drift_move.shape, jnp.int32),
            pltpu.VMEM(drift_cell.shape, jnp.int32),
            drift_weight.shape,
            drift_obs.shape,
            drift_precision.shape,
            (2, 2, DEPTH, 8, cells_lat),
            pltpu.VMEM((2, 8, cells_lat), jnp.int32),
            (2, 8, cells_lat),
            (STEPS * FIELDS, count),
            lon_message,
            lon_message,
            pltpu.SemaphoreType.DMA((11,)),
        ),
        far=True,
        vmem=60,
    )
    inner, outer = swap(inner, outer)
    fields, forcing, beside = call(
        functools.partial(own_kernel, refine, lat_count),
        (jnp.swapaxes(controls, 2, 3), drift_move, drift_cell, drift_weight, drift_obs, drift_precision, beside),
        ((STEPS * FIELDS, count), (2 * STEPS, tall, wide), (2 * FIELDS, 256)),
    )
    message = (3 * FIELDS + tall // 2, 256)
    padded, south, north = call(
        merge_kernel,
        (initial, depth_levels, mixing, beside, inner, outer),
        ((PLANES, tall, wide), message, message),
        {0: surface},
    )
    from_south, from_north = along(north, 1), along(south, -1)
    edge = (2 * DEPTH * HIGH, wide)
    ring = min(RING, lon_count // CORES)
    members = lon_count // (CORES * ring)
    partial, share, inner, outer = call(
        functools.partial(main_kernel, levels, refine, lat_count),
        (forcing, fields, drift_precision, inner, outer, from_south, from_north, padded),
        ((2 * DEPTH, tall, wide), (ring * CORES * lat_count, 2 * STEPS, 4 * GROUP), edge, edge),
        scratch=((2 * DEPTH, tall, wide), (2, tall, wide), edge, edge),
    )
    shares = gather(share, ring, 1, True)
    inner, outer = swap(inner, outer)
    height = -(-(4 * ring + 3) // 4) * 4
    share, own, to_south, to_north = call(
        functools.partial(plane_kernel, lat_count, ctrl_lat // lat_count),
        (shares, partial, inner, outer),
        ((members, STEPS * height, 2 * ctrl_lat), (2 * DEPTH, rows, cells_lat), (rows, 128), (rows, 128)),
        scratch=((4 * ring * CORES * lat_count, 4 * GROUP), (STEPS * height, 2 * ctrl_lat)),
    )
    from_south, from_north = along(to_north, 1), along(to_south, -1)
    shares = gather(share, members, ring, False)
    grad_initial, grad_controls = call(
        functools.partial(finish_kernel, float(STEPS * count * lon_count * lat_count)),
        (own, depth_levels, from_south, from_north, shares),
        (initial.shape, (periods, 2, ctrl_lat, ctrl_lon)),
        scratch=((STEPS, ctrl_lon, 2 * ctrl_lat),),
    )
    return grad_initial, jnp.swapaxes(grad_controls, 2, 3)


def solution(mesh):
    return jax.shard_map(
        shards,
        mesh=mesh,
        in_specs=(
            P(None, None, "lon", "lat"),
            P("lon", "lat"),
            P("lon", "lat"),
            P(),
            P(None, ("lon", "lat")),
            P(None, ("lon", "lat")),
            P(None, None, ("lon", "lat")),
            P(None, None, ("lon", "lat")),
            P(None, ("lon", "lat")),
        ),
        out_specs=(P(None, None, "lon", "lat"), P()),
        check_vma=False,
    )
```

```python
import functools
import math

import jax
import jax.numpy as jnp
from jax import lax
from jax.experimental import pallas as pl
from jax.experimental.pallas import tpu as pltpu
from jax.sharding import PartitionSpec as P

CAPACITY = 128
VISCOUS = 0.1
FRICTION = 0.02
ROTATION = 0.3
STEPS = 2
DEPTH = STEPS + 1
CODES = (0, 1, 2, 3, 5, 6, 7, 8)
FIELDS = 8
PLANES = 2 * DEPTH + 2
LOW, HIGH = 2, 3
X0, Y0 = 8, 128
CORES = 2
RING = 8
GROUP = 32
F32, BF16 = jnp.float32, jnp.bfloat16


def iota(shape, dim):
    return lax.broadcasted_iota(jnp.int32, shape, dim)


def split(value):
    high = value.astype(BF16)
    return high, (value - high.astype(F32)).astype(BF16)


def dot(a, b):
    return lax.dot_general(a, b, (((1,), (0,)), ((), ())), preferred_element_type=F32)


def dot_lanes(a, b):
    return lax.dot_general(a, b, (((1,), (1,)), ((), ())), preferred_element_type=F32)


def roll(value, shift, axis):
    return pltpu.roll(value, shift % value.shape[axis], axis)


def parity(axis):
    return lax.axis_index(axis) % 2


def pick(axis, first, second):
    even = parity(axis) == 0
    one, other = first[...], second[...]
    return jnp.where(even, other, one), jnp.where(even, one, other)


def address(axis, behind, ahead, first, second):
    even = parity(axis) == 0
    first[...] = jnp.where(even, ahead[...], behind[...])
    second[...] = jnp.where(even, behind[...], ahead[...])


def interpolation(offset, refine):
    low = lax.shift_right_arithmetic(offset, refine.bit_length() - 1)
    return low, ((offset - low * refine).astype(F32) + 0.5) / refine


def period_weights(steps_total, periods):
    table = []
    for step in range(steps_total):
        position = (step + 0.5) * (periods - 1) / steps_total
        table.append([max(0.0, 1.0 - abs(position - period)) for period in range(periods)])
    return table


def stage(fields, cell, weight, obs):
    for step in range(STEPS):
        base = step * FIELDS
        for i in range(4):
            fields[base + i : base + i + 1, :] = weight[i, step : step + 1, :]
        for i in range(2):
            fields[base + 4 + i : base + 5 + i, :] = obs[i, step : step + 1, :]
        fields[base + 7 : base + 8, :] = cell[step : step + 1, :].astype(F32)


def own_kernel(refine, lat_count, controls, move, cell, weight, obs, prec, fields, forcing):
    stage(fields, cell, weight, obs)
    for step in range(STEPS):
        row = step * FIELDS + 6
        fields[row : row + 1, :] = jnp.where(move[step : step + 1, :] == 4, prec[step : step + 1, :], 0.0)
    tall, wide = forcing.shape[1:]
    rows, cells_lat = tall - 16, wide - 256
    periods, _, ctrl_lat, ctrl_lon = controls.shape
    table = period_weights(STEPS, periods)
    low, part = interpolation(iota((tall, ctrl_lon), 0) - X0 + lax.axis_index("lon") * rows - refine // 2, refine)
    column = iota((tall, ctrl_lon), 1)
    wrapped, after = (low + ctrl_lon) % ctrl_lon, (low + 1 + ctrl_lon) % ctrl_lon
    lon_interp = jnp.where(column == wrapped, 1.0 - part, 0.0) + jnp.where(column == after, part, 0.0)
    low, part = interpolation(iota((ctrl_lat, wide), 1) - Y0 + lax.axis_index("lat") * cells_lat - refine // 2, refine)
    column = iota((ctrl_lat, wide), 0)
    lat_interp = jnp.where(column == low, 1.0 - part, 0.0) + jnp.where(column == low + 1, part, 0.0)
    lon_interp, lat_interp = lon_interp.astype(BF16), lat_interp.astype(BF16)
    for step in range(STEPS):
        for c in range(2):
            blended = table[step][0] * controls[0, c]
            for period in range(1, periods):
                blended = blended + table[step][period] * controls[period, c]
            high, low = split(blended)
            high, low = split(dot_lanes(lon_interp, high) + dot_lanes(lon_interp, low))
            forcing[2 * step + c] = dot(high, lat_interp) + dot(low, lat_interp)


def near_kernel(beside, near):
    near[...] = beside[...]


def pack_kernel(
    move_far, cell_far, weight_far, obs_far, prec_far, init_far, depth_far, mixing_far, inner, outer, beside,
    move, cell, weight, obs, prec, init, depth, mixing, fields, east, west, arrived,
):
    count = move.shape[1]
    rows = depth_far.shape[0]
    whole_arrays = [(move_far, move), (cell_far, cell), (weight_far, weight), (obs_far, obs), (prec_far, prec)]
    edges = []
    for end, first in enumerate((0, rows - 8)):
        edges.append((init_far.at[:, :DEPTH, pl.ds(first, 8), :], init.at[end]))
        edges.append((depth_far.at[pl.ds(first, 8), :], depth.at[end]))
        edges.append((mixing_far.at[pl.ds(first, 8), :], mixing.at[end]))
    copies = [pltpu.make_async_copy(far, near, arrived.at[i]) for i, (far, near) in enumerate(whole_arrays + edges)]
    for copy in copies:
        copy.start()
    copies[0].wait()
    width = 256
    blocks = count // width
    triangle = (iota((width, width), 0) <= iota((width, width), 1)).astype(F32).astype(BF16)
    code = iota((8, 1), 0)
    code = code + (code >= 4).astype(jnp.int32)
    matches = []
    for step in range(STEPS):
        for block in range(blocks):
            matches.append((move[step : step + 1, block * width : (block + 1) * width] == code).astype(F32))
    ranks = dot(jnp.concatenate(matches, axis=0).astype(BF16), triangle)
    places = []
    for step in range(STEPS):
        carry = jnp.full((8, 1), -1.0, F32)
        for block in range(blocks):
            at = step * blocks + block
            rank = ranks[8 * at : 8 * at + 8]
            places.append(jnp.sum(matches[at] * (rank + carry), axis=0, keepdims=True))
            carry = carry + rank[:, width - 1 :]
    for copy in copies[1:]:
        copy.wait()
    stage(fields, cell, weight, obs)
    for step in range(STEPS):
        fields[step * FIELDS + 6 : step * FIELDS + 7, :] = prec[step : step + 1, :]
    for p in range(PLANES):
        for end, strip, first, size in ((0, west, 0, HIGH), (1, east, 8 - LOW, LOW)):
            if p < 2 * DEPTH:
                line = init[end, p // DEPTH, p % DEPTH, first : first + size, :]
            elif p == 2 * DEPTH:
                line = depth[end, first : first + size, :].astype(F32)
            else:
                line = mixing[end, first : first + size, :]
            strip[3 * FIELDS + size * p : 3 * FIELDS + size * (p + 1), :] = line
    joined = 2
    slot = iota((CAPACITY, joined * width), 0).astype(F32).astype(BF16)
    one, nought = jnp.ones((), BF16), jnp.zeros((), BF16)
    for step in range(STEPS):
        packed = jnp.zeros((8 * 2 * FIELDS, CAPACITY), F32)
        for block in range(0, blocks, joined):
            at = step * blocks + block
            place = jnp.concatenate(places[at : at + joined], axis=1).astype(BF16)
            spots = jnp.where(slot == place, one, nought)
            lanes = slice(block * width, (block + joined) * width)
            both = jnp.concatenate(split(fields[step * FIELDS : (step + 1) * FIELDS, lanes]), axis=0)
            kind = jnp.broadcast_to(move[step : step + 1, lanes].astype(F32), both.shape).astype(BF16)
            masked = jnp.concatenate([jnp.where(kind == jnp.full((), c, BF16), both, nought) for c in CODES], axis=0)
            packed = packed + dot_lanes(masked, spots)
        lanes = slice(step * CAPACITY, (step + 1) * CAPACITY)
        for d in range(8):
            at = d * 2 * FIELDS
            record = packed[at : at + FIELDS] + packed[at + FIELDS : at + 2 * FIELDS]
            if CODES[d] // 3 == 1:
                row = CODES[d] % 3 // 2 * FIELDS
                beside[row : row + FIELDS, lanes] = record
            else:
                row = (CODES[d] % 3) * FIELDS
                (west if CODES[d] // 3 == 0 else east)[row : row + FIELDS, lanes] = record
    address("lon", west, east, inner, outer)


def extend_lon(ext, p, own, from_west, from_east, rows, cells_lat):
    lanes = slice(Y0, Y0 + cells_lat)
    ext[p, X0 : X0 + rows, lanes] = own
    at = 3 * FIELDS + LOW * p
    ext[p, X0 - LOW : X0, lanes] = from_west[at : at + LOW, :]
    at = 3 * FIELDS + HIGH * p
    ext[p, X0 + rows : X0 + rows + HIGH, lanes] = from_east[at : at + HIGH, :]


def merge_kernel(init, depth, mixing, beside, outer, inner, ext, first_out, second_out, south, north):
    from_west, from_east = pick("lon", inner, outer)
    rows, cells_lat = depth.shape
    ext[...] = jnp.zeros_like(ext)
    for p in range(PLANES):
        if p < 2 * DEPTH:
            own = init[p // DEPTH, p % DEPTH]
        else:
            own = depth[...].astype(F32) if p == 2 * DEPTH else mixing[...]
        extend_lon(ext, p, own, from_west, from_east, rows, cells_lat)
    tall = ext.shape[1]
    lane = iota((tall, 128), 1)
    first = jnp.zeros((tall, 128), F32)
    last = jnp.zeros((tall, 128), F32)
    for p in range(PLANES):
        head = jnp.where(lane < HIGH, ext[p, :, Y0 : Y0 + 128], 0.0)
        tail = jnp.where(lane >= 128 - LOW, ext[p, :, Y0 + cells_lat - 128 : Y0 + cells_lat], 0.0)
        first = first + roll(head, HIGH * p, 1)
        last = last + roll(tail, -LOW * p, 1)
    for out, kept, row, strip in ((south, 0, 0, first), (north, 1, 2, last)):
        out[0:FIELDS, :] = beside[kept * FIELDS : (kept + 1) * FIELDS, :]
        out[FIELDS : 2 * FIELDS, :] = from_west[row * FIELDS : (row + 1) * FIELDS, :]
        out[2 * FIELDS : 3 * FIELDS, :] = from_east[row * FIELDS : (row + 1) * FIELDS, :]
        third = tall // 3
        strip = strip[:third] + roll(strip[third : 2 * third], 32, 1) + roll(strip[2 * third :], 64, 1)
        out[3 * FIELDS :, 0:128] = strip[: third // 2]
        out[3 * FIELDS :, 128:] = strip[third // 2 :]
    address("lat", south, north, first_out, second_out)


def lap(v):
    return roll(v, 1, 0) + roll(v, -1, 0) + roll(v, 1, 1) + roll(v, -1, 1) - 4.0 * v


def vz(column, k, levels):
    above = column[max(k - 1, 0)]
    below = min(k + 1, levels - 1)
    total = above - 2.0 * column[k] if k < len(column) else above
    return total + column[below] if below < len(column) else total


def tendency(v, k, mixing, rotation, levels):
    out = []
    for c in range(2):
        value = v[c][k] + mixing(v[c][k]) + VISCOUS * vz(v[c], k, levels) - FRICTION * v[c][k]
        turned = rotation * v[1 - c][k]
        out.append(value + turned if c == 0 else value - turned)
    return out


def main_kernel(
    levels, refine, lat_count, forcing, fields, precision, outer, inner, first, second,
    padded, partial, share, to_inner, to_outer, ext, spot, to_west, to_east,
):
    from_west, from_east = pick("lon", inner, outer)
    from_south, from_north = pick("lat", first, second)
    rows, cells_lat = partial.shape[1] - 16, partial.shape[2] - 256
    tall, wide = ext.shape[1:]
    lat_index = lax.axis_index("lat")
    grid_lat = cells_lat * lat_count
    lane = iota((tall, 128), 1)
    below, above = [
        jnp.concatenate([message[3 * FIELDS :, 0:128], message[3 * FIELDS :, 128:]], axis=0)
        for message in (from_south, from_north)
    ]
    below, above = [jnp.concatenate([v, roll(v, -32, 1), roll(v, -64, 1)], axis=0) for v in (below, above)]
    full = []
    for p in range(PLANES):
        left = jnp.where(lane >= 128 - LOW, roll(below, LOW * p, 1), 0.0)
        right = jnp.where(lane < HIGH, roll(above, -HIGH * p, 1), 0.0)
        full.append(jnp.concatenate([left, padded[p, :, Y0 : Y0 + cells_lat], right], axis=1))
    mixing = full[2 * DEPTH + 1]
    wet = [(full[2 * DEPTH] > float(k)).astype(F32) for k in range(DEPTH)]
    row_ids = iota((1, wide), 1) - Y0 + lat_index * cells_lat
    rotation = ROTATION * jnp.sin((row_ids.astype(F32) + 0.5) * (math.pi / grid_lat) - 0.5 * math.pi)
    state = [[wet[k] * full[c * DEPTH + k] for k in range(DEPTH)] for c in range(2)]
    surfaces = []
    for step in range(STEPS):
        ahead = [[], []]
        for k in range(DEPTH - 1 - step):
            moved = tendency(state, k, lambda v: mixing * lap(v), rotation, levels)
            for c in range(2):
                value = moved[c] + forcing[2 * step + c] if k == 0 else moved[c]
                ahead[c].append(wet[k] * value)
        state = ahead
        surfaces.append([state[0][0], state[1][0]])
    chunk = 512
    lat_of = iota((cells_lat, chunk), 0).astype(F32).astype(BF16)
    lon_of = iota((rows, chunk), 0).astype(F32)
    lon_tile = lon_of.astype(BF16)
    one, nought = jnp.ones((), BF16), jnp.zeros((), BF16)
    sources = []
    for step in range(STEPS):
        views, edges = [], []
        for c in range(2):
            surface = surfaces[step][c][X0 : X0 + rows + 8]
            for view in (surface, roll(surface, -1, 1)):
                views.append(view[:rows, Y0 : Y0 + cells_lat])
                edges.append(view[rows : rows + 1, Y0 : Y0 + cells_lat])
        views = jnp.concatenate(views + edges + [jnp.zeros((4, cells_lat), F32)], axis=0)
        high, low = split(views)
        views = jnp.concatenate([high.astype(F32), low.astype(F32)], axis=0).astype(BF16)
        seen_rows = 4 * rows + 8

        def spread(record, total):
            cell = record[7:8].astype(jnp.int32)
            lon = lax.shift_right_logical(cell, cells_lat.bit_length() - 1).astype(F32)
            lat = (cell & (cells_lat - 1)).astype(F32).astype(BF16)
            hot = jnp.where(lat_of == lat, one, nought)
            found = dot(views, hot)
            found = found[:seen_rows] + found[seen_rows:]
            here, there, edge = lon_of == lon, lon_of == lon + 1.0, lon == rows - 1.0
            near = jnp.where(here, record[0:1], jnp.where(there, record[1:2], 0.0))
            far = jnp.where(here, record[2:3], jnp.where(there, record[3:4], 0.0))
            near_edge, far_edge = jnp.where(edge, record[1:2], 0.0), jnp.where(edge, record[3:4], 0.0)
            lon = lon.astype(BF16)
            here, there = lon_tile == lon, lon_tile == lon + one
            terms, outside = [[], []], []
            for c in range(2):
                at, last = 2 * c * rows, 4 * rows + 2 * c
                seen = near * found[at : at + rows] + far * found[at + rows : at + 2 * rows]
                miss = jnp.sum(seen, axis=0, keepdims=True) - record[4 + c : 5 + c]
                miss = miss + near_edge * found[last : last + 1] + far_edge * found[last + 1 : last + 2]
                parts = split(record[0:4] * (record[6:7] * miss))
                for part, term in zip(parts, terms):
                    outside.append(jnp.where(edge, part.astype(F32), 0.0))
                    for d in (0, 2):
                        term.append(jnp.where(here, part[d : d + 1], jnp.where(there, part[d + 1 : d + 2], nought)))
            outside = jnp.concatenate(outside, axis=0).astype(BF16)
            return total + dot_lanes(jnp.concatenate(terms[0] + terms[1] + [outside], axis=0), hot)

        total = jnp.zeros((8 * rows + 16, cells_lat), F32)
        for at in range(0, fields.shape[1], chunk):
            total = spread(fields[step * FIELDS : (step + 1) * FIELDS, at : at + chunk], total)
        lanes = slice(step * CAPACITY, (step + 1) * CAPACITY)
        came = [from_west[FIELDS : 2 * FIELDS, lanes], from_east[FIELDS : 2 * FIELDS, lanes]]
        came += [message[i * FIELDS : (i + 1) * FIELDS, lanes] for message in (from_south, from_north) for i in range(3)]
        for at in range(0, 8, chunk // CAPACITY):
            total = spread(jnp.concatenate(came[at : at + chunk // CAPACITY], axis=1), total)
        sources.append([])
        outside = total[8 * rows :]
        total = total[: 4 * rows] + total[4 * rows : 8 * rows]
        for c in range(2):
            spot[...] = jnp.zeros_like(spot)
            for d in range(2):
                at, last = (2 * c + d) * rows, 8 * c + 2 * d + 1
                spot[d, X0 : X0 + rows, Y0 : Y0 + cells_lat] = total[at : at + rows]
                edge = outside[last : last + 1] + outside[last + 4 : last + 5]
                spot[d, X0 + rows : X0 + rows + 1, Y0 : Y0 + cells_lat] = edge
            sources[step].append(spot[0] + roll(spot[1], 1, 1))
    adjoint = None
    nudges = [None] * STEPS
    for step in reversed(range(STEPS)):
        if adjoint is None:
            adjoint = [[sources[step][c]] for c in range(2)]
        else:
            adjoint = [[adjoint[c][0] + sources[step][c]] + adjoint[c][1:] for c in range(2)]
        nudged = [[wet[k] * adjoint[c][k] for k in range(len(adjoint[c]))] for c in range(2)]
        nudges[step] = [nudged[0][0], nudged[1][0]]
        reach = len(nudged[0])
        adjoint = [[], []]
        for k in range(reach):
            moved = tendency(nudged, k, lambda v: lap(mixing * v), -rotation, levels)
            for c in range(2):
                adjoint[c].append(moved[c])
        for c in range(2):
            adjoint[c].append(VISCOUS * vz(nudged[c], reach, levels))
    for c in range(2):
        for k in range(DEPTH):
            p = c * DEPTH + k
            ext[p] = adjoint[c][k]
            partial[p] = adjoint[c][k]
            to_west[LOW * p : LOW * (p + 1), :] = ext[p, X0 - LOW : X0, :]
            to_east[HIGH * p : HIGH * (p + 1), :] = ext[p, X0 + rows : X0 + rows + HIGH, :]
    address("lon", to_west, to_east, to_inner, to_outer)
    low, part = interpolation(iota((wide, 4 * GROUP), 0) - Y0 - refine // 2, refine)
    column = iota((wide, 4 * GROUP), 1) % GROUP - 1
    onto_lat = jnp.where(column == low, 1.0 - part, 0.0) + jnp.where(column == low + 1, part, 0.0)
    onto_lat = onto_lat.astype(BF16)
    low, part = interpolation(iota((tall, 4 * GROUP), 0) - X0 - refine // 2, refine)
    column = iota((tall, 4 * GROUP), 1) // GROUP - 1
    onto_lon = jnp.where(column == low, 1.0 - part, 0.0) + jnp.where(column == low + 1, part, 0.0)
    weight = jnp.sum(jnp.sum(precision[...], axis=0, keepdims=True), axis=1, keepdims=True)
    parts = []
    for step in range(STEPS):
        for c in range(2):
            high, rest = split(nudges[step][c])
            across = dot(high, onto_lat) + dot(rest, onto_lat)
            parts.append(jnp.sum(onto_lon * across, axis=0, keepdims=True))
    parts[0] = jnp.where(iota((1, 4 * GROUP), 1) == 4 * GROUP - 1, weight, parts[0])
    share[...] = jnp.broadcast_to(jnp.concatenate(parts, axis=0)[None], share.shape)


def plane_kernel(lat_count, per, shares, partial, outer, inner, out, own, first, second, rows, total):
    join(partial, inner, outer, own, first, second)
    members = shares.shape[0]
    ring = members // (CORES * lat_count)
    ctrl_lat = per * lat_count
    for m in range(members):
        rows[4 * m : 4 * m + 4, :] = shares[m]
    total[...] = jnp.zeros_like(total)
    lane = iota((ring, 4 * GROUP), 1)
    height = total.shape[0] // STEPS
    weight = jnp.zeros((ring, 4 * GROUP), F32)
    for core in range(CORES):
        for step in range(STEPS):
            sums = [jnp.zeros((ring, 4 * GROUP), F32) for _ in range(4)]
            for band in range(lat_count):
                for c in range(2):
                    at = 4 * (core * lat_count + band) + 2 * step + c
                    held = rows[pl.ds(at, ring, stride=4 * CORES * lat_count), :]
                    if step == 0 and c == 0:
                        weight = weight + held
                    start = c * ctrl_lat + per * band - 1
                    first, last = max(start, c * ctrl_lat), min(start + per + 1, (c + 1) * ctrl_lat - 1)
                    mine = (lane >= first) & (lane <= last)
                    for a in range(4):
                        sums[a] = sums[a] + jnp.where(mine, roll(held, start - GROUP * a, 1), 0.0)
            for a in range(4):
                at = step * height + 2 * core + a
                total[pl.ds(at, ring, stride=4), :] = total[pl.ds(at, ring, stride=4), :] + sums[a]
    weight = jnp.sum(jnp.where(lane == 4 * GROUP - 1, weight, 0.0), axis=0, keepdims=True)
    weight = jnp.sum(weight, axis=1, keepdims=True)
    total[4 * ring + 2 : 4 * ring + 3, :] = jnp.broadcast_to(weight, (1, 4 * GROUP))
    out[...] = jnp.broadcast_to(total[...][None], out.shape)


def join(partial, inner, outer, own, first_out, second_out):
    from_west, from_east = pick("lon", inner, outer)
    rows, cells_lat = own.shape[1:]
    lane = iota((rows, 128), 1)
    first = jnp.zeros((rows, 128), F32)
    last = jnp.zeros((rows, 128), F32)
    for p in range(2 * DEPTH):
        partial[p, X0 : X0 + HIGH, :] += from_west[HIGH * p : HIGH * (p + 1), :]
        partial[p, X0 + rows - LOW : X0 + rows, :] += from_east[LOW * p : LOW * (p + 1), :]
        block = partial[p, X0 : X0 + rows, :]
        own[p] = block[:, Y0 : Y0 + cells_lat]
        tail = jnp.where(lane >= 128 - LOW, block[:, Y0 - 128 : Y0], 0.0)
        head = jnp.where(lane < HIGH, block[:, Y0 + cells_lat : Y0 + cells_lat + 128], 0.0)
        first = first + roll(tail, -LOW * p, 1)
        last = last + roll(head, HIGH * p, 1)
    address("lat", first, last, first_out, second_out)


def finish_kernel(normalizer, own, depth, first, second, shares, grad, out, full):
    from_south, from_north = pick("lat", first, second)
    levels, rows, cells_lat = grad.shape[1:]
    periods, _, ctrl_lat, ctrl_lon = out.shape
    table = period_weights(STEPS, periods)
    members, size = shares.shape[:2]
    span = ctrl_lon // members
    total = shares[0, span + 2 : span + 3, :]
    for m in range(1, members):
        total = total + shares[m, span + 2 : span + 3, :]
    scale = normalizer / total[:, 0:1]
    side = iota((rows, 128), 1)
    wet_levels = depth[...]
    for c in range(2):
        for k in range(levels):
            if k >= DEPTH:
                grad[c, k] = jnp.zeros((rows, cells_lat), F32)
                continue
            p = c * DEPTH + k
            low = jnp.where(side < HIGH, roll(from_south, -HIGH * p, 1), 0.0)
            high = jnp.where(side >= 128 - LOW, roll(from_north, LOW * p, 1), 0.0)
            value = own[p] + jnp.concatenate([low, high], axis=1)
            grad[c, k] = jnp.where(wet_levels > k, value * scale, 0.0)
    for step in range(STEPS):
        at = step * size // STEPS
        for m in range(members):
            full[step, m * span : (m + 1) * span, :] = shares[m, at + 1 : at + 1 + span, :]
        for m in range(members):
            before, after = (m * span + ctrl_lon - 1) % ctrl_lon, (m + 1) * span % ctrl_lon
            full[step, before : before + 1, :] += shares[m, at : at + 1, :]
            full[step, after : after + 1, :] += shares[m, at + span + 1 : at + span + 2, :]
    scaled = [scale * full[step] for step in range(STEPS)]
    for period in range(periods):
        value = table[0][period] * scaled[0]
        for step in range(1, STEPS):
            value = value + table[step][period] * scaled[step]
        value = value.T
        for c in range(2):
            out[period, c] = value[c * ctrl_lat : (c + 1) * ctrl_lat]


def swap(axis, first, second, periodic):
    count = lax.axis_size(axis)
    across = [(i, i + 1) for i in range(1, count - 1, 2)]
    if periodic:
        across.append((count - 1, 0))
    second = lax.ppermute(second, axis, across + [(b, a) for a, b in across])
    first = lax.ppermute(first, axis, [(i, i ^ 1) for i in range(count)])
    return first, second


def gather(copies, chips, stride, whole_chips):
    if copies.shape[0] == 1:
        return copies
    count = lax.axis_size("lat")
    per_chip = CORES * count
    inside = [range(per_chip)] if whole_chips else [(i,) for i in range(per_chip)]
    groups = []
    for base in range(lax.axis_size("lon") // CORES):
        if base // stride % chips == 0:
            for few in inside:
                groups.append([(base + chip * stride) * per_chip + i for chip in range(chips) for i in few])
    return lax.all_to_all(copies, ("lon", "lat"), 0, 0, axis_index_groups=groups, tiled=True)


def whole(shape):
    return pl.BlockSpec(shape, lambda i: (0,) * len(shape))


def call(kernel, ins, outs, blocks=None, scratch=(), far=False, vmem=16):
    blocks = blocks or {}
    specs = [whole(blocks.get(i, value.shape)) for i, value in enumerate(ins)]
    if far:
        specs = [pl.BlockSpec(memory_space=pltpu.HBM) for _ in ins]
    return pl.pallas_call(
        kernel,
        grid=(1,),
        out_shape=[jax.ShapeDtypeStruct(shape, F32) for shape in outs],
        in_specs=specs,
        out_specs=[whole(shape) for shape in outs],
        scratch_shapes=[pltpu.VMEM(shape, F32) if isinstance(shape, tuple) else shape for shape in scratch],
        compiler_params=pltpu.CompilerParams(vmem_limit_bytes=vmem * 1024 * 1024),
    )(*ins)


def shards(
    initial, depth_levels, mixing, controls, drift_move, drift_cell, drift_weight, drift_obs, drift_precision
):
    _, levels, rows, cells_lat = initial.shape
    periods, _, ctrl_lon, ctrl_lat = controls.shape
    count = drift_move.shape[1]
    lon_count, lat_count = lax.axis_size("lon"), lax.axis_size("lat")
    refine = rows * lon_count // ctrl_lon
    tall, wide = rows + 16, cells_lat + 256
    surface = (2, DEPTH, rows, cells_lat)
    lon_message = (3 * FIELDS + HIGH * PLANES, 256)
    inner, outer, beside = call(
        pack_kernel,
        (drift_move, drift_cell, drift_weight, drift_obs, drift_precision, initial, depth_levels, mixing),
        (lon_message, lon_message, (2 * FIELDS, 256)),
        scratch=(
            pltpu.VMEM(drift_move.shape, jnp.int32),
            pltpu.VMEM(drift_cell.shape, jnp.int32),
            drift_weight.shape,
            drift_obs.shape,
            drift_precision.shape,
            (2, 2, DEPTH, 8, cells_lat),
            pltpu.VMEM((2, 8, cells_lat), jnp.int32),
            (2, 8, cells_lat),
            (STEPS * FIELDS, count),
            lon_message,
            lon_message,
            pltpu.SemaphoreType.DMA((11,)),
        ),
        far=True,
        vmem=60,
    )
    inner, outer = swap("lon", inner, outer, True)
    fields, forcing = call(
        functools.partial(own_kernel, refine, lat_count),
        (jnp.swapaxes(controls, 2, 3), drift_move, drift_cell, drift_weight, drift_obs, drift_precision),
        ((STEPS * FIELDS, count), (2 * STEPS, tall, wide)),
    )
    message = (3 * FIELDS + tall // 6, 256)
    (beside,) = call(near_kernel, (beside,), ((2 * FIELDS, 256),))
    padded, first, second = call(
        merge_kernel,
        (initial, depth_levels, mixing, beside, outer, inner),
        ((PLANES, tall, wide), message, message),
        {0: surface},
        scratch=(message, message),
    )
    first, second = swap("lat", first, second, False)
    edge = (2 * DEPTH * HIGH, wide)
    ring = min(RING, lon_count // CORES)
    members = lon_count // (CORES * ring)
    partial, share, inner, outer = call(
        functools.partial(main_kernel, levels, refine, lat_count),
        (forcing, fields, drift_precision, outer, inner, first, second, padded),
        ((2 * DEPTH, tall, wide), (ring * CORES * lat_count, 2 * STEPS, 4 * GROUP), edge, edge),
        scratch=((2 * DEPTH, tall, wide), (2, tall, wide), edge, edge),
    )
    shares = gather(share, ring, 1, True)
    inner, outer = swap("lon", inner, outer, True)
    height = -(-(4 * ring + 3) // 4) * 4
    share, own, first, second = call(
        functools.partial(plane_kernel, lat_count, ctrl_lat // lat_count),
        (shares, partial, outer, inner),
        ((members, STEPS * height, 2 * ctrl_lat), (2 * DEPTH, rows, cells_lat), (rows, 128), (rows, 128)),
        scratch=((4 * ring * CORES * lat_count, 4 * GROUP), (STEPS * height, 2 * ctrl_lat)),
    )
    first, second = swap("lat", first, second, False)
    shares = gather(share, members, ring, False)
    grad_initial, grad_controls = call(
        functools.partial(finish_kernel, float(STEPS * count * lon_count * lat_count)),
        (own, depth_levels, first, second, shares),
        (initial.shape, (periods, 2, ctrl_lat, ctrl_lon)),
        scratch=((STEPS, ctrl_lon, 2 * ctrl_lat),),
    )
    return grad_initial, jnp.swapaxes(grad_controls, 2, 3)


def solution(mesh):
    return jax.shard_map(
        shards,
        mesh=mesh,
        in_specs=(
            P(None, None, "lon", "lat"),
            P("lon", "lat"),
            P("lon", "lat"),
            P(),
            P(None, ("lon", "lat")),
            P(None, ("lon", "lat")),
            P(None, None, ("lon", "lat")),
            P(None, None, ("lon", "lat")),
            P(None, ("lon", "lat")),
        ),
        out_specs=(P(None, None, "lon", "lat"), P()),
        check_vma=False,
    )
```

```python
import functools
import math

import jax
import jax.numpy as jnp
from jax import lax
from jax.experimental import pallas as pl
from jax.experimental.pallas import tpu as pltpu
from jax.sharding import PartitionSpec as P

CAPACITY = 128
VISCOUS = 0.1
FRICTION = 0.02
ROTATION = 0.3
STEPS = 2
DEPTH = STEPS + 1
CODES = (0, 1, 2, 3, 5, 6, 7, 8)
FIELDS = 8
PLANES = 2 * DEPTH + 2
LOW, HIGH = 2, 3
X0, Y0 = 8, 128
CORES = 2
RING = 8
GROUP = 32
F32, BF16 = jnp.float32, jnp.bfloat16


def iota(shape, dim):
    return lax.broadcasted_iota(jnp.int32, shape, dim)


def split(value):
    high = value.astype(BF16)
    return high, (value - high.astype(F32)).astype(BF16)


def dot(a, b):
    return lax.dot_general(a, b, (((1,), (0,)), ((), ())), preferred_element_type=F32)


def dot_lanes(a, b):
    return lax.dot_general(a, b, (((1,), (1,)), ((), ())), preferred_element_type=F32)


def roll(value, shift, axis):
    return pltpu.roll(value, shift % value.shape[axis], axis)


def parity(axis):
    return lax.axis_index(axis) % 2


def pick(axis, first, second):
    even = parity(axis) == 0
    one, other = first[...], second[...]
    return jnp.where(even, other, one), jnp.where(even, one, other)


def address(axis, behind, ahead, first, second):
    even = parity(axis) == 0
    first[...] = jnp.where(even, ahead[...], behind[...])
    second[...] = jnp.where(even, behind[...], ahead[...])


def interpolation(offset, refine):
    low = lax.shift_right_arithmetic(offset, refine.bit_length() - 1)
    return low, ((offset - low * refine).astype(F32) + 0.5) / refine


def period_weights(steps_total, periods):
    table = []
    for step in range(steps_total):
        position = (step + 0.5) * (periods - 1) / steps_total
        table.append([max(0.0, 1.0 - abs(position - period)) for period in range(periods)])
    return table


def stage(fields, cell, weight, obs):
    for step in range(STEPS):
        base = step * FIELDS
        for i in range(4):
            fields[base + i : base + i + 1, :] = weight[i, step : step + 1, :]
        for i in range(2):
            fields[base + 4 + i : base + 5 + i, :] = obs[i, step : step + 1, :]
        fields[base + 7 : base + 8, :] = cell[step : step + 1, :].astype(F32)


def own_kernel(refine, lat_count, controls, move, cell, weight, obs, prec, fields, forcing):
    stage(fields, cell, weight, obs)
    for step in range(STEPS):
        row = step * FIELDS + 6
        fields[row : row + 1, :] = jnp.where(move[step : step + 1, :] == 4, prec[step : step + 1, :], 0.0)
    tall, wide = forcing.shape[1:]
    rows, cells_lat = tall - 16, wide - 256
    periods, _, ctrl_lat, ctrl_lon = controls.shape
    table = period_weights(STEPS, periods)
    low, part = interpolation(iota((tall, ctrl_lon), 0) - X0 + lax.axis_index("lon") * rows - refine // 2, refine)
    column = iota((tall, ctrl_lon), 1)
    wrapped, after = (low + ctrl_lon) % ctrl_lon, (low + 1 + ctrl_lon) % ctrl_lon
    lon_interp = jnp.where(column == wrapped, 1.0 - part, 0.0) + jnp.where(column == after, part, 0.0)
    low, part = interpolation(iota((ctrl_lat, wide), 1) - Y0 + lax.axis_index("lat") * cells_lat - refine // 2, refine)
    column = iota((ctrl_lat, wide), 0)
    lat_interp = jnp.where(column == low, 1.0 - part, 0.0) + jnp.where(column == low + 1, part, 0.0)
    lon_interp, lat_interp = lon_interp.astype(BF16), lat_interp.astype(BF16)
    for step in range(STEPS):
        for c in range(2):
            blended = table[step][0] * controls[0, c]
            for period in range(1, periods):
                blended = blended + table[step][period] * controls[period, c]
            high, low = split(blended)
            high, low = split(dot_lanes(lon_interp, high) + dot_lanes(lon_interp, low))
            forcing[2 * step + c] = dot(high, lat_interp) + dot(low, lat_interp)


def near_kernel(beside, near):
    near[...] = beside[...]


def pack_kernel(
    move_far, cell_far, weight_far, obs_far, prec_far, init_far, depth_far, mixing_far, inner, outer, beside,
    move, cell, weight, obs, prec, init, depth, mixing, fields, east, west, arrived,
):
    count = move.shape[1]
    rows = depth_far.shape[0]
    whole_arrays = [(move_far, move), (cell_far, cell), (weight_far, weight), (obs_far, obs), (prec_far, prec)]
    edges = []
    for end, first in enumerate((0, rows - 8)):
        edges.append((init_far.at[:, :DEPTH, pl.ds(first, 8), :], init.at[end]))
        edges.append((depth_far.at[pl.ds(first, 8), :], depth.at[end]))
        edges.append((mixing_far.at[pl.ds(first, 8), :], mixing.at[end]))
    copies = [pltpu.make_async_copy(far, near, arrived.at[i]) for i, (far, near) in enumerate(whole_arrays + edges)]
    for copy in copies:
        copy.start()
    copies[0].wait()
    width = 256
    blocks = count // width
    triangle = (iota((width, width), 0) <= iota((width, width), 1)).astype(F32).astype(BF16)
    code = iota((8, 1), 0)
    code = code + (code >= 4).astype(jnp.int32)
    matches = []
    for step in range(STEPS):
        for block in range(blocks):
            matches.append((move[step : step + 1, block * width : (block + 1) * width] == code).astype(F32))
    ranks = dot(jnp.concatenate(matches, axis=0).astype(BF16), triangle)
    places = []
    for step in range(STEPS):
        carry = jnp.full((8, 1), -1.0, F32)
        for block in range(blocks):
            at = step * blocks + block
            rank = ranks[8 * at : 8 * at + 8]
            places.append(jnp.sum(matches[at] * (rank + carry), axis=0, keepdims=True))
            carry = carry + rank[:, width - 1 :]
    for copy in copies[1:]:
        copy.wait()
    stage(fields, cell, weight, obs)
    for step in range(STEPS):
        fields[step * FIELDS + 6 : step * FIELDS + 7, :] = prec[step : step + 1, :]
    for p in range(PLANES):
        for end, strip, first, size in ((0, west, 0, HIGH), (1, east, 8 - LOW, LOW)):
            if p < 2 * DEPTH:
                line = init[end, p // DEPTH, p % DEPTH, first : first + size, :]
            elif p == 2 * DEPTH:
                line = depth[end, first : first + size, :].astype(F32)
            else:
                line = mixing[end, first : first + size, :]
            strip[3 * FIELDS + size * p : 3 * FIELDS + size * (p + 1), :] = line
    joined = 2
    slot = iota((CAPACITY, joined * width), 0).astype(F32).astype(BF16)
    one, nought = jnp.ones((), BF16), jnp.zeros((), BF16)
    for step in range(STEPS):
        packed = jnp.zeros((8 * 2 * FIELDS, CAPACITY), F32)
        for block in range(0, blocks, joined):
            at = step * blocks + block
            place = jnp.concatenate(places[at : at + joined], axis=1).astype(BF16)
            spots = jnp.where(slot == place, one, nought)
            lanes = slice(block * width, (block + joined) * width)
            both = jnp.concatenate(split(fields[step * FIELDS : (step + 1) * FIELDS, lanes]), axis=0)
            kind = jnp.broadcast_to(move[step : step + 1, lanes].astype(F32), both.shape).astype(BF16)
            masked = jnp.concatenate([jnp.where(kind == jnp.full((), c, BF16), both, nought) for c in CODES], axis=0)
            packed = packed + dot_lanes(masked, spots)
        lanes = slice(step * CAPACITY, (step + 1) * CAPACITY)
        for d in range(8):
            at = d * 2 * FIELDS
            record = packed[at : at + FIELDS] + packed[at + FIELDS : at + 2 * FIELDS]
            if CODES[d] // 3 == 1:
                row = CODES[d] % 3 // 2 * FIELDS
                beside[row : row + FIELDS, lanes] = record
            else:
                row = (CODES[d] % 3) * FIELDS
                (west if CODES[d] // 3 == 0 else east)[row : row + FIELDS, lanes] = record
    address("lon", west, east, inner, outer)


def extend_lon(ext, p, own, from_west, from_east, rows, cells_lat):
    lanes = slice(Y0, Y0 + cells_lat)
    ext[p, X0 : X0 + rows, lanes] = own
    at = 3 * FIELDS + LOW * p
    ext[p, X0 - LOW : X0, lanes] = from_west[at : at + LOW, :]
    at = 3 * FIELDS + HIGH * p
    ext[p, X0 + rows : X0 + rows + HIGH, lanes] = from_east[at : at + HIGH, :]


def merge_kernel(init, depth, mixing, beside, outer, inner, ext, first_out, second_out, south, north):
    from_west, from_east = pick("lon", inner, outer)
    rows, cells_lat = depth.shape
    ext[...] = jnp.zeros_like(ext)
    for p in range(PLANES):
        if p < 2 * DEPTH:
            own = init[p // DEPTH, p % DEPTH]
        else:
            own = depth[...].astype(F32) if p == 2 * DEPTH else mixing[...]
        extend_lon(ext, p, own, from_west, from_east, rows, cells_lat)
    tall = ext.shape[1]
    lane = iota((tall, 128), 1)
    first = jnp.zeros((tall, 128), F32)
    last = jnp.zeros((tall, 128), F32)
    for p in range(PLANES):
        head = jnp.where(lane < HIGH, ext[p, :, Y0 : Y0 + 128], 0.0)
        tail = jnp.where(lane >= 128 - LOW, ext[p, :, Y0 + cells_lat - 128 : Y0 + cells_lat], 0.0)
        first = first + roll(head, HIGH * p, 1)
        last = last + roll(tail, -LOW * p, 1)
    for out, kept, row, strip in ((south, 0, 0, first), (north, 1, 2, last)):
        out[0:FIELDS, :] = beside[kept * FIELDS : (kept + 1) * FIELDS, :]
        out[FIELDS : 2 * FIELDS, :] = from_west[row * FIELDS : (row + 1) * FIELDS, :]
        out[2 * FIELDS : 3 * FIELDS, :] = from_east[row * FIELDS : (row + 1) * FIELDS, :]
        third = tall // 3
        strip = strip[:third] + roll(strip[third : 2 * third], 32, 1) + roll(strip[2 * third :], 64, 1)
        out[3 * FIELDS :, 0:128] = strip[: third // 2]
        out[3 * FIELDS :, 128:] = strip[third // 2 :]
    address("lat", south, north, first_out, second_out)


def lap(v):
    return roll(v, 1, 0) + roll(v, -1, 0) + roll(v, 1, 1) + roll(v, -1, 1) - 4.0 * v


def vz(column, k, levels):
    above = column[max(k - 1, 0)]
    below = min(k + 1, levels - 1)
    total = above - 2.0 * column[k] if k < len(column) else above
    return total + column[below] if below < len(column) else total


def tendency(v, k, mixing, rotation, levels):
    out = []
    for c in range(2):
        value = v[c][k] + mixing(v[c][k]) + VISCOUS * vz(v[c], k, levels) - FRICTION * v[c][k]
        turned = rotation * v[1 - c][k]
        out.append(value + turned if c == 0 else value - turned)
    return out


def main_kernel(
    levels, refine, lat_count, forcing, fields, precision, outer, inner, first, second,
    padded, partial, share, to_inner, to_outer, spot, to_west, to_east,
):
    from_west, from_east = pick("lon", inner, outer)
    from_south, from_north = pick("lat", first, second)
    rows, cells_lat = partial.shape[1] - 16, partial.shape[2] - 256
    tall, wide = padded.shape[1:]
    lat_index = lax.axis_index("lat")
    grid_lat = cells_lat * lat_count
    lane = iota((tall, 128), 1)
    below, above = [
        jnp.concatenate([message[3 * FIELDS :, 0:128], message[3 * FIELDS :, 128:]], axis=0)
        for message in (from_south, from_north)
    ]
    below, above = [jnp.concatenate([v, roll(v, -32, 1), roll(v, -64, 1)], axis=0) for v in (below, above)]
    full = []
    for p in range(PLANES):
        left = jnp.where(lane >= 128 - LOW, roll(below, LOW * p, 1), 0.0)
        right = jnp.where(lane < HIGH, roll(above, -HIGH * p, 1), 0.0)
        full.append(jnp.concatenate([left, padded[p, :, Y0 : Y0 + cells_lat], right], axis=1))
    mixing = full[2 * DEPTH + 1]
    wet = [(full[2 * DEPTH] > float(k)).astype(F32) for k in range(DEPTH)]
    row_ids = iota((1, wide), 1) - Y0 + lat_index * cells_lat
    rotation = ROTATION * jnp.sin((row_ids.astype(F32) + 0.5) * (math.pi / grid_lat) - 0.5 * math.pi)
    state = [[wet[k] * full[c * DEPTH + k] for k in range(DEPTH)] for c in range(2)]
    surfaces = []
    for step in range(STEPS):
        ahead = [[], []]
        for k in range(DEPTH - 1 - step):
            moved = tendency(state, k, lambda v: mixing * lap(v), rotation, levels)
            for c in range(2):
                value = moved[c] + forcing[2 * step + c] if k == 0 else moved[c]
                ahead[c].append(wet[k] * value)
        state = ahead
        surfaces.append([state[0][0], state[1][0]])
    chunk = 512
    lat_of = iota((cells_lat, chunk), 0).astype(F32).astype(BF16)
    lon_of = iota((rows, chunk), 0).astype(F32)
    lon_tile = lon_of.astype(BF16)
    one, nought = jnp.ones((), BF16), jnp.zeros((), BF16)
    sources = []
    for step in range(STEPS):
        views, edges = [], []
        for c in range(2):
            surface = surfaces[step][c][X0 : X0 + rows + 8]
            for view in (surface, roll(surface, -1, 1)):
                views.append(view[:rows, Y0 : Y0 + cells_lat])
                edges.append(view[rows : rows + 1, Y0 : Y0 + cells_lat])
        views = jnp.concatenate(views + edges + [jnp.zeros((4, cells_lat), F32)], axis=0)
        high, low = split(views)
        views = jnp.concatenate([high.astype(F32), low.astype(F32)], axis=0).astype(BF16)
        seen_rows = 4 * rows + 8

        def spread(record, total):
            cell = record[7:8].astype(jnp.int32)
            lon = lax.shift_right_logical(cell, cells_lat.bit_length() - 1).astype(F32)
            lat = (cell & (cells_lat - 1)).astype(F32).astype(BF16)
            hot = jnp.where(lat_of == lat, one, nought)
            found = dot(views, hot)
            found = found[:seen_rows] + found[seen_rows:]
            here, there, edge = lon_of == lon, lon_of == lon + 1.0, lon == rows - 1.0
            near = jnp.where(here, record[0:1], jnp.where(there, record[1:2], 0.0))
            far = jnp.where(here, record[2:3], jnp.where(there, record[3:4], 0.0))
            near_edge, far_edge = jnp.where(edge, record[1:2], 0.0), jnp.where(edge, record[3:4], 0.0)
            lon = lon.astype(BF16)
            here, there = lon_tile == lon, lon_tile == lon + one
            terms, outside = [[], []], []
            for c in range(2):
                at, last = 2 * c * rows, 4 * rows + 2 * c
                seen = near * found[at : at + rows] + far * found[at + rows : at + 2 * rows]
                miss = jnp.sum(seen, axis=0, keepdims=True) - record[4 + c : 5 + c]
                miss = miss + near_edge * found[last : last + 1] + far_edge * found[last + 1 : last + 2]
                parts = split(record[0:4] * (record[6:7] * miss))
                for part, term in zip(parts, terms):
                    outside.append(jnp.where(edge, part.astype(F32), 0.0))
                    for d in (0, 2):
                        term.append(jnp.where(here, part[d : d + 1], jnp.where(there, part[d + 1 : d + 2], nought)))
            outside = jnp.concatenate(outside, axis=0).astype(BF16)
            return total + dot_lanes(jnp.concatenate(terms[0] + terms[1] + [outside], axis=0), hot)

        total = jnp.zeros((8 * rows + 16, cells_lat), F32)
        for at in range(0, fields.shape[1], chunk):
            total = spread(fields[step * FIELDS : (step + 1) * FIELDS, at : at + chunk], total)
        lanes = slice(step * CAPACITY, (step + 1) * CAPACITY)
        came = [from_west[FIELDS : 2 * FIELDS, lanes], from_east[FIELDS : 2 * FIELDS, lanes]]
        came += [message[i * FIELDS : (i + 1) * FIELDS, lanes] for message in (from_south, from_north) for i in range(3)]
        for at in range(0, 8, chunk // CAPACITY):
            total = spread(jnp.concatenate(came[at : at + chunk // CAPACITY], axis=1), total)
        sources.append([])
        outside = total[8 * rows :]
        total = total[: 4 * rows] + total[4 * rows : 8 * rows]
        for c in range(2):
            spot[...] = jnp.zeros_like(spot)
            for d in range(2):
                at, last = (2 * c + d) * rows, 8 * c + 2 * d + 1
                spot[d, X0 : X0 + rows, Y0 : Y0 + cells_lat] = total[at : at + rows]
                edge = outside[last : last + 1] + outside[last + 4 : last + 5]
                spot[d, X0 + rows : X0 + rows + 1, Y0 : Y0 + cells_lat] = edge
            sources[step].append(spot[0] + roll(spot[1], 1, 1))
    adjoint = None
    nudges = [None] * STEPS
    for step in reversed(range(STEPS)):
        if adjoint is None:
            adjoint = [[sources[step][c]] for c in range(2)]
        else:
            adjoint = [[adjoint[c][0] + sources[step][c]] + adjoint[c][1:] for c in range(2)]
        nudged = [[wet[k] * adjoint[c][k] for k in range(len(adjoint[c]))] for c in range(2)]
        nudges[step] = [nudged[0][0], nudged[1][0]]
        reach = len(nudged[0])
        adjoint = [[], []]
        for k in range(reach):
            moved = tendency(nudged, k, lambda v: lap(mixing * v), -rotation, levels)
            for c in range(2):
                adjoint[c].append(moved[c])
        for c in range(2):
            adjoint[c].append(VISCOUS * vz(nudged[c], reach, levels))
    for c in range(2):
        for k in range(DEPTH):
            p = c * DEPTH + k
            partial[p] = adjoint[c][k]
            to_west[LOW * p : LOW * (p + 1), :] = partial[p, X0 - LOW : X0, :]
            to_east[HIGH * p : HIGH * (p + 1), :] = partial[p, X0 + rows : X0 + rows + HIGH, :]
    address("lon", to_west, to_east, to_inner, to_outer)
    low, part = interpolation(iota((wide, 4 * GROUP), 0) - Y0 - refine // 2, refine)
    column = iota((wide, 4 * GROUP), 1) % GROUP - 1
    onto_lat = jnp.where(column == low, 1.0 - part, 0.0) + jnp.where(column == low + 1, part, 0.0)
    onto_lat = onto_lat.astype(BF16)
    low, part = interpolation(iota((tall, 4 * GROUP), 0) - X0 - refine // 2, refine)
    column = iota((tall, 4 * GROUP), 1) // GROUP - 1
    onto_lon = jnp.where(column == low, 1.0 - part, 0.0) + jnp.where(column == low + 1, part, 0.0)
    weight = jnp.sum(jnp.sum(precision[...], axis=0, keepdims=True), axis=1, keepdims=True)
    parts = []
    for step in range(STEPS):
        for c in range(2):
            high, rest = split(nudges[step][c])
            across = dot(high, onto_lat) + dot(rest, onto_lat)
            parts.append(jnp.sum(onto_lon * across, axis=0, keepdims=True))
    parts[0] = jnp.where(iota((1, 4 * GROUP), 1) == 4 * GROUP - 1, weight, parts[0])
    share[...] = jnp.broadcast_to(jnp.concatenate(parts, axis=0)[None], share.shape)


def plane_kernel(lat_count, per, shares, partial, outer, inner, out, own, first, second, rows, total, block):
    join(partial, inner, outer, own, first, second, block)
    members = shares.shape[0]
    ring = members // (CORES * lat_count)
    ctrl_lat = per * lat_count
    for m in range(members):
        rows[4 * m : 4 * m + 4, :] = shares[m]
    total[...] = jnp.zeros_like(total)
    lane = iota((ring, 4 * GROUP), 1)
    height = out.shape[1] // STEPS
    weight = jnp.zeros((ring, 4 * GROUP), F32)
    for core in range(CORES):
        for step in range(STEPS):
            sums = [jnp.zeros((ring, 4 * GROUP), F32) for _ in range(4)]
            for band in range(lat_count):
                for c in range(2):
                    at = 4 * (core * lat_count + band) + 2 * step + c
                    held = rows[pl.ds(at, ring, stride=4 * CORES * lat_count), :]
                    if step == 0 and c == 0:
                        weight = weight + held
                    start = c * ctrl_lat + per * band - 1
                    first, last = max(start, c * ctrl_lat), min(start + per + 1, (c + 1) * ctrl_lat - 1)
                    mine = (lane >= first) & (lane <= last)
                    for a in range(4):
                        sums[a] = sums[a] + jnp.where(mine, roll(held, start - GROUP * a, 1), 0.0)
            for a in range(4):
                at = step * height + 2 * core + a
                total[pl.ds(at, ring, stride=4), :] = total[pl.ds(at, ring, stride=4), :] + sums[a]
    weight = jnp.sum(jnp.where(lane == 4 * GROUP - 1, weight, 0.0), axis=0, keepdims=True)
    weight = jnp.sum(weight, axis=1, keepdims=True)
    total[4 * ring + 2 : 4 * ring + 3, :] = jnp.broadcast_to(weight, (1, 4 * GROUP))
    out[...] = jnp.broadcast_to(total[: out.shape[1], :][None], out.shape)


def join(partial, inner, outer, own, first_out, second_out, block):
    from_west, from_east = pick("lon", inner, outer)
    rows, cells_lat = own.shape[1:]
    lane = iota((rows, 128), 1)
    first = jnp.zeros((rows, 128), F32)
    last = jnp.zeros((rows, 128), F32)
    for p in range(2 * DEPTH):
        block[p] = partial[p, X0 : X0 + rows, :]
        block[p, :HIGH, :] += from_west[HIGH * p : HIGH * (p + 1), :]
        block[p, rows - LOW :, :] += from_east[LOW * p : LOW * (p + 1), :]
        own[p] = block[p, :, Y0 : Y0 + cells_lat]
        tail = jnp.where(lane >= 128 - LOW, block[p, :, Y0 - 128 : Y0], 0.0)
        head = jnp.where(lane < HIGH, block[p, :, Y0 + cells_lat : Y0 + cells_lat + 128], 0.0)
        first = first + roll(tail, -LOW * p, 1)
        last = last + roll(head, HIGH * p, 1)
    address("lat", first, last, first_out, second_out)


def finish_kernel(normalizer, own, depth, first, second, shares, grad, out, full):
    from_south, from_north = pick("lat", first, second)
    levels, rows, cells_lat = grad.shape[1:]
    periods, _, ctrl_lat, ctrl_lon = out.shape
    table = period_weights(STEPS, periods)
    members, size = shares.shape[:2]
    span = ctrl_lon // members
    total = shares[0, span + 2 : span + 3, :]
    for m in range(1, members):
        total = total + shares[m, span + 2 : span + 3, :]
    scale = normalizer / total[:, 0:1]
    side = iota((rows, 128), 1)
    wet_levels = depth[...]
    for c in range(2):
        for k in range(levels):
            if k >= DEPTH:
                grad[c, k] = jnp.zeros((rows, cells_lat), F32)
                continue
            p = c * DEPTH + k
            low = jnp.where(side < HIGH, roll(from_south, -HIGH * p, 1), 0.0)
            high = jnp.where(side >= 128 - LOW, roll(from_north, LOW * p, 1), 0.0)
            value = own[p] + jnp.concatenate([low, high], axis=1)
            grad[c, k] = jnp.where(wet_levels > k, value * scale, 0.0)
    for step in range(STEPS):
        at = step * size // STEPS
        for m in range(members):
            full[step, m * span : (m + 1) * span, :] = shares[m, at + 1 : at + 1 + span, :]
        for m in range(members):
            before, after = (m * span + ctrl_lon - 1) % ctrl_lon, (m + 1) * span % ctrl_lon
            full[step, before : before + 1, :] += shares[m, at : at + 1, :]
            full[step, after : after + 1, :] += shares[m, at + span + 1 : at + span + 2, :]
    scaled = [(scale * full[step]).T for step in range(STEPS)]
    for period in range(periods):
        value = table[0][period] * scaled[0]
        for step in range(1, STEPS):
            value = value + table[step][period] * scaled[step]
        for c in range(2):
            out[period, c] = value[c * ctrl_lat : (c + 1) * ctrl_lat]


def swap(axis, first, second, periodic):
    count = lax.axis_size(axis)
    across = [(i, i + 1) for i in range(1, count - 1, 2)]
    if periodic:
        across.append((count - 1, 0))
    second = lax.ppermute(second, axis, across + [(b, a) for a, b in across])
    first = lax.ppermute(first, axis, [(i, i ^ 1) for i in range(count)])
    return first, second


def gather(copies, chips, stride, whole_chips):
    if copies.shape[0] == 1:
        return copies
    count = lax.axis_size("lat")
    per_chip = CORES * count
    inside = [range(per_chip)] if whole_chips else [(i,) for i in range(per_chip)]
    groups = []
    for base in range(lax.axis_size("lon") // CORES):
        if base // stride % chips == 0:
            for few in inside:
                groups.append([(base + chip * stride) * per_chip + i for chip in range(chips) for i in few])
    return lax.all_to_all(copies, ("lon", "lat"), 0, 0, axis_index_groups=groups, tiled=True)


def whole(shape):
    return pl.BlockSpec(shape, lambda i: (0,) * len(shape))


def call(kernel, ins, outs, blocks=None, scratch=(), far=False, vmem=16):
    blocks = blocks or {}
    specs = [whole(blocks.get(i, value.shape)) for i, value in enumerate(ins)]
    if far:
        specs = [pl.BlockSpec(memory_space=pltpu.HBM) for _ in ins]
    return pl.pallas_call(
        kernel,
        grid=(1,),
        out_shape=[jax.ShapeDtypeStruct(shape, F32) for shape in outs],
        in_specs=specs,
        out_specs=[whole(shape) for shape in outs],
        scratch_shapes=[pltpu.VMEM(shape, F32) if isinstance(shape, tuple) else shape for shape in scratch],
        compiler_params=pltpu.CompilerParams(vmem_limit_bytes=vmem * 1024 * 1024),
    )(*ins)


def shards(
    initial, depth_levels, mixing, controls, drift_move, drift_cell, drift_weight, drift_obs, drift_precision
):
    _, levels, rows, cells_lat = initial.shape
    periods, _, ctrl_lon, ctrl_lat = controls.shape
    count = drift_move.shape[1]
    lon_count, lat_count = lax.axis_size("lon"), lax.axis_size("lat")
    refine = rows * lon_count // ctrl_lon
    tall, wide = rows + 16, cells_lat + 256
    surface = (2, DEPTH, rows, cells_lat)
    lon_message = (3 * FIELDS + HIGH * PLANES, 256)
    inner, outer, beside = call(
        pack_kernel,
        (drift_move, drift_cell, drift_weight, drift_obs, drift_precision, initial, depth_levels, mixing),
        (lon_message, lon_message, (2 * FIELDS, 256)),
        scratch=(
            pltpu.VMEM(drift_move.shape, jnp.int32),
            pltpu.VMEM(drift_cell.shape, jnp.int32),
            drift_weight.shape,
            drift_obs.shape,
            drift_precision.shape,
            (2, 2, DEPTH, 8, cells_lat),
            pltpu.VMEM((2, 8, cells_lat), jnp.int32),
            (2, 8, cells_lat),
            (STEPS * FIELDS, count),
            lon_message,
            lon_message,
            pltpu.SemaphoreType.DMA((11,)),
        ),
        far=True,
        vmem=60,
    )
    inner, outer = swap("lon", inner, outer, True)
    fields, forcing = call(
        functools.partial(own_kernel, refine, lat_count),
        (jnp.swapaxes(controls, 2, 3), drift_move, drift_cell, drift_weight, drift_obs, drift_precision),
        ((STEPS * FIELDS, count), (2 * STEPS, tall, wide)),
    )
    message = (3 * FIELDS + tall // 6, 256)
    (beside,) = call(near_kernel, (beside,), ((2 * FIELDS, 256),))
    padded, first, second = call(
        merge_kernel,
        (initial, depth_levels, mixing, beside, outer, inner),
        ((PLANES, tall, wide), message, message),
        {0: surface},
        scratch=(message, message),
    )
    first, second = swap("lat", first, second, False)
    edge = (2 * DEPTH * HIGH, wide)
    ring = min(RING, lon_count // CORES)
    members = lon_count // (CORES * ring)
    partial, share, inner, outer = call(
        functools.partial(main_kernel, levels, refine, lat_count),
        (forcing, fields, drift_precision, outer, inner, first, second, padded),
        ((2 * DEPTH, tall, wide), (ring * CORES * lat_count, 2 * STEPS, 4 * GROUP), edge, edge),
        scratch=((2, tall, wide), edge, edge),
    )
    shares = gather(share, ring, 1, True)
    inner, outer = swap("lon", inner, outer, True)
    height = -(-(4 * ring + 3) // 4) * 4
    share, own, first, second = call(
        functools.partial(plane_kernel, lat_count, ctrl_lat // lat_count),
        (shares, partial, outer, inner),
        ((members, STEPS * height, 2 * ctrl_lat), (2 * DEPTH, rows, cells_lat), (rows, 128), (rows, 128)),
        scratch=(
            (4 * (ring + 1) * CORES * lat_count, 4 * GROUP),
            (STEPS * height + 8, 2 * ctrl_lat),
            (2 * DEPTH, rows, wide),
        ),
    )
    first, second = swap("lat", first, second, False)
    shares = gather(share, members, ring, False)
    grad_initial, grad_controls = call(
        functools.partial(finish_kernel, float(STEPS * count * lon_count * lat_count)),
        (own, depth_levels, first, second, shares),
        (initial.shape, (periods, 2, ctrl_lat, ctrl_lon)),
        scratch=((STEPS, ctrl_lon, 2 * ctrl_lat),),
    )
    return grad_initial, jnp.swapaxes(grad_controls, 2, 3)


def solution(mesh):
    return jax.shard_map(
        shards,
        mesh=mesh,
        in_specs=(
            P(None, None, "lon", "lat"),
            P("lon", "lat"),
            P("lon", "lat"),
            P(),
            P(None, ("lon", "lat")),
            P(None, ("lon", "lat")),
            P(None, None, ("lon", "lat")),
            P(None, None, ("lon", "lat")),
            P(None, ("lon", "lat")),
        ),
        out_specs=(P(None, None, "lon", "lat"), P()),
        check_vma=False,
    )
```

```python
import functools
import math

import jax
import jax.numpy as jnp
from jax import lax
from jax.experimental import pallas as pl
from jax.experimental.pallas import tpu as pltpu
from jax.sharding import PartitionSpec as P

CAPACITY = 128
VISCOUS = 0.1
FRICTION = 0.02
ROTATION = 0.3
STEPS = 2
DEPTH = STEPS + 1
CODES = (0, 1, 2, 3, 5, 6, 7, 8)
FIELDS = 8
PLANES = 2 * DEPTH + 2
LOW, HIGH = 2, 3
X0, Y0 = 8, 128
CORES = 2
RING = 8
GROUP = 32
F32, BF16 = jnp.float32, jnp.bfloat16


def iota(shape, dim):
    return lax.broadcasted_iota(jnp.int32, shape, dim)


def split(value):
    high = value.astype(BF16)
    return high, (value - high.astype(F32)).astype(BF16)


def dot(a, b):
    return lax.dot_general(a, b, (((1,), (0,)), ((), ())), preferred_element_type=F32)


def dot_lanes(a, b):
    return lax.dot_general(a, b, (((1,), (1,)), ((), ())), preferred_element_type=F32)


def roll(value, shift, axis):
    return pltpu.roll(value, shift % value.shape[axis], axis)


def parity(axis):
    return lax.axis_index(axis) % 2


def pick(axis, first, second):
    even = parity(axis) == 0
    one, other = first[...], second[...]
    return jnp.where(even, other, one), jnp.where(even, one, other)


def address(axis, behind, ahead, first, second):
    even = parity(axis) == 0
    first[...] = jnp.where(even, ahead[...], behind[...])
    second[...] = jnp.where(even, behind[...], ahead[...])


def interpolation(offset, refine):
    low = lax.shift_right_arithmetic(offset, refine.bit_length() - 1)
    return low, ((offset - low * refine).astype(F32) + 0.5) / refine


def period_weights(steps_total, periods):
    table = []
    for step in range(steps_total):
        position = (step + 0.5) * (periods - 1) / steps_total
        table.append([max(0.0, 1.0 - abs(position - period)) for period in range(periods)])
    return table


def stage(fields, cell, weight, obs):
    for step in range(STEPS):
        base = step * FIELDS
        for i in range(4):
            fields[base + i : base + i + 1, :] = weight[i, step : step + 1, :]
        for i in range(2):
            fields[base + 4 + i : base + 5 + i, :] = obs[i, step : step + 1, :]
        fields[base + 7 : base + 8, :] = cell[step : step + 1, :].astype(F32)


def own_kernel(refine, lat_count, controls, move, cell, weight, obs, prec, fields, forcing):
    stage(fields, cell, weight, obs)
    for step in range(STEPS):
        row = step * FIELDS + 6
        fields[row : row + 1, :] = jnp.where(move[step : step + 1, :] == 4, prec[step : step + 1, :], 0.0)
    tall, wide = forcing.shape[1:]
    rows, cells_lat = tall - 16, wide - 256
    periods, _, ctrl_lat, ctrl_lon = controls.shape
    table = period_weights(STEPS, periods)
    low, part = interpolation(iota((tall, ctrl_lon), 0) - X0 + lax.axis_index("lon") * rows - refine // 2, refine)
    column = iota((tall, ctrl_lon), 1)
    wrapped, after = (low + ctrl_lon) % ctrl_lon, (low + 1 + ctrl_lon) % ctrl_lon
    lon_interp = jnp.where(column == wrapped, 1.0 - part, 0.0) + jnp.where(column == after, part, 0.0)
    low, part = interpolation(iota((ctrl_lat, wide), 1) - Y0 + lax.axis_index("lat") * cells_lat - refine // 2, refine)
    column = iota((ctrl_lat, wide), 0)
    lat_interp = jnp.where(column == low, 1.0 - part, 0.0) + jnp.where(column == low + 1, part, 0.0)
    lon_interp, lat_interp = lon_interp.astype(BF16), lat_interp.astype(BF16)
    for step in range(STEPS):
        for c in range(2):
            blended = table[step][0] * controls[0, c]
            for period in range(1, periods):
                blended = blended + table[step][period] * controls[period, c]
            high, low = split(blended)
            high, low = split(dot_lanes(lon_interp, high) + dot_lanes(lon_interp, low))
            forcing[2 * step + c] = dot(high, lat_interp) + dot(low, lat_interp)


def near_kernel(beside, near):
    near[...] = beside[...]


def pack_kernel(
    move_far, cell_far, weight_far, obs_far, prec_far, init_far, depth_far, mixing_far, inner, outer, beside,
    move, cell, weight, obs, prec, init, depth, mixing, fields, east, west, arrived,
):
    count = move.shape[1]
    rows = depth_far.shape[0]
    whole_arrays = [(move_far, move), (cell_far, cell), (weight_far, weight), (obs_far, obs), (prec_far, prec)]
    edges = []
    for end, first in enumerate((0, rows - 8)):
        edges.append((init_far.at[:, :DEPTH, pl.ds(first, 8), :], init.at[end]))
        edges.append((depth_far.at[pl.ds(first, 8), :], depth.at[end]))
        edges.append((mixing_far.at[pl.ds(first, 8), :], mixing.at[end]))
    copies = [pltpu.make_async_copy(far, near, arrived.at[i]) for i, (far, near) in enumerate(whole_arrays + edges)]
    for copy in copies:
        copy.start()
    copies[0].wait()
    width = 256
    blocks = count // width
    triangle = (iota((width, width), 0) <= iota((width, width), 1)).astype(F32).astype(BF16)
    code = iota((8, 1), 0)
    code = code + (code >= 4).astype(jnp.int32)
    matches = []
    for step in range(STEPS):
        for block in range(blocks):
            matches.append((move[step : step + 1, block * width : (block + 1) * width] == code).astype(F32))
    ranks = dot(jnp.concatenate(matches, axis=0).astype(BF16), triangle)
    places = []
    for step in range(STEPS):
        carry = jnp.full((8, 1), -1.0, F32)
        for block in range(blocks):
            at = step * blocks + block
            rank = ranks[8 * at : 8 * at + 8]
            places.append(jnp.sum(matches[at] * (rank + carry), axis=0, keepdims=True))
            carry = carry + rank[:, width - 1 :]
    for copy in copies[1:]:
        copy.wait()
    stage(fields, cell, weight, obs)
    for step in range(STEPS):
        fields[step * FIELDS + 6 : step * FIELDS + 7, :] = prec[step : step + 1, :]
    for p in range(PLANES):
        for end, strip, first, size in ((0, west, 0, HIGH), (1, east, 8 - LOW, LOW)):
            if p < 2 * DEPTH:
                line = init[end, p // DEPTH, p % DEPTH, first : first + size, :]
            elif p == 2 * DEPTH:
                line = depth[end, first : first + size, :].astype(F32)
            else:
                line = mixing[end, first : first + size, :]
            strip[3 * FIELDS + size * p : 3 * FIELDS + size * (p + 1), :] = line
    joined = 2
    slot = iota((CAPACITY, joined * width), 0).astype(F32).astype(BF16)
    one, nought = jnp.ones((), BF16), jnp.zeros((), BF16)
    for step in range(STEPS):
        packed = jnp.zeros((8 * 2 * FIELDS, CAPACITY), F32)
        for block in range(0, blocks, joined):
            at = step * blocks + block
            place = jnp.concatenate(places[at : at + joined], axis=1).astype(BF16)
            spots = jnp.where(slot == place, one, nought)
            lanes = slice(block * width, (block + joined) * width)
            both = jnp.concatenate(split(fields[step * FIELDS : (step + 1) * FIELDS, lanes]), axis=0)
            kind = jnp.broadcast_to(move[step : step + 1, lanes].astype(F32), both.shape).astype(BF16)
            masked = jnp.concatenate([jnp.where(kind == jnp.full((), c, BF16), both, nought) for c in CODES], axis=0)
            packed = packed + dot_lanes(masked, spots)
        lanes = slice(step * CAPACITY, (step + 1) * CAPACITY)
        for d in range(8):
            at = d * 2 * FIELDS
            record = packed[at : at + FIELDS] + packed[at + FIELDS : at + 2 * FIELDS]
            if CODES[d] // 3 == 1:
                row = CODES[d] % 3 // 2 * FIELDS
                beside[row : row + FIELDS, lanes] = record
            else:
                row = (CODES[d] % 3) * FIELDS
                (west if CODES[d] // 3 == 0 else east)[row : row + FIELDS, lanes] = record
    address("lon", west, east, inner, outer)


def extend_lon(ext, p, own, from_west, from_east, rows, cells_lat):
    lanes = slice(Y0, Y0 + cells_lat)
    ext[p, X0 : X0 + rows, lanes] = own
    at = 3 * FIELDS + LOW * p
    ext[p, X0 - LOW : X0, lanes] = from_west[at : at + LOW, :]
    at = 3 * FIELDS + HIGH * p
    ext[p, X0 + rows : X0 + rows + HIGH, lanes] = from_east[at : at + HIGH, :]


def merge_kernel(init, depth, mixing, beside, outer, inner, ext, first_out, second_out, south, north):
    from_west, from_east = pick("lon", inner, outer)
    rows, cells_lat = depth.shape
    ext[...] = jnp.zeros_like(ext)
    for p in range(PLANES):
        if p < 2 * DEPTH:
            own = init[p // DEPTH, p % DEPTH]
        else:
            own = depth[...].astype(F32) if p == 2 * DEPTH else mixing[...]
        extend_lon(ext, p, own, from_west, from_east, rows, cells_lat)
    tall = ext.shape[1]
    lane = iota((tall, 128), 1)
    first = jnp.zeros((tall, 128), F32)
    last = jnp.zeros((tall, 128), F32)
    for p in range(PLANES):
        head = jnp.where(lane < HIGH, ext[p, :, Y0 : Y0 + 128], 0.0)
        tail = jnp.where(lane >= 128 - LOW, ext[p, :, Y0 + cells_lat - 128 : Y0 + cells_lat], 0.0)
        first = first + roll(head, HIGH * p, 1)
        last = last + roll(tail, -LOW * p, 1)
    for out, kept, row, strip in ((south, 0, 0, first), (north, 1, 2, last)):
        out[0:FIELDS, :] = beside[kept * FIELDS : (kept + 1) * FIELDS, :]
        out[FIELDS : 2 * FIELDS, :] = from_west[row * FIELDS : (row + 1) * FIELDS, :]
        out[2 * FIELDS : 3 * FIELDS, :] = from_east[row * FIELDS : (row + 1) * FIELDS, :]
        third = tall // 3
        strip = strip[:third] + roll(strip[third : 2 * third], 32, 1) + roll(strip[2 * third :], 64, 1)
        out[3 * FIELDS :, 0:128] = strip[: third // 2]
        out[3 * FIELDS :, 128:] = strip[third // 2 :]
    address("lat", south, north, first_out, second_out)


def lap(v):
    return roll(v, 1, 0) + roll(v, -1, 0) + roll(v, 1, 1) + roll(v, -1, 1) - 4.0 * v


def vz(column, k, levels):
    above = column[max(k - 1, 0)]
    below = min(k + 1, levels - 1)
    total = above - 2.0 * column[k] if k < len(column) else above
    return total + column[below] if below < len(column) else total


def tendency(v, k, mixing, rotation, levels):
    out = []
    for c in range(2):
        value = v[c][k] + mixing(v[c][k]) + VISCOUS * vz(v[c], k, levels) - FRICTION * v[c][k]
        turned = rotation * v[1 - c][k]
        out.append(value + turned if c == 0 else value - turned)
    return out


def main_kernel(
    levels, refine, lat_count, forcing, fields, precision, outer, inner, second, first,
    padded, partial, share, to_inner, to_outer, spot, to_west, to_east,
):
    from_west, from_east = pick("lon", inner, outer)
    from_south, from_north = pick("lat", first, second)
    rows, cells_lat = partial.shape[1] - 16, partial.shape[2] - 256
    tall, wide = padded.shape[1:]
    lat_index = lax.axis_index("lat")
    grid_lat = cells_lat * lat_count
    lane = iota((tall, 128), 1)
    below, above = [
        jnp.concatenate([message[3 * FIELDS :, 0:128], message[3 * FIELDS :, 128:]], axis=0)
        for message in (from_south, from_north)
    ]
    below, above = [jnp.concatenate([v, roll(v, -32, 1), roll(v, -64, 1)], axis=0) for v in (below, above)]
    full = []
    for p in range(PLANES):
        left = jnp.where(lane >= 128 - LOW, roll(below, LOW * p, 1), 0.0)
        right = jnp.where(lane < HIGH, roll(above, -HIGH * p, 1), 0.0)
        full.append(jnp.concatenate([left, padded[p, :, Y0 : Y0 + cells_lat], right], axis=1))
    mixing = full[2 * DEPTH + 1]
    wet = [(full[2 * DEPTH] > float(k)).astype(F32) for k in range(DEPTH)]
    row_ids = iota((1, wide), 1) - Y0 + lat_index * cells_lat
    rotation = ROTATION * jnp.sin((row_ids.astype(F32) + 0.5) * (math.pi / grid_lat) - 0.5 * math.pi)
    state = [[wet[k] * full[c * DEPTH + k] for k in range(DEPTH)] for c in range(2)]
    surfaces = []
    for step in range(STEPS):
        ahead = [[], []]
        for k in range(DEPTH - 1 - step):
            moved = tendency(state, k, lambda v: mixing * lap(v), rotation, levels)
            for c in range(2):
                value = moved[c] + forcing[2 * step + c] if k == 0 else moved[c]
                ahead[c].append(wet[k] * value)
        state = ahead
        surfaces.append([state[0][0], state[1][0]])
    chunk = 512
    lat_of = iota((cells_lat, chunk), 0).astype(F32).astype(BF16)
    lon_of = iota((rows, chunk), 0).astype(F32)
    lon_tile = lon_of.astype(BF16)
    one, nought = jnp.ones((), BF16), jnp.zeros((), BF16)
    sources = []
    for step in range(STEPS):
        views, edges = [], []
        for c in range(2):
            surface = surfaces[step][c][X0 : X0 + rows + 8]
            for view in (surface, roll(surface, -1, 1)):
                views.append(view[:rows, Y0 : Y0 + cells_lat])
                edges.append(view[rows : rows + 1, Y0 : Y0 + cells_lat])
        views = jnp.concatenate(views + edges + [jnp.zeros((4, cells_lat), F32)], axis=0)
        high, low = split(views)
        views = jnp.concatenate([high.astype(F32), low.astype(F32)], axis=0).astype(BF16)
        seen_rows = 4 * rows + 8

        def spread(record, total):
            cell = record[7:8].astype(jnp.int32)
            lon = lax.shift_right_logical(cell, cells_lat.bit_length() - 1).astype(F32)
            lat = (cell & (cells_lat - 1)).astype(F32).astype(BF16)
            hot = jnp.where(lat_of == lat, one, nought)
            found = dot(views, hot)
            found = found[:seen_rows] + found[seen_rows:]
            here, there, edge = lon_of == lon, lon_of == lon + 1.0, lon == rows - 1.0
            near = jnp.where(here, record[0:1], jnp.where(there, record[1:2], 0.0))
            far = jnp.where(here, record[2:3], jnp.where(there, record[3:4], 0.0))
            near_edge, far_edge = jnp.where(edge, record[1:2], 0.0), jnp.where(edge, record[3:4], 0.0)
            lon = lon.astype(BF16)
            here, there = lon_tile == lon, lon_tile == lon + one
            terms, outside = [[], []], []
            for c in range(2):
                at, last = 2 * c * rows, 4 * rows + 2 * c
                seen = near * found[at : at + rows] + far * found[at + rows : at + 2 * rows]
                miss = jnp.sum(seen, axis=0, keepdims=True) - record[4 + c : 5 + c]
                miss = miss + near_edge * found[last : last + 1] + far_edge * found[last + 1 : last + 2]
                parts = split(record[0:4] * (record[6:7] * miss))
                for part, term in zip(parts, terms):
                    outside.append(jnp.where(edge, part.astype(F32), 0.0))
                    for d in (0, 2):
                        term.append(jnp.where(here, part[d : d + 1], jnp.where(there, part[d + 1 : d + 2], nought)))
            outside = jnp.concatenate(outside, axis=0).astype(BF16)
            return total + dot_lanes(jnp.concatenate(terms[0] + terms[1] + [outside], axis=0), hot)

        total = jnp.zeros((8 * rows + 16, cells_lat), F32)
        for at in range(0, fields.shape[1], chunk):
            total = spread(fields[step * FIELDS : (step + 1) * FIELDS, at : at + chunk], total)
        lanes = slice(step * CAPACITY, (step + 1) * CAPACITY)
        came = [from_west[FIELDS : 2 * FIELDS, lanes], from_east[FIELDS : 2 * FIELDS, lanes]]
        came += [message[i * FIELDS : (i + 1) * FIELDS, lanes] for message in (from_south, from_north) for i in range(3)]
        for at in range(0, 8, chunk // CAPACITY):
            total = spread(jnp.concatenate(came[at : at + chunk // CAPACITY], axis=1), total)
        sources.append([])
        outside = total[8 * rows :]
        total = total[: 4 * rows] + total[4 * rows : 8 * rows]
        for c in range(2):
            spot[...] = jnp.zeros_like(spot)
            for d in range(2):
                at, last = (2 * c + d) * rows, 8 * c + 2 * d + 1
                spot[d, X0 : X0 + rows, Y0 : Y0 + cells_lat] = total[at : at + rows]
                edge = outside[last : last + 1] + outside[last + 4 : last + 5]
                spot[d, X0 + rows : X0 + rows + 1, Y0 : Y0 + cells_lat] = edge
            sources[step].append(spot[0] + roll(spot[1], 1, 1))
    adjoint = None
    nudges = [None] * STEPS
    for step in reversed(range(STEPS)):
        if adjoint is None:
            adjoint = [[sources[step][c]] for c in range(2)]
        else:
            adjoint = [[adjoint[c][0] + sources[step][c]] + adjoint[c][1:] for c in range(2)]
        nudged = [[wet[k] * adjoint[c][k] for k in range(len(adjoint[c]))] for c in range(2)]
        nudges[step] = [nudged[0][0], nudged[1][0]]
        reach = len(nudged[0])
        adjoint = [[], []]
        for k in range(reach):
            moved = tendency(nudged, k, lambda v: lap(mixing * v), -rotation, levels)
            for c in range(2):
                adjoint[c].append(moved[c])
        for c in range(2):
            adjoint[c].append(VISCOUS * vz(nudged[c], reach, levels))
    for c in range(2):
        for k in range(DEPTH):
            p = c * DEPTH + k
            partial[p] = adjoint[c][k]
            to_west[LOW * p : LOW * (p + 1), :] = partial[p, X0 - LOW : X0, :]
            to_east[HIGH * p : HIGH * (p + 1), :] = partial[p, X0 + rows : X0 + rows + HIGH, :]
    address("lon", to_west, to_east, to_inner, to_outer)
    low, part = interpolation(iota((wide, 4 * GROUP), 0) - Y0 - refine // 2, refine)
    column = iota((wide, 4 * GROUP), 1) % GROUP - 1
    onto_lat = jnp.where(column == low, 1.0 - part, 0.0) + jnp.where(column == low + 1, part, 0.0)
    onto_lat = onto_lat.astype(BF16)
    low, part = interpolation(iota((tall, 4 * GROUP), 0) - X0 - refine // 2, refine)
    column = iota((tall, 4 * GROUP), 1) // GROUP - 1
    onto_lon = jnp.where(column == low, 1.0 - part, 0.0) + jnp.where(column == low + 1, part, 0.0)
    weight = jnp.sum(jnp.sum(precision[...], axis=0, keepdims=True), axis=1, keepdims=True)
    parts = []
    for step in range(STEPS):
        for c in range(2):
            high, rest = split(nudges[step][c])
            across = dot(high, onto_lat) + dot(rest, onto_lat)
            parts.append(jnp.sum(onto_lon * across, axis=0, keepdims=True))
    parts[0] = jnp.where(iota((1, 4 * GROUP), 1) == 4 * GROUP - 1, weight, parts[0])
    share[...] = jnp.broadcast_to(jnp.concatenate(parts, axis=0)[None], share.shape)


def plane_kernel(lat_count, per, shares, partial, outer, inner, out, own, first, second, rows, total, block):
    join(partial, inner, outer, own, first, second, block)
    members = shares.shape[0]
    ring = members // (CORES * lat_count)
    ctrl_lat = per * lat_count
    for m in range(members):
        rows[4 * m : 4 * m + 4, :] = shares[m]
    total[...] = jnp.zeros_like(total)
    lane = iota((ring, 4 * GROUP), 1)
    height = out.shape[1] // STEPS
    weight = jnp.zeros((ring, 4 * GROUP), F32)
    for core in range(CORES):
        for step in range(STEPS):
            sums = [jnp.zeros((ring, 4 * GROUP), F32) for _ in range(4)]
            for band in range(lat_count):
                for c in range(2):
                    at = 4 * (core * lat_count + band) + 2 * step + c
                    held = rows[pl.ds(at, ring, stride=4 * CORES * lat_count), :]
                    if step == 0 and c == 0:
                        weight = weight + held
                    start = c * ctrl_lat + per * band - 1
                    first, last = max(start, c * ctrl_lat), min(start + per + 1, (c + 1) * ctrl_lat - 1)
                    mine = (lane >= first) & (lane <= last)
                    for a in range(4):
                        sums[a] = sums[a] + jnp.where(mine, roll(held, start - GROUP * a, 1), 0.0)
            for a in range(4):
                at = step * height + 2 * core + a
                total[pl.ds(at, ring, stride=4), :] = total[pl.ds(at, ring, stride=4), :] + sums[a]
    weight = jnp.sum(jnp.where(lane == 4 * GROUP - 1, weight, 0.0), axis=0, keepdims=True)
    weight = jnp.sum(weight, axis=1, keepdims=True)
    total[4 * ring + 2 : 4 * ring + 3, :] = jnp.broadcast_to(weight, (1, 4 * GROUP))
    out[...] = jnp.broadcast_to(total[: out.shape[1], :][None], out.shape)


def join(partial, inner, outer, own, first_out, second_out, block):
    from_west, from_east = pick("lon", inner, outer)
    rows, cells_lat = own.shape[1:]
    lane = iota((rows, 128), 1)
    first = jnp.zeros((rows, 128), F32)
    last = jnp.zeros((rows, 128), F32)
    for p in range(2 * DEPTH):
        block[p] = partial[p, X0 : X0 + rows, :]
        block[p, :HIGH, :] += from_west[HIGH * p : HIGH * (p + 1), :]
        block[p, rows - LOW :, :] += from_east[LOW * p : LOW * (p + 1), :]
        own[p] = block[p, :, Y0 : Y0 + cells_lat]
        tail = jnp.where(lane >= 128 - LOW, block[p, :, Y0 - 128 : Y0], 0.0)
        head = jnp.where(lane < HIGH, block[p, :, Y0 + cells_lat : Y0 + cells_lat + 128], 0.0)
        first = first + roll(tail, -LOW * p, 1)
        last = last + roll(head, HIGH * p, 1)
    address("lat", first, last, first_out, second_out)


def finish_kernel(normalizer, own, depth, second, first, shares, grad, out, full):
    from_south, from_north = pick("lat", first, second)
    levels, rows, cells_lat = grad.shape[1:]
    periods, _, ctrl_lat, ctrl_lon = out.shape
    table = period_weights(STEPS, periods)
    members, size = shares.shape[:2]
    span = ctrl_lon // members
    total = shares[0, span + 2 : span + 3, :]
    for m in range(1, members):
        total = total + shares[m, span + 2 : span + 3, :]
    scale = normalizer / total[:, 0:1]
    side = iota((rows, 128), 1)
    wet_levels = depth[...]
    for c in range(2):
        for k in range(levels):
            if k >= DEPTH:
                grad[c, k] = jnp.zeros((rows, cells_lat), F32)
                continue
            p = c * DEPTH + k
            low = jnp.where(side < HIGH, roll(from_south, -HIGH * p, 1), 0.0)
            high = jnp.where(side >= 128 - LOW, roll(from_north, LOW * p, 1), 0.0)
            value = own[p] + jnp.concatenate([low, high], axis=1)
            grad[c, k] = jnp.where(wet_levels > k, value * scale, 0.0)
    for step in range(STEPS):
        at = step * size // STEPS
        for m in range(members):
            full[step, m * span : (m + 1) * span, :] = shares[m, at + 1 : at + 1 + span, :]
        for m in range(members):
            before, after = (m * span + ctrl_lon - 1) % ctrl_lon, (m + 1) * span % ctrl_lon
            full[step, before : before + 1, :] += shares[m, at : at + 1, :]
            full[step, after : after + 1, :] += shares[m, at + span + 1 : at + span + 2, :]
    scaled = [(scale * full[step]).T for step in range(STEPS)]
    for period in range(periods):
        value = table[0][period] * scaled[0]
        for step in range(1, STEPS):
            value = value + table[step][period] * scaled[step]
        for c in range(2):
            out[period, c] = value[c * ctrl_lat : (c + 1) * ctrl_lat]


def swap(axis, first, second, periodic):
    count = lax.axis_size(axis)
    across = [(i, i + 1) for i in range(1, count - 1, 2)]
    if periodic:
        across.append((count - 1, 0))
    second = lax.ppermute(second, axis, across + [(b, a) for a, b in across])
    first = lax.ppermute(first, axis, [(i, i ^ 1) for i in range(count)])
    return first, second


def gather(copies, chips, stride, whole_chips):
    if copies.shape[0] == 1:
        return copies
    count = lax.axis_size("lat")
    per_chip = CORES * count
    inside = [range(per_chip)] if whole_chips else [(i,) for i in range(per_chip)]
    groups = []
    for base in range(lax.axis_size("lon") // CORES):
        if base // stride % chips == 0:
            for few in inside:
                groups.append([(base + chip * stride) * per_chip + i for chip in range(chips) for i in few])
    return lax.all_to_all(copies, ("lon", "lat"), 0, 0, axis_index_groups=groups, tiled=True)


def whole(shape):
    return pl.BlockSpec(shape, lambda i: (0,) * len(shape))


def call(kernel, ins, outs, blocks=None, scratch=(), far=False, vmem=16):
    blocks = blocks or {}
    specs = [whole(blocks.get(i, value.shape)) for i, value in enumerate(ins)]
    if far:
        specs = [pl.BlockSpec(memory_space=pltpu.HBM) for _ in ins]
    return pl.pallas_call(
        kernel,
        grid=(1,),
        out_shape=[jax.ShapeDtypeStruct(shape, F32) for shape in outs],
        in_specs=specs,
        out_specs=[whole(shape) for shape in outs],
        scratch_shapes=[pltpu.VMEM(shape, F32) if isinstance(shape, tuple) else shape for shape in scratch],
        compiler_params=pltpu.CompilerParams(vmem_limit_bytes=vmem * 1024 * 1024),
    )(*ins)


def shards(
    initial, depth_levels, mixing, controls, drift_move, drift_cell, drift_weight, drift_obs, drift_precision
):
    _, levels, rows, cells_lat = initial.shape
    periods, _, ctrl_lon, ctrl_lat = controls.shape
    count = drift_move.shape[1]
    lon_count, lat_count = lax.axis_size("lon"), lax.axis_size("lat")
    refine = rows * lon_count // ctrl_lon
    tall, wide = rows + 16, cells_lat + 256
    surface = (2, DEPTH, rows, cells_lat)
    lon_message = (3 * FIELDS + HIGH * PLANES, 256)
    inner, outer, beside = call(
        pack_kernel,
        (drift_move, drift_cell, drift_weight, drift_obs, drift_precision, initial, depth_levels, mixing),
        (lon_message, lon_message, (2 * FIELDS, 256)),
        scratch=(
            pltpu.VMEM(drift_move.shape, jnp.int32),
            pltpu.VMEM(drift_cell.shape, jnp.int32),
            drift_weight.shape,
            drift_obs.shape,
            drift_precision.shape,
            (2, 2, DEPTH, 8, cells_lat),
            pltpu.VMEM((2, 8, cells_lat), jnp.int32),
            (2, 8, cells_lat),
            (STEPS * FIELDS, count),
            lon_message,
            lon_message,
            pltpu.SemaphoreType.DMA((11,)),
        ),
        far=True,
        vmem=60,
    )
    inner, outer = swap("lon", inner, outer, True)
    fields, forcing = call(
        functools.partial(own_kernel, refine, lat_count),
        (jnp.swapaxes(controls, 2, 3), drift_move, drift_cell, drift_weight, drift_obs, drift_precision),
        ((STEPS * FIELDS, count), (2 * STEPS, tall, wide)),
    )
    message = (3 * FIELDS + tall // 6, 256)
    (beside,) = call(near_kernel, (beside,), ((2 * FIELDS, 256),))
    padded, first, second = call(
        merge_kernel,
        (initial, depth_levels, mixing, beside, outer, inner),
        ((PLANES, tall, wide), message, message),
        {0: surface},
        scratch=(message, message),
    )
    first, second = swap("lat", first, second, False)
    edge = (2 * DEPTH * HIGH, wide)
    ring = min(RING, lon_count // CORES)
    members = lon_count // (CORES * ring)
    partial, share, inner, outer = call(
        functools.partial(main_kernel, levels, refine, lat_count),
        (forcing, fields, drift_precision, outer, inner, second, first, padded),
        ((2 * DEPTH, tall, wide), (ring * CORES * lat_count, 2 * STEPS, 4 * GROUP), edge, edge),
        scratch=((2, tall, wide), edge, edge),
    )
    shares = gather(share, ring, 1, True)
    inner, outer = swap("lon", inner, outer, True)
    height = -(-(4 * ring + 3) // 4) * 4
    share, own, first, second = call(
        functools.partial(plane_kernel, lat_count, ctrl_lat // lat_count),
        (shares, partial, outer, inner),
        ((members, STEPS * height, 2 * ctrl_lat), (2 * DEPTH, rows, cells_lat), (rows, 128), (rows, 128)),
        scratch=(
            (4 * (ring + 1) * CORES * lat_count, 4 * GROUP),
            (STEPS * height + 8, 2 * ctrl_lat),
            (2 * DEPTH, rows, wide),
        ),
    )
    first, second = swap("lat", first, second, False)
    shares = gather(share, members, ring, False)
    grad_initial, grad_controls = call(
        functools.partial(finish_kernel, float(STEPS * count * lon_count * lat_count)),
        (own, depth_levels, second, first, shares),
        (initial.shape, (periods, 2, ctrl_lat, ctrl_lon)),
        scratch=((STEPS, ctrl_lon, 2 * ctrl_lat),),
    )
    return grad_initial, jnp.swapaxes(grad_controls, 2, 3)


def solution(mesh):
    return jax.shard_map(
        shards,
        mesh=mesh,
        in_specs=(
            P(None, None, "lon", "lat"),
            P("lon", "lat"),
            P("lon", "lat"),
            P(),
            P(None, ("lon", "lat")),
            P(None, ("lon", "lat")),
            P(None, None, ("lon", "lat")),
            P(None, None, ("lon", "lat")),
            P(None, ("lon", "lat")),
        ),
        out_specs=(P(None, None, "lon", "lat"), P()),
        check_vma=False,
    )
```
